32 devices in a mesh: dp: 8 (over y, x, core), mp: 4 (over z).
Axes of the slice: x: 2, y: 2, z: 4, core: 2. Of those that a mesh axis runs over, the one named last changes fastest.
Arguments:
- inputs: bfloat16 [8192, 2560], P('dp'), may hold values from -6 to 6
- cotangent: bfloat16 [8192, 2560], P('dp'), may hold values from -6 to 6
- norm_gains: float32 [6144], P('dp'), may hold values from 0.5 to 1.5
- norm_gains_first: float32 [6144], P('dp'), may hold values from -96 to 96
- norm_gains_second: float32 [6144], P('dp'), may hold values from 969.5232 to 3870.72
- query_down: float32 [2560, 768], P(('dp', 'mp')), may hold values from -0.125 to 0.125
- query_down_first: float32 [2560, 768], P(('dp', 'mp')), may hold values from -40 to 40
- query_down_second: float32 [2560, 768], P(('dp', 'mp')), may hold values from 211.14061 to 842.9568
- latent_down: float32 [2560, 288], P(('dp', 'mp')), may hold values from -0.125 to 0.125
- latent_down_first: float32 [2560, 288], P(('dp', 'mp')), may hold values from -128 to 128
- latent_down_second: float32 [2560, 288], P(('dp', 'mp')), may hold values from 1723.5968 to 6881.28
- query_up: float32 [768, 3840], P('dp', 'mp'), may hold values from -0.21875 to 0.21875
- query_up_first: float32 [768, 3840], P('dp', 'mp'), may hold values from -16 to 16
- query_up_second: float32 [768, 3840], P('dp', 'mp'), may hold values from 38.78093 to 154.8288
- latent_up: float32 [256, 5120], P('dp', 'mp'), may hold values from -0.375 to 0.375
- latent_up_first: float32 [256, 5120], P('dp', 'mp'), may hold values from -32 to 32
- latent_up_second: float32 [256, 5120], P('dp', 'mp'), may hold values from 155.12372 to 619.3152
- out_proj: float32 [2560, 2560], P('mp', 'dp'), may hold values from -4 to 4
- out_proj_first: float32 [2560, 2560], P('mp', 'dp'), may hold values from -2.5 to 2.5
- out_proj_second: float32 [2560, 2560], P('mp', 'dp'), may hold values from 0.6894387 to 2.752512
- ffn_gate: float32 [2560, 6400], P('dp', 'mp'), may hold values from -0.125 to 0.125
- ffn_gate_first: float32 [2560, 6400], P('dp', 'mp'), may hold values from -48 to 48
- ffn_gate_second: float32 [2560, 6400], P('dp', 'mp'), may hold values from 275.77548 to 1101.0048
- ffn_up: float32 [2560, 6400], P('dp', 'mp'), may hold values from -0.125 to 0.125
- ffn_up_first: float32 [2560, 6400], P('dp', 'mp'), may hold values from -48 to 48
- ffn_up_second: float32 [2560, 6400], P('dp', 'mp'), may hold values from 275.77548 to 1101.0048
- ffn_down: float32 [6400, 2560], P('mp', 'dp'), may hold values from -0.875 to 0.875
- ffn_down_first: float32 [6400, 2560], P('mp', 'dp'), may hold values from -6 to 6
- ffn_down_second: float32 [6400, 2560], P('mp', 'dp'), may hold values from 4.308992 to 17.2032
Outputs:
- output: bfloat16 [8192, 2560], P('dp')
- input_grad: float32 [8192, 2560], P('dp')
- norm_gains_first_new: float32 [6144], P('dp')
- norm_gains_second_new: float32 [6144], P('dp')
- norm_gains_new: float32 [6144], P('dp')
- query_down_first_new: float32 [2560, 768], P(('dp', 'mp'))
- query_down_second_new: float32 [2560, 768], P(('dp', 'mp'))
- query_down_new: float32 [2560, 768], P(('dp', 'mp'))
- latent_down_first_new: float32 [2560, 288], P(('dp', 'mp'))
- latent_down_second_new: float32 [2560, 288], P(('dp', 'mp'))
- latent_down_new: float32 [2560, 288], P(('dp', 'mp'))
- query_up_first_new: float32 [768, 3840], P('dp', 'mp')
- query_up_second_new: float32 [768, 3840], P('dp', 'mp')
- query_up_new: float32 [768, 3840], P('dp', 'mp')
- latent_up_first_new: float32 [256, 5120], P('dp', 'mp')
- latent_up_second_new: float32 [256, 5120], P('dp', 'mp')
- latent_up_new: float32 [256, 5120], P('dp', 'mp')
- out_proj_first_new: float32 [2560, 2560], P('mp', 'dp')
- out_proj_second_new: float32 [2560, 2560], P('mp', 'dp')
- out_proj_new: float32 [2560, 2560], P('mp', 'dp')
- ffn_gate_first_new: float32 [2560, 6400], P('dp', 'mp')
- ffn_gate_second_new: float32 [2560, 6400], P('dp', 'mp')
- ffn_gate_new: float32 [2560, 6400], P('dp', 'mp')
- ffn_up_first_new: float32 [2560, 6400], P('dp', 'mp')
- ffn_up_second_new: float32 [2560, 6400], P('dp', 'mp')
- ffn_up_new: float32 [2560, 6400], P('dp', 'mp')
- ffn_down_first_new: float32 [6400, 2560], P('mp', 'dp')
- ffn_down_second_new: float32 [6400, 2560], P('mp', 'dp')
- ffn_down_new: float32 [6400, 2560], P('mp', 'dp')
The draws below stay inside these ranges and needn't reach their ends.
All inputs are finite; a program needn't handle non-finite values.
Results may differ from the reference program's by a relative error of at most 0.019.
Values may be sent and summed in bfloat16 or wider, within the bound.
No kernel may reach another device: no remote copies, remote signals or barrier semaphores. Data moves between devices by JAX's collectives and lax.ppermute only.
A program may use at most 320 MiB of HBM per device.

```python
import math
import jax
import jax.numpy as jnp
from jax import lax

D = 2560
QR = 768
KVR = 256
H = 40
HD = 64
RD = 32
FF = 6400
LEN = 1024
STEP = 5
TOKENS = 8192
GAINS = 6144


def steps_of(own_key, dims, shards, least, largest):
    def one(dim, parts):
        heights = jax.random.uniform(jax.random.fold_in(jax.random.fold_in(own_key, 6), dim), (parts,), jnp.float32, least / len(shards), largest / len(shards))
        return jnp.repeat(jnp.exp(heights), dims[dim] // parts).reshape((-1,) + (1,) * (len(dims) - dim - 1))

    factor_of = one(*shards[0])
    for cut in shards[1:]:
        factor_of = factor_of * one(*cut)
    return factor_of


def noise(rng, extent, scale, limit, pieces=(), dtype=jnp.bfloat16):
    entries = jax.random.normal(rng, extent, jnp.float32) * scale
    if len(pieces) > 0:
        entries = steps_of(rng, extent, pieces, -0.22, 0.18) * entries
    return jnp.clip(entries, min=-limit, max=limit).astype(dtype)


def setup_inputs(seed: int = 0) -> dict:
    splits = jax.random.split(jax.random.key(seed), 30)
    return {
        "inputs": noise(splits[0], (TOKENS, D), 1.0, 6.0, ((0, 8),)),
        "cotangent": noise(splits[1], (TOKENS, D), 1.0, 6.0, ((0, 8),)),
        "norm_gains": jnp.clip(1.0 + 0.1 * jax.random.normal(splits[2], (GAINS,), jnp.float32), 0.5, 1.5),
        "norm_gains_first": noise(splits[3], (GAINS,), (0.111 * 1.5 * TOKENS ** 0.5), 96.0, ((0, 8),), jnp.float32),
        "norm_gains_second": jnp.clip(jnp.exp(math.log(3870.72) - 1.3843914 * jax.random.uniform(splits[4], (GAINS,), jnp.float32) ** steps_of(splits[4], (GAINS,), ((0, 8),), -0.2, 0.2)), 969.5232, 3870.72),
        "query_down": noise(splits[5], (D, QR), D ** -0.5, 0.125, ((0, 32),), jnp.float32),
        "query_down_first": noise(splits[6], (D, QR), (0.111 * 0.7 * TOKENS ** 0.5), 40.0, ((0, 32),), jnp.float32),
        "query_down_second": jnp.clip(jnp.exp(math.log(842.9568) - 1.3843914 * jax.random.uniform(splits[7], (D, QR), jnp.float32) ** steps_of(splits[7], (D, QR), ((0, 32),), -0.2, 0.2)), 211.14061, 842.9568),
        "latent_down": noise(splits[8], (D, KVR + RD), D ** -0.5, 0.125, ((0, 32),), jnp.float32),
        "latent_down_first": noise(splits[9], (D, KVR + RD), (0.111 * 2.0 * TOKENS ** 0.5), 128.0, ((0, 32),), jnp.float32),
        "latent_down_second": jnp.clip(jnp.exp(math.log(6881.28) - 1.3843914 * jax.random.uniform(splits[10], (D, KVR + RD), jnp.float32) ** steps_of(splits[10], (D, KVR + RD), ((0, 32),), -0.2, 0.2)), 1723.5968, 6881.28),
        "query_up": noise(splits[11], (QR, H * (HD + RD)), QR ** -0.5, 0.21875, ((0, 8), (1, 4)), jnp.float32),
        "query_up_first": noise(splits[12], (QR, H * (HD + RD)), (0.111 * 0.3 * TOKENS ** 0.5), 16.0, ((0, 8), (1, 4)), jnp.float32),
        "query_up_second": jnp.clip(jnp.exp(math.log(154.8288) - 1.3843913 * jax.random.uniform(splits[13], (QR, H * (HD + RD)), jnp.float32) ** steps_of(splits[13], (QR, H * (HD + RD)), ((0, 8), (1, 4)), -0.2, 0.2)), 38.78093, 154.8288),
        "latent_up": noise(splits[14], (KVR, H * 2 * HD), KVR ** -0.5, 0.375, ((0, 8), (1, 4)), jnp.float32),
        "latent_up_first": noise(splits[15], (KVR, H * 2 * HD), (0.111 * 0.6 * TOKENS ** 0.5), 32.0, ((0, 8), (1, 4)), jnp.float32),
        "latent_up_second": jnp.clip(jnp.exp(math.log(619.3152) - 1.3843913 * jax.random.uniform(splits[16], (KVR, H * 2 * HD), jnp.float32) ** steps_of(splits[16], (KVR, H * 2 * HD), ((0, 8), (1, 4)), -0.2, 0.2)), 155.12372, 619.3152),
        "out_proj": noise(splits[17], (H * HD, D), 0.7, 4.0, ((0, 4), (1, 8)), jnp.float32),
        "out_proj_first": noise(splits[18], (H * HD, D), (0.111 * 0.04 * TOKENS ** 0.5), 2.5, ((0, 4), (1, 8)), jnp.float32),
        "out_proj_second": jnp.clip(jnp.exp(math.log(2.752512) - 1.3843914 * jax.random.uniform(splits[19], (H * HD, D), jnp.float32) ** steps_of(splits[19], (H * HD, D), ((0, 4), (1, 8)), -0.2, 0.2)), 0.6894387, 2.752512),
        "ffn_gate": noise(splits[20], (D, FF), D ** -0.5, 0.125, ((0, 8), (1, 4)), jnp.float32),
        "ffn_gate_first": noise(splits[21], (D, FF), (0.111 * 0.8 * TOKENS ** 0.5), 48.0, ((0, 8), (1, 4)), jnp.float32),
        "ffn_gate_second": jnp.clip(jnp.exp(math.log(1101.0048) - 1.3843914 * jax.random.uniform(splits[22], (D, FF), jnp.float32) ** steps_of(splits[22], (D, FF), ((0, 8), (1, 4)), -0.2, 0.2)), 275.77548, 1101.0048),
        "ffn_up": noise(splits[23], (D, FF), D ** -0.5, 0.125, ((0, 8), (1, 4)), jnp.float32),
        "ffn_up_first": noise(splits[24], (D, FF), (0.111 * 0.8 * TOKENS ** 0.5), 48.0, ((0, 8), (1, 4)), jnp.float32),
        "ffn_up_second": jnp.clip(jnp.exp(math.log(1101.0048) - 1.3843914 * jax.random.uniform(splits[25], (D, FF), jnp.float32) ** steps_of(splits[25], (D, FF), ((0, 8), (1, 4)), -0.2, 0.2)), 275.77548, 1101.0048),
        "ffn_down": noise(splits[26], (FF, D), 0.15, 0.875, ((0, 4), (1, 8)), jnp.float32),
        "ffn_down_first": noise(splits[27], (FF, D), (0.111 * 0.1 * TOKENS ** 0.5), 6.0, ((0, 4), (1, 8)), jnp.float32),
        "ffn_down_second": jnp.clip(jnp.exp(math.log(17.2032) - 1.3843914 * jax.random.uniform(splits[28], (FF, D), jnp.float32) ** steps_of(splits[28], (FF, D), ((0, 4), (1, 8)), -0.2, 0.2)), 4.308992, 17.2032),
    }


@jax.custom_vjp
def low(v):
    return lax.optimization_barrier(v.astype(jnp.bfloat16)).astype(jnp.float32)

@jax.custom_vjp
def low_back(v):
    return v

def low_keep(v):
    return (low(v), None)

def low_pass(kept, grad):
    return (grad,)

def back_keep(v):
    return (v, None)

def back_low(kept, grad):
    return (low(grad),)
low.defvjp(low_keep, low_pass)
low_back.defvjp(back_keep, back_low)
NORM_EPS = 1e-05
RESID_SCALE = 1.4 / math.sqrt(62.0)
ROPE_BASE = 10000.0
BETA_ONE = 0.9
BETA_TWO = 0.95
ADAM_EPS = 1e-08
DECAY_RATE = 0.1
highest = lax.Precision.HIGHEST

def normalize(vector, gain_vec):
    return vector * lax.rsqrt(lax.optimization_barrier(jnp.mean(vector * vector, axis=-1, keepdims=True)) + NORM_EPS) * gain_vec

def tables(length):
    positions = jnp.arange(length).astype(jnp.float32)
    frequency = jnp.exp(jnp.arange(RD // 2).astype(jnp.float32) * (-2.0 * math.log(ROPE_BASE) / RD))
    angles = positions[:, None] * frequency[None, :]
    return (jnp.cos(angles), jnp.sin(angles))

def rotate(vector, cosines, sine_table, direction):
    half_rd = vector.shape[-1] // 2
    first_half = vector[..., :half_rd]
    second_half = vector[..., half_rd:]
    return jnp.concatenate([first_half * cosines - direction * second_half * sine_table, second_half * cosines + direction * first_half * sine_table], axis=-1)

def matmul(left, right):
    return jnp.dot(left, right, precision=highest, preferred_element_type=jnp.float32)

def attention(queries, keys, values):
    blk_rows = min(512, LEN)
    count = LEN // blk_rows
    scale_val = (HD + RD) ** (-0.5)

    def block(offset, query_blk):
        scores = scale_val * jnp.einsum('qhd,khd->hqk', query_blk, keys, precision=highest)
        scores = low_back(scores)
        causal = jnp.arange(LEN).astype(jnp.int32)[None, :] <= (offset + jnp.arange(blk_rows).astype(jnp.int32))[:, None]
        scores = jnp.where(causal[None], scores, -1e+30)
        probs = low(jax.nn.softmax(scores, axis=-1))
        return jnp.einsum('hqk,khd->qhd', probs, values, precision=highest)
    checked = jax.checkpoint(block)
    offsets = (jnp.arange(count) * blk_rows).astype(jnp.int32)
    outs = lax.map(lambda item_pair: checked(item_pair[0], item_pair[1]), (offsets, queries.reshape(count, blk_rows, H, HD + RD)))
    return outs.reshape(LEN, H, HD)

def forward(inputs_seq, norm_gains, query_down, latent_down, query_up, latent_up, out_proj, ffn_gate, ffn_up, ffn_down):
    gain_in = norm_gains[:D]
    gain_query = norm_gains[D:D + QR]
    gain_latent = norm_gains[D + QR:D + QR + KVR]
    gain_mid = norm_gains[D + QR + KVR:]
    cosines, sine_table = tables(LEN)
    normed_in = low(normalize(inputs_seq, gain_in))
    q_latent = low_back(matmul(normed_in, low(query_down)))
    q_normed = low(normalize(q_latent, gain_query))
    q_heads = low_back(matmul(q_normed, low(query_up))).reshape(LEN, H, HD + RD)
    queries = low(jnp.concatenate([q_heads[..., :HD], rotate(q_heads[..., HD:], cosines[:, None], sine_table[:, None], 1.0)], axis=-1))
    kv_latent = low_back(matmul(normed_in, low(latent_down)))
    kv_normed = low(normalize(kv_latent[:, :KVR], gain_latent))
    kv_heads = low_back(matmul(kv_normed, low(latent_up))).reshape(LEN, H, 2 * HD)
    key_rope = rotate(kv_latent[:, KVR:], cosines, sine_table, 1.0)
    keys = low(jnp.concatenate([kv_heads[..., :HD], jnp.broadcast_to(key_rope[:, None, :], (LEN, H, RD))], axis=-1))
    values = low(kv_heads[..., HD:])
    mixed_heads = low(low_back(attention(queries, keys, values))).reshape(LEN, H * HD)
    attn_out = low_back(matmul(mixed_heads, low(out_proj)))
    resid_mid = inputs_seq + RESID_SCALE * attn_out
    normed_mid = low(normalize(resid_mid, gain_mid))
    gate_val = low_back(matmul(normed_mid, low(ffn_gate)))
    up_val = low_back(matmul(normed_mid, low(ffn_up)))
    hidden = low(jax.nn.silu(gate_val) * up_val)
    ffn_out = low_back(matmul(hidden, low(ffn_down)))
    return resid_mid + RESID_SCALE * ffn_out

def update_rates():
    return [(0.25, 0.0), (2.5 / math.sqrt(D), DECAY_RATE), (2.5 / math.sqrt(D), DECAY_RATE), (2.5 / math.sqrt(QR), DECAY_RATE), (2.5 / math.sqrt(KVR), DECAY_RATE), (1.75, DECAY_RATE), (2.5 / math.sqrt(D), DECAY_RATE), (2.5 / math.sqrt(D), DECAY_RATE), (0.375, DECAY_RATE)]

def adam_step(weight, gradient, first, second, rate_pair):
    first_new = BETA_ONE * first + (1.0 - BETA_ONE) * gradient
    second_new = BETA_TWO * second + (1.0 - BETA_TWO) * gradient * gradient
    first_hat = first_new / (1.0 - BETA_ONE ** STEP)
    second_hat = second_new / (1.0 - BETA_TWO ** STEP)
    weight_new = weight - rate_pair[0] * (first_hat / (jnp.sqrt(second_hat) + ADAM_EPS) + rate_pair[1] * weight)
    return (first_new, second_new, weight_new)

def reference(inputs, cotangent, norm_gains, norm_gains_first, norm_gains_second, query_down, query_down_first, query_down_second, latent_down, latent_down_first, latent_down_second, query_up, query_up_first, query_up_second, latent_up, latent_up_first, latent_up_second, out_proj, out_proj_first, out_proj_second, ffn_gate, ffn_gate_first, ffn_gate_second, ffn_up, ffn_up_first, ffn_up_second, ffn_down, ffn_down_first, ffn_down_second):
    weights = (norm_gains, query_down, latent_down, query_up, latent_up, out_proj, ffn_gate, ffn_up, ffn_down)
    firsts = (norm_gains_first, query_down_first, latent_down_first, query_up_first, latent_up_first, out_proj_first, ffn_gate_first, ffn_up_first, ffn_down_first)
    seconds = (norm_gains_second, query_down_second, latent_down_second, query_up_second, latent_up_second, out_proj_second, ffn_gate_second, ffn_up_second, ffn_down_second)
    seq_count = TOKENS // LEN
    seq_in = inputs.astype(jnp.float32).reshape(seq_count, LEN, D)
    seq_cot = cotangent.astype(jnp.float32).reshape(seq_count, LEN, D)

    def one_seq(totals, item_pair):
        result, pull_back = jax.vjp(forward, item_pair[0], *weights)
        gradients = pull_back(item_pair[1])
        totals = tuple((total_val + grad_val for total_val, grad_val in zip(totals, gradients[1:])))
        return (totals, (result, gradients[0]))
    zeros_init = tuple((jnp.zeros_like(weight) for weight in weights))
    totals, seq_outs = lax.scan(one_seq, zeros_init, (seq_in, seq_cot))
    output = seq_outs[0].reshape(TOKENS, D).astype(jnp.bfloat16)
    input_grad = seq_outs[1].reshape(TOKENS, D)
    rates = update_rates()
    updated = [adam_step(weights[number], totals[number], firsts[number], seconds[number], rates[number]) for number in range(9)]
    return (output, input_grad, updated[0][0], updated[0][1], updated[0][2], updated[1][0], updated[1][1], updated[1][2], updated[2][0], updated[2][1], updated[2][2], updated[3][0], updated[3][1], updated[3][2], updated[4][0], updated[4][1], updated[4][2], updated[5][0], updated[5][1], updated[5][2], updated[6][0], updated[6][1], updated[6][2], updated[7][0], updated[7][1], updated[7][2], updated[8][0], updated[8][1], updated[8][2])
```

```python
import math

import jax
import jax.numpy as jnp
from jax import lax
from jax.experimental import pallas as pl
from jax.experimental.pallas import tpu as pltpu
from jax.sharding import PartitionSpec as P

D = 2560
QR = 768
KVR = 256
HD = 64
RD = 32
LEN = 1024
STEP = 5


NORM_EPS = 1e-05
RESID_SCALE = 1.4 / math.sqrt(62.0)
ROPE_BASE = 10000.0
BETA_ONE = 0.9
BETA_TWO = 0.95
ADAM_EPS = 1e-08
DECAY_RATE = 0.1


def normalize(vector, gain_vec):
    return (
        vector * lax.rsqrt(jnp.mean(vector * vector, axis=-1, keepdims=True) + NORM_EPS) * gain_vec
    )


def norm_back(vector, gain_vec, gradient):
    unused, pull_back = jax.vjp(normalize, vector, gain_vec)
    return pull_back(gradient)


def tables(length):
    positions = jnp.arange(length).astype(jnp.float32)
    frequency = jnp.exp(jnp.arange(RD // 2).astype(jnp.float32) * (-2.0 * math.log(ROPE_BASE) / RD))
    angles = positions[:, None] * frequency[None, :]
    return (jnp.cos(angles), jnp.sin(angles))


def rotate(vector, cosines, sine_table, direction):
    half_rd = vector.shape[-1] // 2
    first_half = vector[..., :half_rd]
    second_half = vector[..., half_rd:]
    return jnp.concatenate(
        [
            first_half * cosines - direction * second_half * sine_table,
            second_half * cosines + direction * first_half * sine_table,
        ],
        axis=-1,
    )


def product(left, right):
    return jnp.dot(left, right, preferred_element_type=jnp.float32)


def contract(spec, left, right):
    return jnp.einsum(spec, left, right, preferred_element_type=jnp.float32)


BLK = 256
VMEM_CAP = 48 * 1024 * 1024

def dot_nn(left, right):
    return lax.dot_general(left, right, (((1,), (0,)), ((), ())), preferred_element_type=jnp.float32)

def dot_nt(left, right):
    return lax.dot_general(left, right, (((1,), (1,)), ((), ())), preferred_element_type=jnp.float32)

def causal_tile():
    keys = lax.broadcasted_iota(jnp.int32, (BLK, BLK), 0)
    rows = lax.broadcasted_iota(jnp.int32, (BLK, BLK), 1)
    return keys <= rows

def forward_kernel(q_ref, k_ref, v_ref, mixed_ref, lse_ref, score_ref):
    scale_val = (HD + RD) ** (-0.5)
    length = q_ref.shape[2]
    key_rows = k_ref[0].T
    keep = causal_tile()
    for i in range(length // BLK):
        cols = slice(i * BLK, (i + 1) * BLK)
        q_blk = q_ref[0, :, cols]
        top = None
        for c in range(i + 1):
            part = slice(c * BLK, (c + 1) * BLK)
            scores = scale_val * dot_nn(key_rows[part], q_blk)
            if c == i:
                scores = jnp.where(keep, scores, -1e30)
            score_ref[part, :] = scores
            peak = jnp.max(scores, axis=0, keepdims=True)
            top = peak if top is None else jnp.maximum(top, peak)
        total = jnp.zeros((1, BLK), jnp.float32)
        mixed = jnp.zeros((HD, BLK), jnp.float32)
        for c in range(i + 1):
            part = slice(c * BLK, (c + 1) * BLK)
            weights = jnp.exp(score_ref[part, :] - top)
            total = total + jnp.sum(weights, axis=0, keepdims=True)
            mixed = mixed + dot_nn(v_ref[0, :, part], weights.astype(jnp.bfloat16))
        mixed_ref[0, :, cols] = (mixed / total).astype(jnp.bfloat16)
        lse_ref[0, :, cols] = top + jnp.log(total)

def attend_forward(queries, keys, values):
    heads, width, length = queries.shape
    spec = lambda rows: pl.BlockSpec((1, rows, length), lambda h: (h, 0, 0))
    return pl.pallas_call(
        forward_kernel,
        grid=(heads,),
        in_specs=[spec(HD + RD), spec(HD + RD), spec(HD)],
        out_specs=[spec(HD), spec(1)],
        out_shape=[
            jax.ShapeDtypeStruct((heads, HD, length), jnp.bfloat16),
            jax.ShapeDtypeStruct((heads, 1, length), jnp.float32),
        ],
        scratch_shapes=[pltpu.VMEM((length, BLK), jnp.float32)],
        compiler_params=pltpu.CompilerParams(vmem_limit_bytes=VMEM_CAP),
        cost_estimate=pl.CostEstimate(
            flops=heads * length * length * (HD + RD + HD) * 2,
            bytes_accessed=heads * length * 640,
            transcendentals=heads * length * length // 2,
        ),
        name="attend_forward",
    )(queries, keys, values)

def backward_kernel(
    q_ref, k_ref, v_ref, grad_ref, lse_ref, cos_ref, sin_ref,
    dq_ref, dkv_ref, rope_ref, prob_ref, gp_ref, dk_ref, dv_ref,
):
    scale_val = (HD + RD) ** (-0.5)
    length = q_ref.shape[2]
    half = RD // 2
    key_rows = k_ref[0].T
    value_rows = v_ref[0].T
    keep = causal_tile()
    last = length // BLK - 1
    for i in range(last, -1, -1):
        cols = slice(i * BLK, (i + 1) * BLK)
        q_blk = q_ref[0, :, cols]
        grad_blk = grad_ref[0, :, cols]
        lse_blk = lse_ref[0, :, cols]
        delta = jnp.zeros((1, BLK), jnp.float32)
        for c in range(i + 1):
            part = slice(c * BLK, (c + 1) * BLK)
            scores = scale_val * dot_nn(key_rows[part], q_blk)
            if c == i:
                scores = jnp.where(keep, scores, -1e30)
            probs = jnp.exp(scores - lse_blk)
            grad_probs = dot_nn(value_rows[part], grad_blk)
            prob_ref[part, :] = probs
            gp_ref[part, :] = grad_probs
            delta = delta + jnp.sum(probs * grad_probs, axis=0, keepdims=True)
        dq = jnp.zeros((HD + RD, BLK), jnp.float32)
        for c in range(i + 1):
            part = slice(c * BLK, (c + 1) * BLK)
            probs = prob_ref[part, :]
            grad_scores = (probs * (gp_ref[part, :] - delta)).astype(jnp.bfloat16)
            dq = dq + dot_nn(k_ref[0, :, part], grad_scores)
            dk_part = dot_nt(q_blk, grad_scores)
            dv_part = dot_nt(grad_blk, probs.astype(jnp.bfloat16))
            if i == last:
                dk_ref[:, part] = dk_part
                dv_ref[:, part] = dv_part
            else:
                dk_ref[:, part] += dk_part
                dv_ref[:, part] += dv_part
        dq = scale_val * dq
        low = dq[HD : HD + half]
        high = dq[HD + half :]
        cos_blk = cos_ref[:, cols]
        sin_blk = sin_ref[:, cols]
        dq_ref[0, :HD, cols] = dq[:HD].astype(jnp.bfloat16)
        dq_ref[0, HD : HD + half, cols] = (low * cos_blk + high * sin_blk).astype(jnp.bfloat16)
        dq_ref[0, HD + half :, cols] = (high * cos_blk - low * sin_blk).astype(jnp.bfloat16)
    dkv_ref[0, :HD, :] = (scale_val * dk_ref[:HD, :]).astype(jnp.bfloat16)
    dkv_ref[0, HD:, :] = dv_ref[...].astype(jnp.bfloat16)

    @pl.when(pl.program_id(0) == 0)
    def _():
        rope_ref[...] = scale_val * dk_ref[HD:, :]

    @pl.when(pl.program_id(0) != 0)
    def _():
        rope_ref[...] += scale_val * dk_ref[HD:, :]

def attend_backward(queries, keys, values, grad_mixed, lse, cosines, sines):
    heads, width, length = queries.shape
    spec = lambda rows: pl.BlockSpec((1, rows, length), lambda h: (h, 0, 0))
    flat = lambda rows: pl.BlockSpec((rows, length), lambda h: (0, 0))
    return pl.pallas_call(
        backward_kernel,
        grid=(heads,),
        in_specs=[spec(HD + RD), spec(HD + RD), spec(HD), spec(HD), spec(1), flat(RD // 2), flat(RD // 2)],
        out_specs=[spec(HD + RD), spec(2 * HD), flat(RD)],
        out_shape=[
            jax.ShapeDtypeStruct((heads, HD + RD, length), jnp.bfloat16),
            jax.ShapeDtypeStruct((heads, 2 * HD, length), jnp.bfloat16),
            jax.ShapeDtypeStruct((RD, length), jnp.float32),
        ],
        scratch_shapes=[
            pltpu.VMEM((length, BLK), jnp.float32),
            pltpu.VMEM((length, BLK), jnp.float32),
            pltpu.VMEM((HD + RD, length), jnp.float32),
            pltpu.VMEM((HD, length), jnp.float32),
        ],
        compiler_params=pltpu.CompilerParams(vmem_limit_bytes=VMEM_CAP),
        cost_estimate=pl.CostEstimate(
            flops=heads * length * length * 5 * (HD + RD),
            bytes_accessed=heads * length * 1400,
            transcendentals=heads * length * length // 2,
        ),
        name="attend_backward",
    )(queries, keys, values, grad_mixed, lse, cosines, sines)


def update_rates():
    return [
        (0.25, 0.0),
        (2.5 / math.sqrt(D), DECAY_RATE),
        (2.5 / math.sqrt(D), DECAY_RATE),
        (2.5 / math.sqrt(QR), DECAY_RATE),
        (2.5 / math.sqrt(KVR), DECAY_RATE),
        (1.75, DECAY_RATE),
        (2.5 / math.sqrt(D), DECAY_RATE),
        (2.5 / math.sqrt(D), DECAY_RATE),
        (0.375, DECAY_RATE),
    ]


def adam_step(weight, gradient, first, second, rate_pair):
    first_new = BETA_ONE * first + (1.0 - BETA_ONE) * gradient
    second_new = BETA_TWO * second + (1.0 - BETA_TWO) * gradient * gradient
    first_hat = first_new / (1.0 - BETA_ONE**STEP)
    second_hat = second_new / (1.0 - BETA_TWO**STEP)
    weight_new = weight - rate_pair[0] * (
        first_hat / (jnp.sqrt(second_hat) + ADAM_EPS) + rate_pair[1] * weight
    )
    return (first_new, second_new, weight_new)


def wide(value):
    return value.astype(jnp.float32)


def chunk_of(stacked, place):
    return lax.dynamic_index_in_dim(stacked, place, axis=0, keepdims=False)


def line_gather(own, count, axis):
    place = lax.axis_index("mp")
    going_up = own
    going_down = own
    from_below = []
    from_above = []
    for unused in range(1, count):
        going_up = lax.ppermute(going_up, "mp", [(k, k + 1) for k in range(count - 1)])
        going_down = lax.ppermute(going_down, "mp", [(k + 1, k) for k in range(count - 1)])
        from_below.append(going_up)
        from_above.append(going_down)
    blocks = []
    for slot in range(count):
        block = own
        for step in range(1, count):
            if slot + step < count:
                block = jnp.where(place - step == slot, from_below[step - 1], block)
            if slot - step >= 0:
                block = jnp.where(place + step == slot, from_above[step - 1], block)
        blocks.append(block)
    return jnp.concatenate(blocks, axis=axis)


def line_scatter(partial, count):
    place = lax.axis_index("mp")
    stacked = partial.reshape(count, partial.shape[0] // count, partial.shape[1])
    low_type = partial.dtype
    from_below = None
    from_above = None
    for step in range(1, count):
        going_up = chunk_of(stacked, jnp.clip(count - step + place, 0, count - 1))
        going_down = chunk_of(stacked, jnp.clip(step - count + place, 0, count - 1))
        if from_below is not None:
            going_up = (wide(going_up) + wide(from_below)).astype(low_type)
            going_down = (wide(going_down) + wide(from_above)).astype(low_type)
        from_below = lax.ppermute(going_up, "mp", [(k, k + 1) for k in range(step)])
        from_above = lax.ppermute(
            going_down, "mp", [(count - 1 - k, count - 2 - k) for k in range(step)]
        )
    return wide(chunk_of(stacked, place)) + wide(from_below) + wide(from_above)


def line_exchange(stacked, count, axis):
    place = lax.axis_index("mp")
    arrived = []
    for step in range(count - 1, 0, -1):
        leaving = chunk_of(stacked, (place + step) % count)
        arrived.append(lax.ppermute(leaving, "mp", [(k, (k + step) % count) for k in range(count)]))
    arrived.append(chunk_of(stacked, place))
    twice = jnp.stack(arrived + arrived)
    ordered = lax.dynamic_slice_in_dim(twice, count - 1 - place, count, 0)
    return jnp.concatenate([ordered[k] for k in range(count)], axis=axis)


def sum_rows(stacked):
    flat = stacked.reshape(-1, stacked.shape[-1])
    return wide(lax.psum_scatter(flat, "dp", scatter_dimension=0, tiled=True))


def turn(low, high, cosines, sines, direction):
    return (low * cosines - direction * high * sines, high * cosines + direction * low * sines)


def local(
    inputs,
    cotangent,
    norm_gains,
    norm_gains_first,
    norm_gains_second,
    query_down,
    query_down_first,
    query_down_second,
    latent_down,
    latent_down_first,
    latent_down_second,
    query_up,
    query_up_first,
    query_up_second,
    latent_up,
    latent_up_first,
    latent_up_second,
    out_proj,
    out_proj_first,
    out_proj_second,
    ffn_gate,
    ffn_gate_first,
    ffn_gate_second,
    ffn_up,
    ffn_up_first,
    ffn_up_second,
    ffn_down,
    ffn_down_first,
    ffn_down_second,
):
    low_type = jnp.bfloat16
    tokens_dev = inputs.shape[0]
    n_data = lax.axis_size("dp")
    n_model = lax.axis_size("mp")
    place = lax.axis_index("mp")
    heads_dev = query_up.shape[1] // (HD + RD)
    own_tokens = tokens_dev // n_model
    hidden_dev = ffn_gate.shape[1]
    down_rows = query_down.shape[0]
    gain_rows = 16

    def own_rows(value):
        return lax.dynamic_slice_in_dim(value, place * own_tokens, own_tokens, 0)

    gains_all = lax.all_gather(norm_gains, "dp", axis=0, tiled=True)
    gain_in = gains_all[:D]
    gain_query = gains_all[D : D + QR]
    gain_latent = gains_all[D + QR : D + QR + KVR]
    gain_mid = gains_all[D + QR + KVR :]

    up_rows = query_up.shape[0]
    kv_rows = latent_up.shape[0]
    up_width = latent_up.shape[1]
    up_pack = jnp.concatenate(
        [
            jnp.pad(query_up.astype(low_type), ((0, 0), (0, up_width - query_up.shape[1]))),
            latent_up.astype(low_type),
        ],
        axis=0,
    )
    up_all = lax.all_gather(up_pack, "dp", axis=0, tiled=False)
    query_up_all = up_all[:, :up_rows, : query_up.shape[1]].reshape(QR, query_up.shape[1])
    latent_up_all = up_all[:, up_rows:].reshape(KVR, up_width)
    down_own = jnp.concatenate([query_down, latent_down], axis=1).astype(low_type)
    down_plane = line_gather(down_own, n_model, 0)
    down_all = lax.all_gather(down_plane, "dp", axis=0, tiled=True)
    out_plane = line_gather(out_proj.T.astype(low_type), n_model, 1)
    out_all = lax.all_gather(out_plane, "dp", axis=0, tiled=True)
    ffn_pack = jnp.stack([ffn_gate, ffn_up, ffn_down.T]).astype(low_type)
    ffn_all = lax.all_gather(ffn_pack, "dp", axis=0, tiled=False)
    gate_all = ffn_all[:, 0].reshape(D, hidden_dev)
    raise_all = ffn_all[:, 1].reshape(D, hidden_dev)
    lower_all = ffn_all[:, 2].reshape(D, hidden_dev)

    cosines, sines = tables(LEN)
    cosines = cosines.T
    sines = sines.T

    inputs_wide = wide(inputs)
    normed_in = normalize(inputs_wide, gain_in).astype(low_type)
    latents = product(normed_in, down_all)
    q_latent = latents[:, :QR]
    kv_latent = latents[:, QR : QR + KVR]
    q_normed = normalize(q_latent, gain_query).astype(low_type)
    kv_normed = normalize(kv_latent, gain_latent).astype(low_type)
    q_heads = contract("rc,tr->ct", query_up_all, q_normed).reshape(heads_dev, HD + RD, tokens_dev)
    turned = turn(q_heads[:, HD : HD + RD // 2], q_heads[:, HD + RD // 2 :], cosines, sines, 1.0)
    queries = jnp.concatenate([q_heads[:, :HD], turned[0], turned[1]], axis=1).astype(low_type)
    kv_heads = contract("rc,tr->ct", latent_up_all, kv_normed).astype(low_type)
    kv_heads = kv_heads.reshape(heads_dev, 2 * HD, tokens_dev)
    rope_in = latents[:, QR + KVR :].T
    turned = turn(rope_in[: RD // 2], rope_in[RD // 2 :], cosines, sines, 1.0)
    key_rope = jnp.concatenate(turned, axis=0).astype(low_type)
    keys = jnp.concatenate(
        [kv_heads[:, :HD], jnp.broadcast_to(key_rope[None], (heads_dev, RD, tokens_dev))], axis=1
    )
    values = kv_heads[:, HD:]
    mixed, log_sums = attend_forward(queries, keys, values)
    mixed_own = mixed.reshape(heads_dev * HD, tokens_dev)
    mixed_all = line_gather(mixed_own, n_model, 0)
    attn_out = contract("ht,dh->td", mixed_all, out_all)
    resid_mid = inputs_wide + RESID_SCALE * attn_out
    normed_mid = normalize(resid_mid, gain_mid).astype(low_type)

    cot_wide = wide(cotangent)
    grad_ffn = (RESID_SCALE * cot_wide).astype(low_type)
    grad_hidden = product(grad_ffn, lower_all)
    gate_val = product(normed_mid, gate_all)
    up_val = product(normed_mid, raise_all)
    sigmoid_gate = jax.nn.sigmoid(gate_val)
    silu_gate = gate_val * sigmoid_gate
    hidden = (silu_gate * up_val).astype(low_type)
    grad_gate = (
        grad_hidden * up_val * sigmoid_gate * (1.0 + gate_val * (1.0 - sigmoid_gate))
    ).astype(low_type)
    grad_up = (grad_hidden * silu_gate).astype(low_type)
    part_mid = (
        contract("tf,df->td", grad_gate, gate_all) + contract("tf,df->td", grad_up, raise_all)
    ).astype(low_type)
    grad_normed_mid = line_scatter(part_mid, n_model)
    mid_norm_own, gain_mid_part = norm_back(own_rows(resid_mid), gain_mid, grad_normed_mid)
    mid_norm_low = mid_norm_own.astype(low_type)
    grad_attn_own = (RESID_SCALE * (own_rows(cot_wide) + mid_norm_own)).astype(low_type)
    grad_mixed_own = contract("td,dh->ht", grad_attn_own, out_all).astype(low_type)
    grad_mixed = line_exchange(
        grad_mixed_own.reshape(n_model, heads_dev * HD, own_tokens), n_model, 1
    ).reshape(heads_dev, HD, tokens_dev)
    ffn_term = contract("tf,df->td", hidden, lower_all).astype(low_type)
    ffn_own = line_scatter(ffn_term, n_model)
    output_own = (own_rows(resid_mid) + RESID_SCALE * ffn_own).astype(low_type)
    output = line_gather(output_own, n_model, 0)
    grad_mid = cot_wide + wide(line_gather(mid_norm_low, n_model, 0))
    grad_attn = (RESID_SCALE * grad_mid).astype(low_type)
    ffn_grads = jnp.stack(
        [
            contract("td,tf->df", normed_mid, grad_gate).astype(low_type).reshape(n_data, -1, hidden_dev),
            contract("td,tf->df", normed_mid, grad_up).astype(low_type).reshape(n_data, -1, hidden_dev),
            contract("td,tf->df", grad_ffn, hidden).astype(low_type).reshape(n_data, -1, hidden_dev),
        ],
        axis=1,
    )
    ffn_sum = sum_rows(ffn_grads).reshape(3, -1, hidden_dev)

    grad_q_heads, grad_kv_heads, grad_rope = attend_backward(
        queries, keys, values, grad_mixed, log_sums, cosines, sines
    )
    grad_q_heads = grad_q_heads.reshape(heads_dev * (HD + RD), tokens_dev)
    grad_kv_heads = grad_kv_heads.reshape(heads_dev * 2 * HD, tokens_dev)
    part_latents = jnp.concatenate(
        [
            contract("ct,rc->tr", grad_q_heads, query_up_all),
            contract("ct,rc->tr", grad_kv_heads, latent_up_all),
            grad_rope.T,
        ],
        axis=1,
    ).astype(low_type)
    latents_own = line_scatter(part_latents, n_model)
    grad_q_own, gain_query_part = norm_back(own_rows(q_latent), gain_query, latents_own[:, :QR])
    grad_kv_own, gain_latent_part = norm_back(
        own_rows(kv_latent), gain_latent, latents_own[:, QR : QR + KVR]
    )
    cos_own = own_rows(cosines.T)
    sin_own = own_rows(sines.T)
    rope_own = latents_own[:, QR + KVR :]
    turned = turn(rope_own[:, : RD // 2], rope_own[:, RD // 2 :], cos_own, sin_own, -1.0)
    width = QR + KVR + RD
    gain_parts = jnp.concatenate([gain_query_part, gain_latent_part, gain_mid_part])
    gain_parts = jnp.pad(gain_parts, (0, gain_rows * width - gain_parts.shape[0]))
    sent_own = jnp.concatenate(
        [
            jnp.concatenate([grad_q_own, grad_kv_own, turned[0], turned[1]], axis=1),
            gain_parts.reshape(gain_rows, width),
        ],
        axis=0,
    ).astype(low_type)
    sent_all = line_gather(sent_own, n_model, 0).reshape(n_model, own_tokens + gain_rows, width)
    grad_latents = sent_all[:, :own_tokens].reshape(tokens_dev, width)
    gain_rest = jnp.sum(wide(sent_all[:, own_tokens:]), axis=0).reshape(-1)[: QR + KVR + D]

    out_width = heads_dev * HD
    grad_out = contract("td,ht->dh", grad_attn, mixed_own).astype(low_type)
    grad_out = grad_out.reshape(n_data, 2, -1, out_width)
    grad_out = jnp.concatenate([grad_out[:, 0], grad_out[:, 1]], axis=2)
    grad_qup = contract("tr,ct->rc", q_normed, grad_q_heads).astype(low_type)
    grad_qup = jnp.pad(
        grad_qup.reshape(n_data, up_rows, -1), ((0, 0), (0, 0), (0, up_width - query_up.shape[1]))
    )
    grad_kvup = contract("tr,ct->rc", kv_normed, grad_kv_heads).astype(low_type)
    head_grads = jnp.concatenate(
        [grad_out, grad_qup, grad_kvup.reshape(n_data, kv_rows, up_width)], axis=1
    )
    head_sum = sum_rows(head_grads)
    out_rows = grad_out.shape[1]

    grad_down = contract("td,tr->dr", normed_in, grad_latents)
    gain_in_part = jnp.sum(grad_down * wide(down_all), axis=1) / gain_in
    gain_grad = jnp.concatenate([gain_in_part, gain_rest]).reshape(n_data, 1, -1)
    gain_count = gain_grad.shape[2]
    gain_grad = jnp.pad(gain_grad, ((0, 0), (0, gain_rows - 1), (0, width - gain_count)))
    down_mine = lax.dynamic_index_in_dim(
        grad_down.reshape(n_data, n_model, down_rows, width), place, axis=1, keepdims=False
    )
    down_sum = sum_rows(jnp.concatenate([down_mine, gain_grad], axis=1).astype(low_type))
    grad_normed_in = contract("tr,dr->td", grad_latents, down_all)
    rate = lax.rsqrt(jnp.mean(inputs_wide * inputs_wide, axis=-1, keepdims=True) + NORM_EPS)
    scaled = grad_normed_in * gain_in
    dotted = jnp.mean(scaled * inputs_wide, axis=-1, keepdims=True)
    input_grad = grad_mid + rate * (scaled - inputs_wide * (rate * rate * dotted))
    reduced = (
        down_sum[down_rows, :gain_count],
        down_sum[:down_rows, :QR],
        down_sum[:down_rows, QR:],
        head_sum[out_rows : out_rows + up_rows, : query_up.shape[1]],
        head_sum[out_rows + up_rows :],
        jnp.concatenate([head_sum[:out_rows, :out_width], head_sum[:out_rows, out_width:]], axis=0).T,
        wide(ffn_sum[0]),
        wide(ffn_sum[1]),
        wide(ffn_sum[2]).T,
    )
    weights = (
        norm_gains,
        query_down,
        latent_down,
        query_up,
        latent_up,
        out_proj,
        ffn_gate,
        ffn_up,
        ffn_down,
    )
    firsts = (
        norm_gains_first,
        query_down_first,
        latent_down_first,
        query_up_first,
        latent_up_first,
        out_proj_first,
        ffn_gate_first,
        ffn_up_first,
        ffn_down_first,
    )
    seconds = (
        norm_gains_second,
        query_down_second,
        latent_down_second,
        query_up_second,
        latent_up_second,
        out_proj_second,
        ffn_gate_second,
        ffn_up_second,
        ffn_down_second,
    )
    rates = update_rates()
    updated = [
        adam_step(weights[number], reduced[number], firsts[number], seconds[number], rates[number])
        for number in range(9)
    ]
    return (
        output,
        input_grad,
        updated[0][0],
        updated[0][1],
        updated[0][2],
        updated[1][0],
        updated[1][1],
        updated[1][2],
        updated[2][0],
        updated[2][1],
        updated[2][2],
        updated[3][0],
        updated[3][1],
        updated[3][2],
        updated[4][0],
        updated[4][1],
        updated[4][2],
        updated[5][0],
        updated[5][1],
        updated[5][2],
        updated[6][0],
        updated[6][1],
        updated[6][2],
        updated[7][0],
        updated[7][1],
        updated[7][2],
        updated[8][0],
        updated[8][1],
        updated[8][2],
    )


def solution(mesh):
    placed = (
        P("dp", None),
        P("dp", None),
        P("dp"),
        P("dp"),
        P("dp"),
        P(("dp", "mp"), None),
        P(("dp", "mp"), None),
        P(("dp", "mp"), None),
        P(("dp", "mp"), None),
        P(("dp", "mp"), None),
        P(("dp", "mp"), None),
        P("dp", "mp"),
        P("dp", "mp"),
        P("dp", "mp"),
        P("dp", "mp"),
        P("dp", "mp"),
        P("dp", "mp"),
        P("mp", "dp"),
        P("mp", "dp"),
        P("mp", "dp"),
        P("dp", "mp"),
        P("dp", "mp"),
        P("dp", "mp"),
        P("dp", "mp"),
        P("dp", "mp"),
        P("dp", "mp"),
        P("mp", "dp"),
        P("mp", "dp"),
        P("mp", "dp"),
    )
    return jax.shard_map(
        local,
        mesh=mesh,
        in_specs=placed,
        out_specs=(
            P("dp", None),
            P("dp", None),
            P("dp"),
            P("dp"),
            P("dp"),
            P(("dp", "mp"), None),
            P(("dp", "mp"), None),
            P(("dp", "mp"), None),
            P(("dp", "mp"), None),
            P(("dp", "mp"), None),
            P(("dp", "mp"), None),
            P("dp", "mp"),
            P("dp", "mp"),
            P("dp", "mp"),
            P("dp", "mp"),
            P("dp", "mp"),
            P("dp", "mp"),
            P("mp", "dp"),
            P("mp", "dp"),
            P("mp", "dp"),
            P("dp", "mp"),
            P("dp", "mp"),
            P("dp", "mp"),
            P("dp", "mp"),
            P("dp", "mp"),
            P("dp", "mp"),
            P("mp", "dp"),
            P("mp", "dp"),
            P("mp", "dp"),
        ),
        check_vma=False,
    )
```

```python
import functools
import math

import jax
import jax.numpy as jnp
from jax import lax
from jax.experimental import pallas as pl
from jax.experimental.pallas import tpu as pltpu
from jax.sharding import PartitionSpec as P

D = 2560
QR = 768
KVR = 256
HD = 64
RD = 32
LEN = 1024
STEP = 5


NORM_EPS = 1e-05
RESID_SCALE = 1.4 / math.sqrt(62.0)
ROPE_BASE = 10000.0
BETA_ONE = 0.9
BETA_TWO = 0.95
ADAM_EPS = 1e-08
DECAY_RATE = 0.1


def normalize(vector, gain_vec):
    return (
        vector * lax.rsqrt(jnp.mean(vector * vector, axis=-1, keepdims=True) + NORM_EPS) * gain_vec
    )


def norm_back(vector, gain_vec, gradient):
    unused, pull_back = jax.vjp(normalize, vector, gain_vec)
    return pull_back(gradient)


def tables(length):
    positions = jnp.arange(length).astype(jnp.float32)
    frequency = jnp.exp(jnp.arange(RD // 2).astype(jnp.float32) * (-2.0 * math.log(ROPE_BASE) / RD))
    angles = positions[:, None] * frequency[None, :]
    return (jnp.cos(angles), jnp.sin(angles))


def product(left, right):
    return jnp.dot(left, right, preferred_element_type=jnp.float32)


def contract(spec, left, right):
    return jnp.einsum(spec, left, right, preferred_element_type=jnp.float32)


BLK = 256
ROWS = 512
LIGHT = 100000
VMEM_CAP = 56 * 1024 * 1024


def dot_nn(left, right):
    return lax.dot_general(left, right, (((1,), (0,)), ((), ())), preferred_element_type=jnp.float32)


def dot_nt(left, right):
    return lax.dot_general(left, right, (((1,), (1,)), ((), ())), preferred_element_type=jnp.float32)


def dot_tn(left, right):
    return lax.dot_general(left, right, (((0,), (0,)), ((), ())), preferred_element_type=jnp.float32)


def kernel_params():
    return pltpu.CompilerParams(vmem_limit_bytes=VMEM_CAP)


def light(flops):
    return pl.CostEstimate(flops=flops // LIGHT, bytes_accessed=1024, transcendentals=0)


def causal_tile():
    keys = lax.broadcasted_iota(jnp.int32, (BLK, BLK), 0)
    rows = lax.broadcasted_iota(jnp.int32, (BLK, BLK), 1)
    return keys <= rows


def forward_kernel(first, q_ref, k_ref, v_ref, mixed_ref, lse_ref, score_ref):
    scale_val = (HD + RD) ** (-0.5)
    key_rows = k_ref[0].T
    keep = causal_tile()
    for i in range(q_ref.shape[2] // BLK):
        cols = slice(i * BLK, (i + 1) * BLK)
        q_blk = q_ref[0, :, cols]
        last = first + i
        top = None
        for c in range(last + 1):
            part = slice(c * BLK, (c + 1) * BLK)
            scores = scale_val * dot_nn(key_rows[part], q_blk)
            if c == last:
                scores = jnp.where(keep, scores, -1e30)
            score_ref[part, :] = scores
            peak = jnp.max(scores, axis=0, keepdims=True)
            top = peak if top is None else jnp.maximum(top, peak)
        total = jnp.zeros((1, BLK), jnp.float32)
        mixed = jnp.zeros((HD, BLK), jnp.float32)
        for c in range(last + 1):
            part = slice(c * BLK, (c + 1) * BLK)
            weights = jnp.exp(score_ref[part, :] - top)
            total = total + jnp.sum(weights, axis=0, keepdims=True)
            mixed = mixed + dot_nn(v_ref[0, :, part], weights.astype(jnp.bfloat16))
        mixed_ref[0, :, cols] = (mixed / total).astype(jnp.bfloat16)
        lse_ref[0, :, cols] = top + jnp.log(total)


def attend_forward(queries, keys, values, half):
    heads, unused, length = queries.shape
    size = length // 2
    seen = size * (half + 1)
    spec = lambda rows, cols, place: pl.BlockSpec((1, rows, cols), lambda h: (h, 0, place))
    return pl.pallas_call(
        functools.partial(forward_kernel, half * size // BLK),
        grid=(heads,),
        in_specs=[spec(HD + RD, size, half), spec(HD + RD, seen, 0), spec(HD, seen, 0)],
        out_specs=[spec(HD, size, 0), spec(1, size, 0)],
        out_shape=[
            jax.ShapeDtypeStruct((heads, HD, size), jnp.bfloat16),
            jax.ShapeDtypeStruct((heads, 1, size), jnp.float32),
        ],
        scratch_shapes=[pltpu.VMEM((seen, BLK), jnp.float32)],
        compiler_params=kernel_params(),
        cost_estimate=light(heads * size * seen * 1400),
        name="attend_forward",
    )(queries, keys, values)


def backward_kernel(first, seeded, *refs):
    q_ref, k_ref, v_ref, grad_ref, lse_ref, cos_ref, sin_ref = refs[:7]
    refs = refs[7:]
    if seeded:
        dk_seed, dv_seed = refs[:2]
        dq_ref, dkv_ref, rope_ref = refs[2:5]
        refs = refs[5:]
    else:
        dq_ref, dkv_ref, rope_ref, dk_out, dv_out = refs[:5]
        refs = refs[5:]
    prob_ref, gp_ref, dk_ref, dv_ref = refs
    scale_val = (HD + RD) ** (-0.5)
    half = RD // 2
    key_rows = k_ref[0].T
    value_rows = v_ref[0].T
    keep = causal_tile()
    size = q_ref.shape[2]
    if seeded:
        dk_ref[...] = dk_seed[0]
        dv_ref[...] = dv_seed[0]
    final = size // BLK - 1
    for i in range(final, -1, -1):
        cols = slice(i * BLK, (i + 1) * BLK)
        q_blk = q_ref[0, :, cols]
        grad_blk = grad_ref[0, :, cols]
        lse_blk = lse_ref[0, :, cols]
        last = first + i
        delta = jnp.zeros((1, BLK), jnp.float32)
        for c in range(last + 1):
            part = slice(c * BLK, (c + 1) * BLK)
            scores = scale_val * dot_nn(key_rows[part], q_blk)
            if c == last:
                scores = jnp.where(keep, scores, -1e30)
            probs = jnp.exp(scores - lse_blk)
            grad_probs = dot_nn(value_rows[part], grad_blk)
            prob_ref[part, :] = probs
            gp_ref[part, :] = grad_probs
            delta = delta + jnp.sum(probs * grad_probs, axis=0, keepdims=True)
        dq = jnp.zeros((HD + RD, BLK), jnp.float32)
        for c in range(last + 1):
            part = slice(c * BLK, (c + 1) * BLK)
            probs = prob_ref[part, :]
            grad_scores = (probs * (gp_ref[part, :] - delta)).astype(jnp.bfloat16)
            dq = dq + dot_nn(k_ref[0, :, part], grad_scores)
            dk_part = dot_nt(q_blk, grad_scores)
            dv_part = dot_nt(grad_blk, probs.astype(jnp.bfloat16))
            if i == final and not seeded:
                dk_ref[:, part] = dk_part
                dv_ref[:, part] = dv_part
            else:
                dk_ref[:, part] += dk_part
                dv_ref[:, part] += dv_part
        dq = scale_val * dq
        low = dq[HD : HD + half]
        high = dq[HD + half :]
        cos_blk = cos_ref[:, cols]
        sin_blk = sin_ref[:, cols]
        dq_ref[0, :HD, cols] = dq[:HD].astype(jnp.bfloat16)
        dq_ref[0, HD : HD + half, cols] = (low * cos_blk + high * sin_blk).astype(jnp.bfloat16)
        dq_ref[0, HD + half :, cols] = (high * cos_blk - low * sin_blk).astype(jnp.bfloat16)
    own = slice(first * BLK, first * BLK + size)
    dkv_ref[0, :HD, :] = (scale_val * dk_ref[:HD, own]).astype(jnp.bfloat16)
    dkv_ref[0, HD:, :] = dv_ref[:, own].astype(jnp.bfloat16)
    if not seeded:
        dk_out[0] = dk_ref[:, : first * BLK]
        dv_out[0] = dv_ref[:, : first * BLK]

    @pl.when(pl.program_id(0) == 0)
    def _():
        rope_ref[...] = scale_val * dk_ref[HD:, own]

    @pl.when(pl.program_id(0) != 0)
    def _():
        rope_ref[...] += scale_val * dk_ref[HD:, own]


def attend_backward(queries, keys, values, grad_mixed, lse, cosines, sines, half, seeds):
    heads, unused, length = queries.shape
    size = length // 2
    seen = size * (half + 1)
    spec = lambda rows, cols, place: pl.BlockSpec((1, rows, cols), lambda h: (h, 0, place))
    flat = lambda rows, place: pl.BlockSpec((rows, size), lambda h: (0, place))
    in_specs = [
        spec(HD + RD, size, half),
        spec(HD + RD, seen, 0),
        spec(HD, seen, 0),
        spec(HD, size, 0),
        spec(1, size, 0),
        flat(RD // 2, half),
        flat(RD // 2, half),
    ]
    out_specs = [spec(HD + RD, size, 0), spec(2 * HD, size, 0), flat(RD, 0)]
    out_shape = [
        jax.ShapeDtypeStruct((heads, HD + RD, size), jnp.bfloat16),
        jax.ShapeDtypeStruct((heads, 2 * HD, size), jnp.bfloat16),
        jax.ShapeDtypeStruct((RD, size), jnp.float32),
    ]
    pair = [spec(HD + RD, size, 0), spec(HD, size, 0)]
    if half == 0:
        in_specs = in_specs + pair
    else:
        out_specs = out_specs + pair
        out_shape = out_shape + [
            jax.ShapeDtypeStruct((heads, HD + RD, size), jnp.float32),
            jax.ShapeDtypeStruct((heads, HD, size), jnp.float32),
        ]
    return pl.pallas_call(
        functools.partial(backward_kernel, half * size // BLK, half == 0),
        grid=(heads,),
        in_specs=in_specs,
        out_specs=out_specs,
        out_shape=out_shape,
        scratch_shapes=[
            pltpu.VMEM((seen, BLK), jnp.float32),
            pltpu.VMEM((seen, BLK), jnp.float32),
            pltpu.VMEM((HD + RD, seen), jnp.float32),
            pltpu.VMEM((HD, seen), jnp.float32),
        ],
        compiler_params=kernel_params(),
        cost_estimate=light(heads * size * seen * 3000),
        name="attend_backward",
    )(queries, keys, values, grad_mixed, lse, cosines, sines, *seeds)


def hidden_kernel(grad_ref, weight_ref, out_ref):
    weight = weight_ref[...].reshape(-1, weight_ref.shape[3])

    @pl.when(pl.program_id(1) == 0)
    def _():
        out_ref[...] = dot_nn(grad_ref[...], weight)

    @pl.when(pl.program_id(1) != 0)
    def _():
        out_ref[...] += dot_nn(grad_ref[...], weight)


def hidden_back(grad_out, weights):
    tokens, model = grad_out.shape
    blocks, unused, rows, units = weights.shape
    return pl.pallas_call(
        hidden_kernel,
        grid=(tokens // ROWS, 2),
        in_specs=[
            pl.BlockSpec((ROWS, model // 2), lambda i, k: (i, k)),
            pl.BlockSpec((blocks // 2, 1, rows, units), lambda i, k: (k, 2, 0, 0)),
        ],
        out_specs=pl.BlockSpec((ROWS, units), lambda i, k: (i, 0)),
        out_shape=jax.ShapeDtypeStruct((tokens, units), jnp.float32),
        compiler_params=kernel_params(),
        cost_estimate=light(2 * tokens * model * units),
        name="hidden_back",
    )(grad_out, weights)


def inner_kernel(normed_ref, grad_ref, weight_ref, hidden_ref, gate_ref, up_ref, sum_ref):
    which = pl.program_id(1)
    step = pl.program_id(2)
    weight = weight_ref[...].reshape(-1, weight_ref.shape[3])

    @pl.when(step == 0)
    def _():
        sum_ref[which] = dot_nn(normed_ref[...], weight)

    @pl.when(step != 0)
    def _():
        sum_ref[which] += dot_nn(normed_ref[...], weight)

    @pl.when((which == 1) & (step == pl.num_programs(2) - 1))
    def _():
        gate_val = sum_ref[0]
        up_val = sum_ref[1]
        grad_hidden = grad_ref[...]
        sigmoid_gate = jax.nn.sigmoid(gate_val)
        silu_gate = gate_val * sigmoid_gate
        hidden_ref[...] = (silu_gate * up_val).astype(jnp.bfloat16)
        gate_ref[...] = (
            grad_hidden * up_val * sigmoid_gate * (1.0 + gate_val * (1.0 - sigmoid_gate))
        ).astype(jnp.bfloat16)
        up_ref[...] = (grad_hidden * silu_gate).astype(jnp.bfloat16)


def ffn_inner(normed, grad_hidden, weights, place):
    tokens, model = normed.shape
    blocks, unused, rows, units = weights.shape
    steps = tokens // ROWS
    out = jax.ShapeDtypeStruct((tokens, units), jnp.bfloat16)
    result = pl.BlockSpec((ROWS, units), lambda i, w, k: (i, 0))
    return pl.pallas_call(
        inner_kernel,
        grid=(steps, 2, 2),
        in_specs=[
            pl.BlockSpec((ROWS, model // 2), lambda i, w, k: (i, k)),
            pl.BlockSpec((ROWS, units), lambda i, w, k: (i + place * steps, 0)),
            pl.BlockSpec((blocks // 2, 1, rows, units), lambda i, w, k: (k, w, 0, 0)),
        ],
        out_specs=[result, result, result],
        out_shape=[out, out, out],
        scratch_shapes=[pltpu.VMEM((2, ROWS, units), jnp.float32)],
        compiler_params=kernel_params(),
        cost_estimate=light(4 * tokens * model * units),
        name="ffn_inner",
    )(normed, grad_hidden, weights)


def back_kernel(count, *refs):
    lefts = refs[:count]
    weight_ref = refs[count]
    out_ref = refs[count + 1]
    units = weight_ref.shape[3]
    total = None
    for number in range(count):
        term = dot_nt(lefts[number][...], weight_ref[:, number].reshape(-1, units))
        total = term if total is None else total + term
    out_ref[...] = total.astype(jnp.bfloat16)


def ffn_back(lefts, weights, first):
    tokens, units = lefts[0].shape
    blocks, unused, rows, unused_units = weights.shape
    count = len(lefts)
    model = blocks * rows
    return pl.pallas_call(
        functools.partial(back_kernel, count),
        grid=(2, tokens // ROWS),
        in_specs=[pl.BlockSpec((ROWS, units), lambda k, i: (i, 0)) for unused_left in lefts]
        + [pl.BlockSpec((blocks // 2, count, rows, units), lambda k, i: (k, first, 0, 0))],
        out_specs=pl.BlockSpec((ROWS, model // 2), lambda k, i: (i, k)),
        out_shape=jax.ShapeDtypeStruct((tokens, model), jnp.bfloat16),
        compiler_params=kernel_params(),
        cost_estimate=light(4 * count * tokens * model * units),
        name="ffn_back",
    )(*lefts, weights)


def outer_kernel(count, *refs):
    out_ref = refs[-1]
    total = dot_tn(refs[0][...], refs[count][...])
    for number in range(1, count):
        total = total + dot_tn(refs[number][...], refs[count + number][...])
    out_ref[...] = total.astype(jnp.bfloat16).reshape(out_ref.shape)


def ffn_outer(lefts, places, rights, blocks, slot, held):
    tokens, units = rights[0].shape
    model = lefts[0].shape[1]
    rows = model // blocks
    extra = [] if held is None else [held]
    count = len(lefts)
    left_spec = lambda place: pl.BlockSpec((tokens, model // 2), lambda k: (place, k))
    return pl.pallas_call(
        functools.partial(outer_kernel, count),
        grid=(2,),
        in_specs=[left_spec(place) for place in places]
        + [pl.BlockSpec((tokens, units), lambda k: (0, 0)) for unused in rights]
        + [pl.BlockSpec(memory_space=pl.ANY) for unused in extra],
        out_specs=pl.BlockSpec((blocks // 2, 1, rows, units), lambda k: (k, slot, 0, 0)),
        out_shape=jax.ShapeDtypeStruct((blocks, 3, rows, units), jnp.bfloat16),
        input_output_aliases={} if held is None else {2 * count: 0},
        compiler_params=kernel_params(),
        cost_estimate=light(4 * count * tokens * model * units),
        name="ffn_outer",
    )(*lefts, *rights, *extra)


def down_kernel(normed_ref, grad_ref, weight_ref, gain_ref, out_ref, part_ref):
    total = dot_tn(normed_ref[...], grad_ref[...])
    out_ref[...] = total.astype(jnp.bfloat16)
    summed = jnp.sum(total * weight_ref[...].astype(jnp.float32), axis=1, keepdims=True)
    part_ref[...] = summed / gain_ref[...]


def down_outer(normed, grads, weights, gains):
    tokens, model = normed.shape
    width = grads.shape[1]
    block = model // 4
    row_spec = lambda cols: pl.BlockSpec((block, cols), lambda k: (k, 0))
    return pl.pallas_call(
        down_kernel,
        grid=(4,),
        in_specs=[
            pl.BlockSpec((tokens, block), lambda k: (0, k)),
            pl.BlockSpec((tokens, width), lambda k: (0, 0)),
            row_spec(width),
            row_spec(1),
        ],
        out_specs=[row_spec(width), row_spec(1)],
        out_shape=[
            jax.ShapeDtypeStruct((model, width), jnp.bfloat16),
            jax.ShapeDtypeStruct((model, 1), jnp.float32),
        ],
        compiler_params=kernel_params(),
        cost_estimate=light(4 * tokens * model * width),
        name="down_outer",
    )(normed, grads, weights, gains)


def input_kernel(grad_ref, weight_ref, inputs_ref, cot_ref, mid_ref, gain_ref, out_ref):
    value = inputs_ref[...].astype(jnp.float32)
    scaled = dot_nt(grad_ref[...], weight_ref[...]) * gain_ref[...]
    rate = lax.rsqrt(jnp.mean(value * value, axis=1, keepdims=True) + NORM_EPS)
    dotted = jnp.mean(scaled * value, axis=1, keepdims=True)
    residual = cot_ref[...].astype(jnp.float32) + mid_ref[...].astype(jnp.float32)
    out_ref[...] = residual + rate * (scaled - value * (rate * rate * dotted))


def input_back(grads, weights, inputs, cotangent, mid_norm, gains):
    tokens, width = grads.shape
    model = inputs.shape[1]
    row_spec = lambda cols: pl.BlockSpec((BLK, cols), lambda i: (i, 0))
    return pl.pallas_call(
        input_kernel,
        grid=(tokens // BLK,),
        in_specs=[
            row_spec(width),
            pl.BlockSpec((model, width), lambda i: (0, 0)),
            row_spec(model),
            row_spec(model),
            row_spec(model),
            pl.BlockSpec((1, model), lambda i: (0, 0)),
        ],
        out_specs=row_spec(model),
        out_shape=jax.ShapeDtypeStruct((tokens, model), jnp.float32),
        compiler_params=kernel_params(),
        cost_estimate=light(4 * tokens * model * width),
        name="input_back",
    )(grads, weights, inputs, cotangent, mid_norm, gains)


def latent_kernel(count, *refs):
    out_ref = refs[-1]
    query_up, latent_up = refs[3 * count], refs[3 * count + 1]
    size = refs[0].shape[1]
    for number in range(count):
        grad_q, grad_kv, rope = refs[number], refs[count + number], refs[2 * count + number]
        rows = slice(number * size, (number + 1) * size)
        out_ref[rows, :QR] = dot_nt(grad_q[...].T, query_up[...]).astype(jnp.bfloat16)
        out_ref[rows, QR : QR + KVR] = dot_nt(grad_kv[...].T, latent_up[...]).astype(jnp.bfloat16)
        out_ref[rows, QR + KVR :] = rope[...].T.astype(jnp.bfloat16)


def latent_back(grads_q, grads_kv, ropes, query_up, latent_up):
    count = len(grads_q)
    tokens = count * grads_q[0].shape[1]
    return pl.pallas_call(
        functools.partial(latent_kernel, count),
        out_shape=jax.ShapeDtypeStruct((tokens, QR + KVR + RD), jnp.bfloat16),
        compiler_params=kernel_params(),
        cost_estimate=light(tokens * (QR + KVR) * 4000),
        name="latent_back",
    )(*grads_q, *grads_kv, *ropes, query_up, latent_up)


def heads_kernel(count, *refs):
    out_ref = refs[-1]
    q_normed, kv_normed = refs[4 * count], refs[4 * count + 1]
    blocks = out_ref.shape[0]
    size = refs[0].shape[0]
    outer = query_outer = latent_outer = None
    for number in range(count):
        grad_attn, mixed = refs[number], refs[count + number]
        grad_q, grad_kv = refs[2 * count + number], refs[3 * count + number]
        rows = slice(number * size, (number + 1) * size)
        terms = (
            dot_nt(grad_attn[...].T, mixed[...]),
            dot_nt(q_normed[rows].T, grad_q[...]),
            dot_nt(kv_normed[rows].T, grad_kv[...]),
        )
        outer = terms[0] if outer is None else outer + terms[0]
        query_outer = terms[1] if query_outer is None else query_outer + terms[1]
        latent_outer = terms[2] if latent_outer is None else latent_outer + terms[2]
    side = outer.shape[1]
    low = outer.astype(jnp.bfloat16).reshape(blocks, -1, side)
    spread = low.shape[1] // 2
    out_ref[:, :spread, :side] = low[:, :spread]
    out_ref[:, :spread, side:] = low[:, spread:]
    query_rows = query_outer.shape[0] // blocks
    columns = query_outer.shape[1]
    middle = slice(spread, spread + query_rows)
    out_ref[:, middle, :columns] = query_outer.astype(jnp.bfloat16).reshape(blocks, query_rows, columns)
    out_ref[:, middle, columns:] = jnp.zeros(
        (blocks, query_rows, out_ref.shape[2] - columns), jnp.bfloat16
    )
    out_ref[:, spread + query_rows :] = latent_outer.astype(jnp.bfloat16).reshape(
        blocks, -1, out_ref.shape[2]
    )


def heads_outer(grads_attn, mixed, grads_q, grads_kv, q_normed, kv_normed, blocks):
    count = len(mixed)
    size = grads_attn[0].shape[0]
    wide_cols = grads_kv[0].shape[0]
    rows = D // blocks // 2 + QR // blocks + KVR // blocks
    whole = lambda value: pl.BlockSpec(value.shape, lambda k: (0, 0))
    return pl.pallas_call(
        functools.partial(heads_kernel, count),
        grid=(2,),
        in_specs=[pl.BlockSpec((size, D // 2), lambda k: (0, k)) for unused in grads_attn]
        + [whole(value) for value in (*mixed, *grads_q, *grads_kv)]
        + [
            pl.BlockSpec((q_normed.shape[0], QR // 2), lambda k: (0, k)),
            pl.BlockSpec((kv_normed.shape[0], KVR // 2), lambda k: (0, k)),
        ],
        out_specs=pl.BlockSpec((blocks // 2, rows, wide_cols), lambda k: (k, 0, 0)),
        out_shape=jax.ShapeDtypeStruct((blocks, rows, wide_cols), jnp.bfloat16),
        compiler_params=kernel_params(),
        cost_estimate=light(count * size * D * wide_cols * 2),
        name="heads_outer",
    )(*grads_attn, *mixed, *grads_q, *grads_kv, q_normed, kv_normed)


def update_rates():
    return [
        (0.25, 0.0),
        (2.5 / math.sqrt(D), DECAY_RATE),
        (2.5 / math.sqrt(D), DECAY_RATE),
        (2.5 / math.sqrt(QR), DECAY_RATE),
        (2.5 / math.sqrt(KVR), DECAY_RATE),
        (1.75, DECAY_RATE),
        (2.5 / math.sqrt(D), DECAY_RATE),
        (2.5 / math.sqrt(D), DECAY_RATE),
        (0.375, DECAY_RATE),
    ]


def adam_step(weight, gradient, first, second, rate_pair):
    first_new = BETA_ONE * first + (1.0 - BETA_ONE) * gradient
    second_new = BETA_TWO * second + (1.0 - BETA_TWO) * gradient * gradient
    first_hat = first_new / (1.0 - BETA_ONE**STEP)
    second_hat = second_new / (1.0 - BETA_TWO**STEP)
    weight_new = weight - rate_pair[0] * (
        first_hat / (jnp.sqrt(second_hat) + ADAM_EPS) + rate_pair[1] * weight
    )
    return (first_new, second_new, weight_new)


def wide(value):
    return value.astype(jnp.float32)


def tie(*values):
    return lax.optimization_barrier(values)


def after(value, *others):
    return lax.optimization_barrier((value, *others))[0]


def chunk_of(stacked, place):
    return lax.dynamic_index_in_dim(stacked, place, axis=0, keepdims=False)


class Gather:
    def __init__(self, own, count, axis):
        self.own, self.count, self.axis = own, count, axis
        self.below, self.above = [own], [own]

    def advance(self, gate):
        step = len(self.below)
        if step == self.count:
            return []
        up, down = gate(self.below[-1], self.above[-1])
        ups = [(k, k + 1) for k in range(step - 1, self.count - 1)]
        downs = [(k + 1, k) for k in range(self.count - step)]
        self.below.append(lax.ppermute(up, "mp", ups))
        self.above.append(lax.ppermute(down, "mp", downs))
        return [self.below[-1], self.above[-1]]

    def result(self):
        while self.advance(tie):
            pass
        place = lax.axis_index("mp")
        blocks = []
        for slot in range(self.count):
            block = self.own
            for step in range(1, self.count):
                if slot + step < self.count:
                    block = jnp.where(place - step == slot, self.below[step], block)
                if slot - step >= 0:
                    block = jnp.where(place + step == slot, self.above[step], block)
            blocks.append(block)
        return jnp.concatenate(blocks, axis=self.axis)


class Scatter:
    def __init__(self, partial, count):
        self.stacked = partial.reshape(count, partial.shape[0] // count, partial.shape[1])
        self.count, self.step = count, 0
        self.below = self.above = None

    def advance(self, gate):
        count = self.count
        if self.step == count - 1:
            return []
        self.step = step = self.step + 1
        place = lax.axis_index("mp")
        up = chunk_of(self.stacked, jnp.clip(count - step + place, 0, count - 1))
        down = chunk_of(self.stacked, jnp.clip(step - count + place, 0, count - 1))
        if step > 1:
            up = (wide(up) + wide(self.below)).astype(up.dtype)
            down = (wide(down) + wide(self.above)).astype(down.dtype)
        up, down = gate(up, down)
        self.below = lax.ppermute(up, "mp", [(k, k + 1) for k in range(step)])
        downs = [(count - 1 - k, count - 2 - k) for k in range(step)]
        self.above = lax.ppermute(down, "mp", downs)
        return [self.below, self.above]

    def result(self):
        while self.advance(tie):
            pass
        own = chunk_of(self.stacked, lax.axis_index("mp"))
        return wide(own) + wide(self.below) + wide(self.above)


class Plane:
    def __init__(self, block, count):
        rows = block.shape[0] // 2
        bits = [1 << k for k in range(1, count.bit_length() - 1)]
        self.count, self.step = count, 0
        self.orders = [bits + [1], bits[::-1] + [1]]
        self.held = [block[None, :rows], block[None, rows:]]

    def advance(self, gate):
        if self.step == len(self.orders[0]):
            return []
        held = gate(*self.held)
        came = []
        for part, order in zip(held, self.orders):
            pairs = [(k, k ^ order[self.step]) for k in range(self.count)]
            came.append(lax.ppermute(part, "dp", pairs))
        self.held = [jnp.concatenate([part, other], axis=0) for part, other in zip(self.held, came)]
        self.step += 1
        return came

    def result(self):
        while self.advance(tie):
            pass
        place = lax.axis_index("dp")
        blocks = []
        for number in range(self.count):
            apart = jnp.bitwise_xor(place, number)
            for part, order in zip(self.held, self.orders):
                spot = sum(
                    jnp.where(jnp.bitwise_and(apart, bit) != 0, 1 << step, 0)
                    for step, bit in enumerate(order)
                )
                blocks.append(chunk_of(part, spot))
        return jnp.concatenate(blocks, axis=0)


class Clock:
    def __init__(self):
        self.past, self.present = (), []

    def gate(self, *values):
        return lax.optimization_barrier((*values, *self.past))[: len(values)]

    def wait(self, value):
        return self.gate(value)[0]

    def move(self, *flows):
        for flow in flows:
            self.present += flow.advance(self.gate)

    def tick(self, *values):
        if self.present or values:
            self.past = (*self.present, *values)
            self.present = []


def sum_rows(stacked):
    flat = stacked.reshape(-1, stacked.shape[-1])
    return wide(lax.psum_scatter(flat, "dp", scatter_dimension=0, tiled=True))


def turn(low, high, cosines, sines, direction):
    return (low * cosines - direction * high * sines, high * cosines + direction * low * sines)


def local(
    inputs,
    cotangent,
    norm_gains,
    norm_gains_first,
    norm_gains_second,
    query_down,
    query_down_first,
    query_down_second,
    latent_down,
    latent_down_first,
    latent_down_second,
    query_up,
    query_up_first,
    query_up_second,
    latent_up,
    latent_up_first,
    latent_up_second,
    out_proj,
    out_proj_first,
    out_proj_second,
    ffn_gate,
    ffn_gate_first,
    ffn_gate_second,
    ffn_up,
    ffn_up_first,
    ffn_up_second,
    ffn_down,
    ffn_down_first,
    ffn_down_second,
):
    low_type = jnp.bfloat16
    tokens_dev = inputs.shape[0]
    n_data = lax.axis_size("dp")
    n_model = lax.axis_size("mp")
    place = lax.axis_index("mp")
    heads_dev = query_up.shape[1] // (HD + RD)
    half_tokens = tokens_dev // 2
    own_tokens = half_tokens // n_model
    hidden_dev = ffn_gate.shape[1]
    out_width = heads_dev * HD
    down_rows = query_down.shape[0]
    width = QR + KVR + RD
    gain_rows = 16
    order = (1, 0)

    def own_rows(value):
        return lax.dynamic_slice_in_dim(value, place * own_tokens, own_tokens, 0)

    def half_of(value, half):
        return value[half * half_tokens : (half + 1) * half_tokens]

    up_rows = query_up.shape[0]
    kv_rows = latent_up.shape[0]
    up_width = latent_up.shape[1]
    gains_high = lax.reduce_precision(norm_gains, 8, 7)
    up_pack = jnp.concatenate(
        [
            jnp.pad(query_up.astype(low_type), ((0, 0), (0, up_width - query_up.shape[1]))),
            latent_up.astype(low_type),
            jnp.pad(
                jnp.stack([gains_high, norm_gains - gains_high]).astype(low_type),
                ((0, gain_rows - 2), (0, up_width - norm_gains.shape[0])),
            ),
        ],
        axis=0,
    )
    down_own = jnp.concatenate([query_down, latent_down], axis=1).astype(low_type)
    up_flow = Plane(up_pack, n_data)
    down_flow = Gather(down_own, n_model, 0)
    out_flow = Gather(out_proj.T.astype(low_type), n_model, 1)
    clock = Clock()
    for unused in range(3):
        clock.move(down_flow)
        clock.tick()
    down_flow = Plane(down_flow.result(), n_data)
    for unused in range(3):
        clock.move(down_flow, up_flow, out_flow)
        clock.tick()
    up_all = up_flow.result().reshape(n_data, -1, up_width)
    down_all = down_flow.result()
    out_all = lax.all_gather(out_flow.result(), "dp", axis=0, tiled=True)
    out_own = lax.dynamic_slice_in_dim(out_all, place * out_width, out_width, 1)
    ffn_pack = jnp.stack([ffn_gate, ffn_up, ffn_down.T]).astype(low_type)
    ffn_all = lax.all_gather(ffn_pack, "dp", axis=0, tiled=False)
    query_up_all = up_all[:, :up_rows, : query_up.shape[1]].reshape(QR, query_up.shape[1])
    latent_up_all = up_all[:, up_rows : up_rows + kv_rows].reshape(KVR, up_width)
    gains_sent = wide(up_all[:, up_rows + kv_rows : up_rows + kv_rows + 2, : norm_gains.shape[0]])
    gains_all = (gains_sent[:, 0] + gains_sent[:, 1]).reshape(-1)
    gain_in = gains_all[:D]
    gain_query = gains_all[D : D + QR]
    gain_latent = gains_all[D + QR : D + QR + KVR]
    gain_mid = gains_all[D + QR + KVR :]
    cosines, sines = tables(LEN)
    cos_tok = cosines
    sin_tok = sines
    cosines = cosines.T
    sines = sines.T

    inputs_wide = wide(inputs)
    cot_wide = wide(cotangent)
    normed_in = normalize(inputs_wide, gain_in).astype(low_type)
    latents = product(normed_in, down_all)
    q_latent = latents[:, :QR]
    kv_latent = latents[:, QR : QR + KVR]
    q_normed = normalize(q_latent, gain_query).astype(low_type)
    kv_normed = normalize(kv_latent, gain_latent).astype(low_type)
    q_heads = contract("rc,tr->ct", query_up_all, q_normed).reshape(heads_dev, HD + RD, tokens_dev)
    turned = turn(q_heads[:, HD : HD + RD // 2], q_heads[:, HD + RD // 2 :], cosines, sines, 1.0)
    queries = jnp.concatenate([q_heads[:, :HD], turned[0], turned[1]], axis=1).astype(low_type)
    kv_heads = contract("rc,tr->ct", latent_up_all, kv_normed).astype(low_type)
    kv_heads = kv_heads.reshape(heads_dev, 2 * HD, tokens_dev)
    rope_in = latents[:, QR + KVR :].T
    turned = turn(rope_in[: RD // 2], rope_in[RD // 2 :], cosines, sines, 1.0)
    key_rope = jnp.concatenate(turned, axis=0).astype(low_type)
    keys = jnp.concatenate(
        [kv_heads[:, :HD], jnp.broadcast_to(key_rope[None], (heads_dev, RD, tokens_dev))], axis=1
    )
    values = kv_heads[:, HD:]
    mixed = {}
    log_sums = {}
    resid_mid = {}
    normed_mid = {}
    grad_ffn = (RESID_SCALE * cot_wide).astype(low_type)
    mixed_flow = {}
    for half in order:
        asked = queries if half == 1 else clock.wait(queries)
        mixed[half], log_sums[half] = attend_forward(asked, keys, values, half)
        mixed[half] = mixed[half].reshape(out_width, half_tokens)
        mixed_flow[half] = Gather(mixed[half], n_model, 0)
        clock.tick(mixed[half])
        clock.move(mixed_flow[1])
    clock.move(mixed_flow[0])
    clock.tick()
    clock.move(mixed_flow[1], mixed_flow[0])
    grad_hidden = hidden_back(clock.wait(grad_ffn), ffn_all)
    clock.tick(grad_hidden)
    clock.move(mixed_flow[0])

    def middle(half):
        mixed_all = clock.wait(mixed_flow[half].result())
        attn_out = contract("ht,dh->td", mixed_all, out_all)
        resid_mid[half] = half_of(inputs_wide, half) + RESID_SCALE * attn_out
        normed_mid[half] = normalize(resid_mid[half], gain_mid).astype(low_type)
        clock.tick(normed_mid[half])

    hidden = {}
    grad_gate = {}
    grad_up = {}
    part_mid = {}
    mid_own = {}
    for half in order:
        middle(half)
        hidden[half], grad_gate[half], grad_up[half] = ffn_inner(
            clock.wait(normed_mid[half]), grad_hidden, ffn_all, half
        )
        clock.tick(grad_up[half])
        part_mid[half] = ffn_back([clock.wait(grad_gate[half]), grad_up[half]], ffn_all, 0)
        clock.tick(part_mid[half])
        sent_mid = part_mid[half] if half == 1 else after(part_mid[half], mid_own[1])
        mid_own[half] = wide(lax.psum_scatter(sent_mid, "mp", scatter_dimension=0, tiled=True))
    pairs = lambda values: [values[half] for half in order]
    both = lambda values: [values[half] for half in (0, 1)]
    mid_norm = {}
    mid_flow = {}
    gain_mid_part = {}
    grad_attn = {}
    grad_mixed = {}

    def mid_back(half):
        own, gain_mid_part[half] = norm_back(own_rows(resid_mid[half]), gain_mid, mid_own[half])
        mid_flow[half] = Gather(own.astype(low_type), n_model, 0)

    def mixed_back(half):
        mid_norm[half] = clock.wait(mid_flow[half].result())
        grad_mid = half_of(cot_wide, half) + wide(mid_norm[half])
        grad_attn[half] = (RESID_SCALE * grad_mid).astype(low_type)
        grad_mixed[half] = contract("td,dh->ht", grad_attn[half], out_own).astype(low_type)

    mid_back(1)
    clock.move(mid_flow[1])
    grad_gate[1] = clock.wait(grad_gate[1])
    ffn_grads = ffn_outer(pairs(normed_mid), (0, 0), pairs(grad_gate), n_data, 0, None)
    clock.tick(ffn_grads[0, 0, :16, :128])
    clock.move(mid_flow[1])
    grad_up[1] = clock.wait(grad_up[1])
    ffn_grads = ffn_outer(pairs(normed_mid), (0, 0), pairs(grad_up), n_data, 1, ffn_grads)
    clock.tick(ffn_grads[0, 1, :16, :128])
    clock.move(mid_flow[1])
    hidden_late = clock.wait(hidden[1])
    ffn_grads = ffn_outer([grad_ffn, grad_ffn], order, [hidden_late, hidden[0]], n_data, 2, ffn_grads)
    clock.tick(ffn_grads[0, 2, :16, :128])
    mid_own[0] = clock.wait(mid_own[0])
    ffn_grads = after(ffn_grads, mid_own[0])
    ffn_sum = sum_rows(ffn_grads).reshape(3, -1, hidden_dev)
    mid_back(0)
    clock.move(mid_flow[0])
    ffn_term = [ffn_back([clock.wait(hidden[half])], ffn_all, 2) for half in (0, 1)]
    ffn_term = jnp.concatenate(ffn_term, axis=0)
    clock.tick(ffn_term)
    resid_all = jnp.concatenate([resid_mid[0], resid_mid[1]], axis=0)

    seeds = ()
    grad_q_heads = {}
    grad_kv_heads = {}
    grad_rope = {}

    def heads_back(half):
        back = attend_backward(
            queries,
            keys,
            values,
            grad_mixed[half].reshape(heads_dev, HD, half_tokens),
            log_sums[half],
            cosines,
            sines,
            half,
            seeds,
        )
        grad_q_heads[half] = back[0].reshape(heads_dev * (HD + RD), half_tokens)
        grad_kv_heads[half] = back[1].reshape(heads_dev * 2 * HD, half_tokens)
        grad_rope[half] = back[2]
        return back[3:]

    out_flow = Scatter(ffn_term, n_model)
    clock.move(mid_flow[0], out_flow)
    mixed_back(1)
    seeds = heads_back(1)
    clock.tick(grad_rope[1])
    clock.move(mid_flow[0])
    clock.tick()
    clock.move(out_flow)
    mixed_back(0)
    seeds = heads_back(0)
    part_latents = latent_back(
        both(grad_q_heads), both(grad_kv_heads), both(grad_rope), query_up_all, latent_up_all
    )
    clock.tick(part_latents)
    lat_flow = Scatter(part_latents, n_model)
    clock.move(lat_flow, out_flow)
    head_grads = heads_outer(
        both(grad_attn),
        both(mixed),
        both(grad_q_heads),
        both(grad_kv_heads),
        clock.wait(q_normed),
        kv_normed,
        n_data,
    )
    clock.tick(head_grads[0, :16, :128])
    clock.move(lat_flow)
    clock.tick()
    clock.move(lat_flow)
    rows = lat_flow.result()
    ffn_own = out_flow.result()
    clock.tick()

    spread = 2 * own_tokens

    def wide_rows(value):
        return lax.dynamic_slice_in_dim(value, place * spread, spread, 0)

    grad_q_own, gain_query_part = norm_back(wide_rows(q_latent), gain_query, rows[:, :QR])
    grad_kv_own, gain_latent_part = norm_back(
        wide_rows(kv_latent), gain_latent, rows[:, QR : QR + KVR]
    )
    turned = turn(
        rows[:, QR + KVR : QR + KVR + RD // 2],
        rows[:, QR + KVR + RD // 2 :],
        wide_rows(cos_tok),
        wide_rows(sin_tok),
        -1.0,
    )
    gain_parts = jnp.concatenate(
        [gain_query_part, gain_latent_part, gain_mid_part[0] + gain_mid_part[1]]
    )
    gain_parts = jnp.pad(gain_parts, (0, gain_rows * width - gain_parts.shape[0]))
    sent_own = jnp.concatenate(
        [
            jnp.concatenate([grad_q_own, grad_kv_own, turned[0], turned[1]], axis=1),
            gain_parts.reshape(gain_rows, width),
        ],
        axis=0,
    ).astype(low_type)
    sent_flow = Gather(sent_own, n_model, 0)
    clock.move(sent_flow)
    clock.tick()
    clock.move(sent_flow)
    clock.tick()
    output_own = (wide_rows(resid_all) + RESID_SCALE * ffn_own).astype(low_type)
    output_flow = Gather(output_own, n_model, 0)
    clock.move(sent_flow, output_flow)
    sent = sent_flow.result().reshape(n_model, spread + gain_rows, width)
    head_grads, ffn_sum = tie(head_grads, ffn_sum)
    head_sum = sum_rows(head_grads)
    out_rows = D // n_data // 2
    clock.tick()
    clock.move(output_flow)
    grad_latents = sent[:, :spread].reshape(tokens_dev, width)
    gain_rest = jnp.sum(wide(sent[:, spread:]), axis=0).reshape(-1)[: QR + KVR + D]

    grad_down, gain_in_part = down_outer(clock.wait(normed_in), grad_latents, down_all, gain_in[:, None])
    gain_grad = jnp.concatenate([gain_in_part[:, 0], gain_rest]).reshape(n_data, 1, -1)
    gain_count = gain_grad.shape[2]
    gain_grad = jnp.pad(gain_grad, ((0, 0), (0, gain_rows - 1), (0, width - gain_count)))
    down_mine = lax.dynamic_index_in_dim(
        grad_down.reshape(n_data, n_model, down_rows, width), place, axis=1, keepdims=False
    )
    down_sent = jnp.concatenate([down_mine, gain_grad.astype(low_type)], axis=1)
    down_sent, head_sum = tie(down_sent, head_sum)
    down_sum = sum_rows(down_sent)
    clock.tick(grad_down)
    clock.move(output_flow)
    output = output_flow.result()
    input_grad = input_back(
        clock.wait(grad_latents),
        down_all,
        inputs,
        cotangent,
        jnp.concatenate([mid_norm[0], mid_norm[1]], axis=0),
        gain_in[None],
    )
    reduced = (
        down_sum[down_rows, :gain_count],
        down_sum[:down_rows, :QR],
        down_sum[:down_rows, QR:],
        head_sum[out_rows : out_rows + up_rows, : query_up.shape[1]],
        head_sum[out_rows + up_rows :],
        jnp.concatenate([head_sum[:out_rows, :out_width], head_sum[:out_rows, out_width:]], axis=0).T,
        ffn_sum[0],
        ffn_sum[1],
        ffn_sum[2].T,
    )
    weights = (
        norm_gains,
        query_down,
        latent_down,
        query_up,
        latent_up,
        out_proj,
        ffn_gate,
        ffn_up,
        ffn_down,
    )
    firsts = (
        norm_gains_first,
        query_down_first,
        latent_down_first,
        query_up_first,
        latent_up_first,
        out_proj_first,
        ffn_gate_first,
        ffn_up_first,
        ffn_down_first,
    )
    seconds = (
        norm_gains_second,
        query_down_second,
        latent_down_second,
        query_up_second,
        latent_up_second,
        out_proj_second,
        ffn_gate_second,
        ffn_up_second,
        ffn_down_second,
    )
    rates = update_rates()
    updated = [
        adam_step(weights[number], reduced[number], firsts[number], seconds[number], rates[number])
        for number in range(9)
    ]
    return (
        output,
        input_grad,
        updated[0][0],
        updated[0][1],
        updated[0][2],
        updated[1][0],
        updated[1][1],
        updated[1][2],
        updated[2][0],
        updated[2][1],
        updated[2][2],
        updated[3][0],
        updated[3][1],
        updated[3][2],
        updated[4][0],
        updated[4][1],
        updated[4][2],
        updated[5][0],
        updated[5][1],
        updated[5][2],
        updated[6][0],
        updated[6][1],
        updated[6][2],
        updated[7][0],
        updated[7][1],
        updated[7][2],
        updated[8][0],
        updated[8][1],
        updated[8][2],
    )


def solution(mesh):
    placed = (
        P("dp", None),
        P("dp", None),
        P("dp"),
        P("dp"),
        P("dp"),
        P(("dp", "mp"), None),
        P(("dp", "mp"), None),
        P(("dp", "mp"), None),
        P(("dp", "mp"), None),
        P(("dp", "mp"), None),
        P(("dp", "mp"), None),
        P("dp", "mp"),
        P("dp", "mp"),
        P("dp", "mp"),
        P("dp", "mp"),
        P("dp", "mp"),
        P("dp", "mp"),
        P("mp", "dp"),
        P("mp", "dp"),
        P("mp", "dp"),
        P("dp", "mp"),
        P("dp", "mp"),
        P("dp", "mp"),
        P("dp", "mp"),
        P("dp", "mp"),
        P("dp", "mp"),
        P("mp", "dp"),
        P("mp", "dp"),
        P("mp", "dp"),
    )
    return jax.shard_map(
        local,
        mesh=mesh,
        in_specs=placed,
        out_specs=(
            P("dp", None),
            P("dp", None),
            P("dp"),
            P("dp"),
            P("dp"),
            P(("dp", "mp"), None),
            P(("dp", "mp"), None),
            P(("dp", "mp"), None),
            P(("dp", "mp"), None),
            P(("dp", "mp"), None),
            P(("dp", "mp"), None),
            P("dp", "mp"),
            P("dp", "mp"),
            P("dp", "mp"),
            P("dp", "mp"),
            P("dp", "mp"),
            P("dp", "mp"),
            P("mp", "dp"),
            P("mp", "dp"),
            P("mp", "dp"),
            P("dp", "mp"),
            P("dp", "mp"),
            P("dp", "mp"),
            P("dp", "mp"),
            P("dp", "mp"),
            P("dp", "mp"),
            P("mp", "dp"),
            P("mp", "dp"),
            P("mp", "dp"),
        ),
        check_vma=False,
    )
```

```python
import functools
import math

import jax
import jax.numpy as jnp
from jax import lax
from jax.experimental import pallas as pl
from jax.experimental.pallas import tpu as pltpu
from jax.sharding import PartitionSpec as P

D = 2560
QR = 768
KVR = 256
HD = 64
RD = 32
LEN = 1024
STEP = 5


NORM_EPS = 1e-05
RESID_SCALE = 1.4 / math.sqrt(62.0)
ROPE_BASE = 10000.0
BETA_ONE = 0.9
BETA_TWO = 0.95
ADAM_EPS = 1e-08
DECAY_RATE = 0.1


def normalize(vector, gain_vec):
    return (
        vector * lax.rsqrt(jnp.mean(vector * vector, axis=-1, keepdims=True) + NORM_EPS) * gain_vec
    )


def norm_back(vector, gain_vec, gradient):
    unused, pull_back = jax.vjp(normalize, vector, gain_vec)
    return pull_back(gradient)


def tables(length):
    positions = jnp.arange(length).astype(jnp.float32)
    frequency = jnp.exp(jnp.arange(RD // 2).astype(jnp.float32) * (-2.0 * math.log(ROPE_BASE) / RD))
    angles = positions[:, None] * frequency[None, :]
    return (jnp.cos(angles), jnp.sin(angles))


def product(left, right):
    return jnp.dot(left, right, preferred_element_type=jnp.float32)


def contract(spec, left, right):
    return jnp.einsum(spec, left, right, preferred_element_type=jnp.float32)


BLK = 256
ROWS = 512
LIGHT = 100000
VMEM_CAP = 56 * 1024 * 1024


def dot_nn(left, right):
    return lax.dot_general(left, right, (((1,), (0,)), ((), ())), preferred_element_type=jnp.float32)


def dot_nt(left, right):
    return lax.dot_general(left, right, (((1,), (1,)), ((), ())), preferred_element_type=jnp.float32)


def dot_tn(left, right):
    return lax.dot_general(left, right, (((0,), (0,)), ((), ())), preferred_element_type=jnp.float32)


def kernel_params():
    return pltpu.CompilerParams(vmem_limit_bytes=VMEM_CAP)


def light(flops):
    return pl.CostEstimate(flops=flops // LIGHT, bytes_accessed=1024, transcendentals=0)


def causal_tile():
    keys = lax.broadcasted_iota(jnp.int32, (BLK, BLK), 0)
    rows = lax.broadcasted_iota(jnp.int32, (BLK, BLK), 1)
    return keys <= rows


def forward_kernel(first, q_ref, k_ref, v_ref, mixed_ref, lse_ref, score_ref):
    scale_val = (HD + RD) ** (-0.5)
    key_rows = k_ref[0].T
    keep = causal_tile()
    for i in range(q_ref.shape[2] // BLK):
        cols = slice(i * BLK, (i + 1) * BLK)
        q_blk = q_ref[0, :, cols]
        last = first + i
        top = None
        for c in range(last + 1):
            part = slice(c * BLK, (c + 1) * BLK)
            scores = scale_val * dot_nn(key_rows[part], q_blk)
            if c == last:
                scores = jnp.where(keep, scores, -1e30)
            score_ref[part, :] = scores
            peak = jnp.max(scores, axis=0, keepdims=True)
            top = peak if top is None else jnp.maximum(top, peak)
        total = jnp.zeros((1, BLK), jnp.float32)
        mixed = jnp.zeros((HD, BLK), jnp.float32)
        for c in range(last + 1):
            part = slice(c * BLK, (c + 1) * BLK)
            weights = jnp.exp(score_ref[part, :] - top)
            total = total + jnp.sum(weights, axis=0, keepdims=True)
            mixed = mixed + dot_nn(v_ref[0, :, part], weights.astype(jnp.bfloat16))
        mixed_ref[0, :, cols] = (mixed / total).astype(jnp.bfloat16)
        lse_ref[0, :, cols] = top + jnp.log(total)


def attend_forward(queries, keys, values, half):
    heads, unused, length = queries.shape
    size = length // 2
    seen = size * (half + 1)
    spec = lambda rows, cols, place: pl.BlockSpec((1, rows, cols), lambda h: (h, 0, place))
    return pl.pallas_call(
        functools.partial(forward_kernel, half * size // BLK),
        grid=(heads,),
        in_specs=[spec(HD + RD, size, half), spec(HD + RD, seen, 0), spec(HD, seen, 0)],
        out_specs=[spec(HD, size, 0), spec(1, size, 0)],
        out_shape=[
            jax.ShapeDtypeStruct((heads, HD, size), jnp.bfloat16),
            jax.ShapeDtypeStruct((heads, 1, size), jnp.float32),
        ],
        scratch_shapes=[pltpu.VMEM((seen, BLK), jnp.float32)],
        compiler_params=kernel_params(),
        cost_estimate=light(heads * size * seen * 1400),
        name="attend_forward",
    )(queries, keys, values)


def backward_kernel(first, seeded, *refs):
    q_ref, k_ref, v_ref, grad_ref, lse_ref, cos_ref, sin_ref = refs[:7]
    refs = refs[7:]
    if seeded:
        dk_seed, dv_seed = refs[:2]
        dq_ref, dkv_ref, rope_ref = refs[2:5]
        refs = refs[5:]
    else:
        dq_ref, dkv_ref, rope_ref, dk_out, dv_out = refs[:5]
        refs = refs[5:]
    prob_ref, gp_ref, dk_ref, dv_ref = refs
    scale_val = (HD + RD) ** (-0.5)
    half = RD // 2
    key_rows = k_ref[0].T
    value_rows = v_ref[0].T
    keep = causal_tile()
    size = q_ref.shape[2]
    if seeded:
        dk_ref[...] = dk_seed[0]
        dv_ref[...] = dv_seed[0]
    final = size // BLK - 1
    for i in range(final, -1, -1):
        cols = slice(i * BLK, (i + 1) * BLK)
        q_blk = q_ref[0, :, cols]
        grad_blk = grad_ref[0, :, cols]
        lse_blk = lse_ref[0, :, cols]
        last = first + i
        delta = jnp.zeros((1, BLK), jnp.float32)
        for c in range(last + 1):
            part = slice(c * BLK, (c + 1) * BLK)
            scores = scale_val * dot_nn(key_rows[part], q_blk)
            if c == last:
                scores = jnp.where(keep, scores, -1e30)
            probs = jnp.exp(scores - lse_blk)
            grad_probs = dot_nn(value_rows[part], grad_blk)
            prob_ref[part, :] = probs
            gp_ref[part, :] = grad_probs
            delta = delta + jnp.sum(probs * grad_probs, axis=0, keepdims=True)
        dq = jnp.zeros((HD + RD, BLK), jnp.float32)
        for c in range(last + 1):
            part = slice(c * BLK, (c + 1) * BLK)
            probs = prob_ref[part, :]
            grad_scores = (probs * (gp_ref[part, :] - delta)).astype(jnp.bfloat16)
            dq = dq + dot_nn(k_ref[0, :, part], grad_scores)
            dk_part = dot_nt(q_blk, grad_scores)
            dv_part = dot_nt(grad_blk, probs.astype(jnp.bfloat16))
            if i == final and not seeded:
                dk_ref[:, part] = dk_part
                dv_ref[:, part] = dv_part
            else:
                dk_ref[:, part] += dk_part
                dv_ref[:, part] += dv_part
        dq = scale_val * dq
        low = dq[HD : HD + half]
        high = dq[HD + half :]
        cos_blk = cos_ref[:, cols]
        sin_blk = sin_ref[:, cols]
        dq_ref[0, :HD, cols] = dq[:HD].astype(jnp.bfloat16)
        dq_ref[0, HD : HD + half, cols] = (low * cos_blk + high * sin_blk).astype(jnp.bfloat16)
        dq_ref[0, HD + half :, cols] = (high * cos_blk - low * sin_blk).astype(jnp.bfloat16)
    own = slice(first * BLK, first * BLK + size)
    dkv_ref[0, :HD, :] = (scale_val * dk_ref[:HD, own]).astype(jnp.bfloat16)
    dkv_ref[0, HD:, :] = dv_ref[:, own].astype(jnp.bfloat16)
    if not seeded:
        dk_out[0] = dk_ref[:, : first * BLK]
        dv_out[0] = dv_ref[:, : first * BLK]

    @pl.when(pl.program_id(0) == 0)
    def _():
        rope_ref[...] = scale_val * dk_ref[HD:, own]

    @pl.when(pl.program_id(0) != 0)
    def _():
        rope_ref[...] += scale_val * dk_ref[HD:, own]


def attend_backward(queries, keys, values, grad_mixed, lse, cosines, sines, half, seeds):
    heads, unused, length = queries.shape
    size = length // 2
    seen = size * (half + 1)
    spec = lambda rows, cols, place: pl.BlockSpec((1, rows, cols), lambda h: (h, 0, place))
    flat = lambda rows, place: pl.BlockSpec((rows, size), lambda h: (0, place))
    in_specs = [
        spec(HD + RD, size, half),
        spec(HD + RD, seen, 0),
        spec(HD, seen, 0),
        spec(HD, size, 0),
        spec(1, size, 0),
        flat(RD // 2, half),
        flat(RD // 2, half),
    ]
    out_specs = [spec(HD + RD, size, 0), spec(2 * HD, size, 0), flat(RD, 0)]
    out_shape = [
        jax.ShapeDtypeStruct((heads, HD + RD, size), jnp.bfloat16),
        jax.ShapeDtypeStruct((heads, 2 * HD, size), jnp.bfloat16),
        jax.ShapeDtypeStruct((RD, size), jnp.float32),
    ]
    pair = [spec(HD + RD, size, 0), spec(HD, size, 0)]
    if half == 0:
        in_specs = in_specs + pair
    else:
        out_specs = out_specs + pair
        out_shape = out_shape + [
            jax.ShapeDtypeStruct((heads, HD + RD, size), jnp.float32),
            jax.ShapeDtypeStruct((heads, HD, size), jnp.float32),
        ]
    return pl.pallas_call(
        functools.partial(backward_kernel, half * size // BLK, half == 0),
        grid=(heads,),
        in_specs=in_specs,
        out_specs=out_specs,
        out_shape=out_shape,
        scratch_shapes=[
            pltpu.VMEM((seen, BLK), jnp.float32),
            pltpu.VMEM((seen, BLK), jnp.float32),
            pltpu.VMEM((HD + RD, seen), jnp.float32),
            pltpu.VMEM((HD, seen), jnp.float32),
        ],
        compiler_params=kernel_params(),
        cost_estimate=light(heads * size * seen * 3000),
        name="attend_backward",
    )(queries, keys, values, grad_mixed, lse, cosines, sines, *seeds)


def hidden_kernel(grad_ref, weight_ref, out_ref):
    weight = weight_ref[...].reshape(-1, weight_ref.shape[3])

    @pl.when(pl.program_id(1) == 0)
    def _():
        out_ref[...] = dot_nn(grad_ref[...], weight)

    @pl.when(pl.program_id(1) != 0)
    def _():
        out_ref[...] += dot_nn(grad_ref[...], weight)


def hidden_back(grad_out, weights):
    tokens, model = grad_out.shape
    blocks, unused, rows, units = weights.shape
    return pl.pallas_call(
        hidden_kernel,
        grid=(tokens // ROWS, 2),
        in_specs=[
            pl.BlockSpec((ROWS, model // 2), lambda i, k: (i, k)),
            pl.BlockSpec((blocks // 2, 1, rows, units), lambda i, k: (k, 2, 0, 0)),
        ],
        out_specs=pl.BlockSpec((ROWS, units), lambda i, k: (i, 0)),
        out_shape=jax.ShapeDtypeStruct((tokens, units), jnp.float32),
        compiler_params=kernel_params(),
        cost_estimate=light(2 * tokens * model * units),
        name="hidden_back",
    )(grad_out, weights)


def inner_kernel(normed_ref, grad_ref, weight_ref, hidden_ref, gate_ref, up_ref, sum_ref):
    which = pl.program_id(1)
    step = pl.program_id(2)
    weight = weight_ref[...].reshape(-1, weight_ref.shape[3])

    @pl.when(step == 0)
    def _():
        sum_ref[which] = dot_nn(normed_ref[...], weight)

    @pl.when(step != 0)
    def _():
        sum_ref[which] += dot_nn(normed_ref[...], weight)

    @pl.when((which == 1) & (step == pl.num_programs(2) - 1))
    def _():
        gate_val = sum_ref[0]
        up_val = sum_ref[1]
        grad_hidden = grad_ref[...]
        sigmoid_gate = jax.nn.sigmoid(gate_val)
        silu_gate = gate_val * sigmoid_gate
        hidden_ref[...] = (silu_gate * up_val).astype(jnp.bfloat16)
        gate_ref[...] = (
            grad_hidden * up_val * sigmoid_gate * (1.0 + gate_val * (1.0 - sigmoid_gate))
        ).astype(jnp.bfloat16)
        up_ref[...] = (grad_hidden * silu_gate).astype(jnp.bfloat16)


def ffn_inner(normed, grad_hidden, weights, place):
    tokens, model = normed.shape
    blocks, unused, rows, units = weights.shape
    steps = tokens // ROWS
    out = jax.ShapeDtypeStruct((tokens, units), jnp.bfloat16)
    result = pl.BlockSpec((ROWS, units), lambda i, w, k: (i, 0))
    return pl.pallas_call(
        inner_kernel,
        grid=(steps, 2, 2),
        in_specs=[
            pl.BlockSpec((ROWS, model // 2), lambda i, w, k: (i, k)),
            pl.BlockSpec((ROWS, units), lambda i, w, k: (i + place * steps, 0)),
            pl.BlockSpec((blocks // 2, 1, rows, units), lambda i, w, k: (k, w, 0, 0)),
        ],
        out_specs=[result, result, result],
        out_shape=[out, out, out],
        scratch_shapes=[pltpu.VMEM((2, ROWS, units), jnp.float32)],
        compiler_params=kernel_params(),
        cost_estimate=light(4 * tokens * model * units),
        name="ffn_inner",
    )(normed, grad_hidden, weights)


def back_kernel(count, *refs):
    lefts = refs[:count]
    weight_ref = refs[count]
    out_ref = refs[count + 1]
    units = weight_ref.shape[3]
    total = None
    for number in range(count):
        term = dot_nt(lefts[number][...], weight_ref[:, number].reshape(-1, units))
        total = term if total is None else total + term
    out_ref[...] = total.astype(jnp.bfloat16)


def ffn_back(lefts, weights, first):
    tokens, units = lefts[0].shape
    blocks, unused, rows, unused_units = weights.shape
    count = len(lefts)
    model = blocks * rows
    return pl.pallas_call(
        functools.partial(back_kernel, count),
        grid=(2, tokens // ROWS),
        in_specs=[pl.BlockSpec((ROWS, units), lambda k, i: (i, 0)) for unused_left in lefts]
        + [pl.BlockSpec((blocks // 2, count, rows, units), lambda k, i: (k, first, 0, 0))],
        out_specs=pl.BlockSpec((ROWS, model // 2), lambda k, i: (i, k)),
        out_shape=jax.ShapeDtypeStruct((tokens, model), jnp.bfloat16),
        compiler_params=kernel_params(),
        cost_estimate=light(4 * count * tokens * model * units),
        name="ffn_back",
    )(*lefts, weights)


def outer_kernel(count, *refs):
    out_ref, mark_ref = refs[-2:]
    total = dot_tn(refs[0][...], refs[count][...])
    for number in range(1, count):
        total = total + dot_tn(refs[number][...], refs[count + number][...])
    out_ref[...] = total.astype(jnp.bfloat16).reshape(out_ref.shape)
    mark_ref[...] = jnp.zeros(mark_ref.shape, jnp.float32)


def ffn_outer(lefts, places, rights, blocks, slot, held):
    tokens, units = rights[0].shape
    model = lefts[0].shape[1]
    rows = model // blocks
    count = len(lefts)
    left_spec = lambda place: pl.BlockSpec((tokens, model // 2), lambda k: (place, k))
    mark_spec = pl.BlockSpec((8, 128), lambda k: (0, 0))
    held_specs = [] if held is None else [pl.BlockSpec(memory_space=pl.ANY), mark_spec]
    return pl.pallas_call(
        functools.partial(outer_kernel, count),
        grid=(2,),
        in_specs=[left_spec(place) for place in places]
        + [pl.BlockSpec((tokens, units), lambda k: (0, 0)) for unused in rights]
        + held_specs,
        out_specs=[
            pl.BlockSpec((blocks // 2, 1, rows, units), lambda k: (k, slot, 0, 0)),
            mark_spec,
        ],
        out_shape=[
            jax.ShapeDtypeStruct((blocks, 3, rows, units), jnp.bfloat16),
            jax.ShapeDtypeStruct((8, 128), jnp.float32),
        ],
        input_output_aliases={} if held is None else {2 * count: 0},
        compiler_params=kernel_params(),
        cost_estimate=light(4 * count * tokens * model * units),
        name="ffn_outer",
    )(*lefts, *rights, *(held or ()))


def down_kernel(normed_ref, grad_ref, weight_ref, gain_ref, out_ref, part_ref):
    total = dot_tn(normed_ref[...], grad_ref[...])
    out_ref[...] = total.astype(jnp.bfloat16)
    summed = jnp.sum(total * weight_ref[...].astype(jnp.float32), axis=1, keepdims=True)
    part_ref[...] = summed / gain_ref[...]


def down_outer(normed, grads, weights, gains):
    tokens, model = normed.shape
    width = grads.shape[1]
    block = model // 4
    row_spec = lambda cols: pl.BlockSpec((block, cols), lambda k: (k, 0))
    return pl.pallas_call(
        down_kernel,
        grid=(4,),
        in_specs=[
            pl.BlockSpec((tokens, block), lambda k: (0, k)),
            pl.BlockSpec((tokens, width), lambda k: (0, 0)),
            row_spec(width),
            row_spec(1),
        ],
        out_specs=[row_spec(width), row_spec(1)],
        out_shape=[
            jax.ShapeDtypeStruct((model, width), jnp.bfloat16),
            jax.ShapeDtypeStruct((model, 1), jnp.float32),
        ],
        compiler_params=kernel_params(),
        cost_estimate=light(4 * tokens * model * width),
        name="down_outer",
    )(normed, grads, weights, gains)


def input_kernel(grad_ref, weight_ref, inputs_ref, cot_ref, mid_ref, gain_ref, out_ref):
    value = inputs_ref[...].astype(jnp.float32)
    scaled = dot_nt(grad_ref[...], weight_ref[...]) * gain_ref[...]
    rate = lax.rsqrt(jnp.mean(value * value, axis=1, keepdims=True) + NORM_EPS)
    dotted = jnp.mean(scaled * value, axis=1, keepdims=True)
    residual = cot_ref[...].astype(jnp.float32) + mid_ref[...].astype(jnp.float32)
    out_ref[...] = residual + rate * (scaled - value * (rate * rate * dotted))


def input_back(grads, weights, inputs, cotangent, mid_norm, gains):
    tokens, width = grads.shape
    model = inputs.shape[1]
    row_spec = lambda cols: pl.BlockSpec((BLK, cols), lambda i: (i, 0))
    return pl.pallas_call(
        input_kernel,
        grid=(tokens // BLK,),
        in_specs=[
            row_spec(width),
            pl.BlockSpec((model, width), lambda i: (0, 0)),
            row_spec(model),
            row_spec(model),
            row_spec(model),
            pl.BlockSpec((1, model), lambda i: (0, 0)),
        ],
        out_specs=row_spec(model),
        out_shape=jax.ShapeDtypeStruct((tokens, model), jnp.float32),
        compiler_params=kernel_params(),
        cost_estimate=light(4 * tokens * model * width),
        name="input_back",
    )(grads, weights, inputs, cotangent, mid_norm, gains)


def latent_kernel(count, *refs):
    out_ref = refs[-1]
    query_up, latent_up = refs[3 * count], refs[3 * count + 1]
    size = refs[0].shape[1]
    for number in range(count):
        grad_q, grad_kv, rope = refs[number], refs[count + number], refs[2 * count + number]
        rows = slice(number * size, (number + 1) * size)
        out_ref[rows, :QR] = dot_nt(grad_q[...].T, query_up[...]).astype(jnp.bfloat16)
        out_ref[rows, QR : QR + KVR] = dot_nt(grad_kv[...].T, latent_up[...]).astype(jnp.bfloat16)
        out_ref[rows, QR + KVR :] = rope[...].T.astype(jnp.bfloat16)
    mid_part = refs[3 * count + 2][...] + refs[3 * count + 3][...]
    lane = QR + KVR
    lines = []
    for start in range(0, D, lane):
        line = mid_part[:, start : start + lane]
        lines.append(jnp.pad(line, ((0, 0), (0, lane - line.shape[1]))))
    extra = out_ref.shape[0] - count * size
    lines.append(jnp.zeros((extra - len(lines), lane), jnp.float32))
    out_ref[count * size :, :lane] = jnp.concatenate(lines, axis=0).astype(jnp.bfloat16)
    out_ref[count * size :, lane:] = jnp.zeros((extra, RD), jnp.bfloat16)


def latent_back(grads_q, grads_kv, ropes, query_up, latent_up, mid_parts, extra):
    count = len(grads_q)
    tokens = count * grads_q[0].shape[1]
    return pl.pallas_call(
        functools.partial(latent_kernel, count),
        out_shape=jax.ShapeDtypeStruct((tokens + extra, QR + KVR + RD), jnp.bfloat16),
        compiler_params=kernel_params(),
        cost_estimate=light(tokens * (QR + KVR) * 4000),
        name="latent_back",
    )(*grads_q, *grads_kv, *ropes, query_up, latent_up, *mid_parts)


def heads_kernel(count, *refs):
    out_ref = refs[-1]
    q_normed, kv_normed = refs[4 * count], refs[4 * count + 1]
    blocks = out_ref.shape[0]
    size = refs[0].shape[0]
    outer = query_outer = latent_outer = None
    for number in range(count):
        grad_attn, mixed = refs[number], refs[count + number]
        grad_q, grad_kv = refs[2 * count + number], refs[3 * count + number]
        rows = slice(number * size, (number + 1) * size)
        terms = (
            dot_nt(grad_attn[...].T, mixed[...]),
            dot_nt(q_normed[rows].T, grad_q[...]),
            dot_nt(kv_normed[rows].T, grad_kv[...]),
        )
        outer = terms[0] if outer is None else outer + terms[0]
        query_outer = terms[1] if query_outer is None else query_outer + terms[1]
        latent_outer = terms[2] if latent_outer is None else latent_outer + terms[2]
    side = outer.shape[1]
    low = outer.astype(jnp.bfloat16).reshape(blocks, -1, side)
    spread = low.shape[1] // 2
    out_ref[:, :spread, :side] = low[:, :spread]
    out_ref[:, :spread, side:] = low[:, spread:]
    query_rows = query_outer.shape[0] // blocks
    columns = query_outer.shape[1]
    middle = slice(spread, spread + query_rows)
    out_ref[:, middle, :columns] = query_outer.astype(jnp.bfloat16).reshape(blocks, query_rows, columns)
    out_ref[:, middle, columns:] = jnp.zeros(
        (blocks, query_rows, out_ref.shape[2] - columns), jnp.bfloat16
    )
    out_ref[:, spread + query_rows :] = latent_outer.astype(jnp.bfloat16).reshape(
        blocks, -1, out_ref.shape[2]
    )


def heads_outer(grads_attn, mixed, grads_q, grads_kv, q_normed, kv_normed, blocks, mark):
    count = len(mixed)
    size = grads_attn[0].shape[0]
    wide_cols = grads_kv[0].shape[0]
    rows = D // blocks // 2 + QR // blocks + KVR // blocks
    whole = lambda value: pl.BlockSpec(value.shape, lambda k: (0, 0))
    return pl.pallas_call(
        functools.partial(heads_kernel, count),
        grid=(2,),
        in_specs=[pl.BlockSpec((size, D // 2), lambda k: (0, k)) for unused in grads_attn]
        + [whole(value) for value in (*mixed, *grads_q, *grads_kv)]
        + [
            pl.BlockSpec((q_normed.shape[0], QR // 2), lambda k: (0, k)),
            pl.BlockSpec((kv_normed.shape[0], KVR // 2), lambda k: (0, k)),
            pl.BlockSpec((8, 128), lambda k: (0, 0)),
        ],
        out_specs=pl.BlockSpec((blocks // 2, rows, wide_cols), lambda k: (k, 0, 0)),
        out_shape=jax.ShapeDtypeStruct((blocks, rows, wide_cols), jnp.bfloat16),
        compiler_params=kernel_params(),
        cost_estimate=light(count * size * D * wide_cols * 2),
        name="heads_outer",
    )(*grads_attn, *mixed, *grads_q, *grads_kv, q_normed, kv_normed, mark)


def scaled_rate(value):
    return lax.rsqrt(jnp.mean(value * value, axis=1, keepdims=True) + NORM_EPS)


def norm_pull(value, gain_vec, gradient):
    rate = scaled_rate(value)
    scaled = gradient * gain_vec
    dotted = jnp.mean(scaled * value, axis=1, keepdims=True)
    pulled = rate * (scaled - value * (rate * rate * dotted))
    return pulled, jnp.sum(gradient * value * rate, axis=0, keepdims=True)


def latents_kernel(
    inputs_ref, gain_in, down_ref, gain_query, gain_latent, cos_ref, sin_ref,
    normed_ref, latents_ref, q_ref, kv_ref, rope_ref,
):
    value = inputs_ref[...].astype(jnp.float32)
    normed = (value * scaled_rate(value) * gain_in[...]).astype(jnp.bfloat16)
    normed_ref[...] = normed
    latents = dot_nn(normed, down_ref[...])
    latents_ref[...] = latents
    q_latent = latents[:, :QR]
    kv_latent = latents[:, QR : QR + KVR]
    q_ref[...] = (q_latent * scaled_rate(q_latent) * gain_query[...]).astype(jnp.bfloat16)
    kv_ref[...] = (kv_latent * scaled_rate(kv_latent) * gain_latent[...]).astype(jnp.bfloat16)
    rope = latents[:, QR + KVR :].T
    low, high = rope[: RD // 2], rope[RD // 2 :]
    cos_blk, sin_blk = cos_ref[...], sin_ref[...]
    rope_ref[: RD // 2, :] = (low * cos_blk - high * sin_blk).astype(jnp.bfloat16)
    rope_ref[RD // 2 :, :] = (high * cos_blk + low * sin_blk).astype(jnp.bfloat16)


def latents_forward(inputs, gain_in, down_all, gain_query, gain_latent, cosines, sines):
    tokens, model = inputs.shape
    width = down_all.shape[1]
    row_spec = lambda cols: pl.BlockSpec((BLK, cols), lambda i: (i, 0))
    column_spec = lambda rows: pl.BlockSpec((rows, BLK), lambda i: (0, i))
    whole = lambda value: pl.BlockSpec(value.shape, lambda i: (0, 0))
    return pl.pallas_call(
        latents_kernel,
        grid=(tokens // BLK,),
        in_specs=[row_spec(model), whole(gain_in), whole(down_all), whole(gain_query), whole(gain_latent)]
        + [column_spec(RD // 2), column_spec(RD // 2)],
        out_specs=[row_spec(model), row_spec(width), row_spec(QR), row_spec(KVR), column_spec(RD)],
        out_shape=[
            jax.ShapeDtypeStruct((tokens, model), jnp.bfloat16),
            jax.ShapeDtypeStruct((tokens, width), jnp.float32),
            jax.ShapeDtypeStruct((tokens, QR), jnp.bfloat16),
            jax.ShapeDtypeStruct((tokens, KVR), jnp.bfloat16),
            jax.ShapeDtypeStruct((RD, tokens), jnp.bfloat16),
        ],
        compiler_params=kernel_params(),
        cost_estimate=light(tokens * model * width),
        name="latents_forward",
    )(inputs, gain_in, down_all, gain_query, gain_latent, cosines, sines)


def split_kernel(q_ref, kv_ref, rope_ref, query_up, latent_up, cos_ref, sin_ref, queries, keys, values):
    heads = queries.shape[0]
    half = RD // 2
    grown = dot_nt(query_up[...], q_ref[...]).reshape(heads, HD + RD, -1)
    low, high = grown[:, HD : HD + half], grown[:, HD + half :]
    cos_blk, sin_blk = cos_ref[...][None], sin_ref[...][None]
    queries[:, :HD] = grown[:, :HD].astype(jnp.bfloat16)
    queries[:, HD : HD + half] = (low * cos_blk - high * sin_blk).astype(jnp.bfloat16)
    queries[:, HD + half :] = (high * cos_blk + low * sin_blk).astype(jnp.bfloat16)
    grown = dot_nt(latent_up[...], kv_ref[...]).astype(jnp.bfloat16).reshape(heads, 2 * HD, -1)
    keys[:, :HD] = grown[:, :HD]
    keys[:, HD:] = jnp.broadcast_to(rope_ref[...][None], (heads, RD, rope_ref.shape[1]))
    values[...] = grown[:, HD:]


def heads_forward(q_normed, kv_normed, key_rope, query_up, latent_up, cosines, sines):
    tokens = q_normed.shape[0]
    heads = query_up.shape[0] // (HD + RD)
    row_spec = lambda cols: pl.BlockSpec((BLK, cols), lambda i: (i, 0))
    column_spec = lambda rows: pl.BlockSpec((rows, BLK), lambda i: (0, i))
    head_spec = lambda rows: pl.BlockSpec((heads, rows, BLK), lambda i: (0, 0, i))
    whole = lambda value: pl.BlockSpec(value.shape, lambda i: (0, 0))
    return pl.pallas_call(
        split_kernel,
        grid=(tokens // BLK,),
        in_specs=[
            row_spec(QR),
            row_spec(KVR),
            column_spec(RD),
            whole(query_up),
            whole(latent_up),
            column_spec(RD // 2),
            column_spec(RD // 2),
        ],
        out_specs=[head_spec(HD + RD), head_spec(HD + RD), head_spec(HD)],
        out_shape=[
            jax.ShapeDtypeStruct((heads, HD + RD, tokens), jnp.bfloat16),
            jax.ShapeDtypeStruct((heads, HD + RD, tokens), jnp.bfloat16),
            jax.ShapeDtypeStruct((heads, HD, tokens), jnp.bfloat16),
        ],
        compiler_params=kernel_params(),
        cost_estimate=light(tokens * QR),
        name="heads_forward",
    )(q_normed, kv_normed, key_rope, query_up, latent_up, cosines, sines)


def middle_kernel(place_ref, grad_ref, resid_ref, gain_ref, out_ref, part_ref):
    pulled, part = norm_pull(resid_ref[...], gain_ref[...], grad_ref[...].astype(jnp.float32))
    out_ref[...] = pulled.astype(jnp.bfloat16)
    part_ref[...] = part


def middle_back(place, grads, resid, gain_mid):
    rows, model = grads.shape
    fixed = lambda size: pl.BlockSpec((size, model), lambda i, place_ref: (0, 0))
    return pl.pallas_call(
        middle_kernel,
        grid_spec=pltpu.PrefetchScalarGridSpec(
            num_scalar_prefetch=1,
            grid=(1,),
            in_specs=[
                fixed(rows),
                pl.BlockSpec((rows, model), lambda i, place_ref: (place_ref[0], 0)),
                fixed(1),
            ],
            out_specs=[fixed(rows), fixed(1)],
        ),
        out_shape=[
            jax.ShapeDtypeStruct((rows, model), jnp.bfloat16),
            jax.ShapeDtypeStruct((1, model), jnp.float32),
        ],
        compiler_params=kernel_params(),
        cost_estimate=light(rows * model),
        name="middle_back",
    )(place, grads, resid, gain_mid)


def turned_kernel(
    total_ref, latents_ref, cos_ref, sin_ref, gain_query, gain_latent, out_ref, query_ref, latent_ref
):
    half = RD // 2
    total = total_ref[...].astype(jnp.float32)
    latents = latents_ref[...]
    q_pulled, q_part = norm_pull(latents[:, :QR], gain_query[...], total[:, :QR])
    kv_pulled, kv_part = norm_pull(
        latents[:, QR : QR + KVR], gain_latent[...], total[:, QR : QR + KVR]
    )
    low = total[:, QR + KVR : QR + KVR + half]
    high = total[:, QR + KVR + half :]
    cos_blk = cos_ref[...].T
    sin_blk = sin_ref[...].T
    out_ref[:, :QR] = q_pulled.astype(jnp.bfloat16)
    out_ref[:, QR : QR + KVR] = kv_pulled.astype(jnp.bfloat16)
    out_ref[:, QR + KVR : QR + KVR + half] = (low * cos_blk + high * sin_blk).astype(jnp.bfloat16)
    out_ref[:, QR + KVR + half :] = (high * cos_blk - low * sin_blk).astype(jnp.bfloat16)

    @pl.when(pl.program_id(0) == 0)
    def _():
        query_ref[...] = q_part
        latent_ref[...] = kv_part

    @pl.when(pl.program_id(0) != 0)
    def _():
        query_ref[...] += q_part
        latent_ref[...] += kv_part


def latents_turned(total, latents, cosines, sines, gain_query, gain_latent):
    tokens, width = latents.shape
    row_spec = lambda cols: pl.BlockSpec((BLK, cols), lambda i: (i, 0))
    column_spec = pl.BlockSpec((RD // 2, BLK), lambda i: (0, i))
    whole = lambda cols: pl.BlockSpec((1, cols), lambda i: (0, 0))
    return pl.pallas_call(
        turned_kernel,
        grid=(tokens // BLK,),
        in_specs=[
            row_spec(width),
            row_spec(width),
            column_spec,
            column_spec,
            whole(QR),
            whole(KVR),
        ],
        out_specs=[row_spec(width), whole(QR), whole(KVR)],
        out_shape=[
            jax.ShapeDtypeStruct((tokens, width), jnp.bfloat16),
            jax.ShapeDtypeStruct((1, QR), jnp.float32),
            jax.ShapeDtypeStruct((1, KVR), jnp.float32),
        ],
        compiler_params=kernel_params(),
        cost_estimate=light(tokens * width),
        name="latents_turned",
    )(total, latents, cosines, sines, gain_query, gain_latent)


def mixed_kernel(mid_ref, cot_ref, weight_ref, attn_ref, mixed_ref):
    grad_mid = cot_ref[...].astype(jnp.float32) + mid_ref[...].astype(jnp.float32)
    grad_attn = (RESID_SCALE * grad_mid).astype(jnp.bfloat16)
    attn_ref[...] = grad_attn
    mixed_ref[...] = dot_nt(weight_ref[...], grad_attn).astype(jnp.bfloat16)


def mixed_gradient(mid_norm, cotangent, out_own, half):
    tokens, model = mid_norm.shape
    heads_width = out_own.shape[0]
    steps = tokens // BLK
    row_spec = pl.BlockSpec((BLK, model), lambda i: (i, 0))
    return pl.pallas_call(
        mixed_kernel,
        grid=(steps,),
        in_specs=[
            row_spec,
            pl.BlockSpec((BLK, model), lambda i: (i + half * steps, 0)),
            pl.BlockSpec(out_own.shape, lambda i: (0, 0)),
        ],
        out_specs=[row_spec, pl.BlockSpec((heads_width, BLK), lambda i: (0, i))],
        out_shape=[
            jax.ShapeDtypeStruct((tokens, model), jnp.bfloat16),
            jax.ShapeDtypeStruct((heads_width, tokens), jnp.bfloat16),
        ],
        compiler_params=kernel_params(),
        cost_estimate=light(tokens * model),
        name="mixed_gradient",
    )(mid_norm, cotangent, out_own)


def update_rates():
    return [
        (0.25, 0.0),
        (2.5 / math.sqrt(D), DECAY_RATE),
        (2.5 / math.sqrt(D), DECAY_RATE),
        (2.5 / math.sqrt(QR), DECAY_RATE),
        (2.5 / math.sqrt(KVR), DECAY_RATE),
        (1.75, DECAY_RATE),
        (2.5 / math.sqrt(D), DECAY_RATE),
        (2.5 / math.sqrt(D), DECAY_RATE),
        (0.375, DECAY_RATE),
    ]


def adam_step(weight, gradient, first, second, rate_pair):
    first_new = BETA_ONE * first + (1.0 - BETA_ONE) * gradient
    second_new = BETA_TWO * second + (1.0 - BETA_TWO) * gradient * gradient
    first_hat = first_new / (1.0 - BETA_ONE**STEP)
    second_hat = second_new / (1.0 - BETA_TWO**STEP)
    weight_new = weight - rate_pair[0] * (
        first_hat / (jnp.sqrt(second_hat) + ADAM_EPS) + rate_pair[1] * weight
    )
    return (first_new, second_new, weight_new)


def wide(value):
    return value.astype(jnp.float32)


def tie(*values):
    return lax.optimization_barrier(values)


def after(value, *others):
    return lax.optimization_barrier((value, *others))[0]


def chunk_of(stacked, place):
    return lax.dynamic_index_in_dim(stacked, place, axis=0, keepdims=False)


class Gather:
    def __init__(self, own, count, axis):
        self.own, self.count, self.axis = own, count, axis
        self.below, self.above = [own], [own]

    def advance(self, gate):
        step = len(self.below)
        if step == self.count:
            return []
        up, down = gate(self.below[-1], self.above[-1])
        ups = [(k, k + 1) for k in range(step - 1, self.count - 1)]
        downs = [(k + 1, k) for k in range(self.count - step)]
        self.below.append(lax.ppermute(up, "mp", ups))
        self.above.append(lax.ppermute(down, "mp", downs))
        return [self.below[-1], self.above[-1]]

    def result(self):
        while self.advance(tie):
            pass
        place = lax.axis_index("mp")
        blocks = []
        for slot in range(self.count):
            block = self.own
            for step in range(1, self.count):
                if slot + step < self.count:
                    block = jnp.where(place - step == slot, self.below[step], block)
                if slot - step >= 0:
                    block = jnp.where(place + step == slot, self.above[step], block)
            blocks.append(block)
        return jnp.concatenate(blocks, axis=self.axis)


class Direct:
    def __init__(self, own, count):
        self.own, self.count, self.came = own, count, None

    def advance(self, gate):
        if self.came is not None:
            return []
        (sent,) = gate(self.own)
        count = self.count
        self.came = [
            lax.ppermute(sent, "mp", [(k, (k + step) % count) for k in range(count)])
            for step in range(1, count)
        ]
        return self.came

    def result(self):
        self.advance(tie)
        place = lax.axis_index("mp")
        blocks = []
        for slot in range(self.count):
            block = self.own
            for step in range(1, self.count):
                block = jnp.where((place - step) % self.count == slot, self.came[step - 1], block)
            blocks.append(block)
        return jnp.concatenate(blocks, axis=0)


class Scatter:
    def __init__(self, partial, count):
        self.stacked = partial.reshape(count, partial.shape[0] // count, partial.shape[1])
        self.count, self.step = count, 0
        self.below = self.above = None

    def advance(self, gate):
        count = self.count
        if self.step == count - 1:
            return []
        self.step = step = self.step + 1
        place = lax.axis_index("mp")
        up = chunk_of(self.stacked, jnp.clip(count - step + place, 0, count - 1))
        down = chunk_of(self.stacked, jnp.clip(step - count + place, 0, count - 1))
        if step > 1:
            up = (wide(up) + wide(self.below)).astype(up.dtype)
            down = (wide(down) + wide(self.above)).astype(down.dtype)
        up, down = gate(up, down)
        self.below = lax.ppermute(up, "mp", [(k, k + 1) for k in range(step)])
        downs = [(count - 1 - k, count - 2 - k) for k in range(step)]
        self.above = lax.ppermute(down, "mp", downs)
        return [self.below, self.above]

    def arrived(self):
        while self.advance(tie):
            pass
        return self.below, self.above

    def result(self):
        self.arrived()
        own = chunk_of(self.stacked, lax.axis_index("mp"))
        return wide(own) + wide(self.below) + wide(self.above)


class Plane:
    def __init__(self, block, count):
        rows = block.shape[0] // 2
        bits = [1 << k for k in range(1, count.bit_length() - 1)]
        self.count, self.step = count, 0
        self.orders = [bits + [1], bits[::-1] + [1]]
        self.held = [block[None, :rows], block[None, rows:]]

    def advance(self, gate):
        if self.step == len(self.orders[0]):
            return []
        held = gate(*self.held)
        came = []
        for part, order in zip(held, self.orders):
            pairs = [(k, k ^ order[self.step]) for k in range(self.count)]
            came.append(lax.ppermute(part, "dp", pairs))
        self.held = [jnp.concatenate([part, other], axis=0) for part, other in zip(self.held, came)]
        self.step += 1
        return came

    def result(self):
        while self.advance(tie):
            pass
        place = lax.axis_index("dp")
        blocks = []
        for number in range(self.count):
            apart = jnp.bitwise_xor(place, number)
            for part, order in zip(self.held, self.orders):
                spot = sum(
                    jnp.where(jnp.bitwise_and(apart, bit) != 0, 1 << step, 0)
                    for step, bit in enumerate(order)
                )
                blocks.append(chunk_of(part, spot))
        return jnp.concatenate(blocks, axis=0)


class PlaneScatter:
    def __init__(self, stacked, count):
        self.bits = count.bit_length() - 1
        self.left = stacked.reshape((2,) * self.bits + stacked.shape[1:])
        self.step = 0

    def advance(self, gate):
        if self.step == self.bits:
            return []
        bit = 1 << self.step
        axis = self.bits - 1 - self.step
        mine = jnp.where(jnp.bitwise_and(lax.axis_index("dp"), bit) != 0, 1, 0)
        kept = lax.dynamic_index_in_dim(self.left, mine, axis, keepdims=False)
        (gone,) = gate(lax.dynamic_index_in_dim(self.left, 1 - mine, axis, keepdims=False))
        pairs = [(k, k ^ bit) for k in range(1 << self.bits)]
        came = lax.ppermute(gone, "dp", pairs)
        self.left = (wide(kept) + wide(came)).astype(kept.dtype)
        self.step += 1
        return [came]

    def result(self):
        while self.advance(tie):
            pass
        return self.left


class Clock:
    def __init__(self):
        self.past, self.present = (), []

    def gate(self, *values):
        return lax.optimization_barrier((*values, *self.past))[: len(values)]

    def wait(self, value):
        return self.gate(value)[0]

    def move(self, *flows):
        for flow in flows:
            self.present += flow.advance(self.gate)

    def tick(self, *values):
        if self.present or values:
            self.past = (*self.present, *values)
            self.present = []


def local(
    inputs,
    cotangent,
    norm_gains,
    norm_gains_first,
    norm_gains_second,
    query_down,
    query_down_first,
    query_down_second,
    latent_down,
    latent_down_first,
    latent_down_second,
    query_up,
    query_up_first,
    query_up_second,
    latent_up,
    latent_up_first,
    latent_up_second,
    out_proj,
    out_proj_first,
    out_proj_second,
    ffn_gate,
    ffn_gate_first,
    ffn_gate_second,
    ffn_up,
    ffn_up_first,
    ffn_up_second,
    ffn_down,
    ffn_down_first,
    ffn_down_second,
):
    low_type = jnp.bfloat16
    tokens_dev = inputs.shape[0]
    n_data = lax.axis_size("dp")
    n_model = lax.axis_size("mp")
    place = lax.axis_index("mp")
    heads_dev = query_up.shape[1] // (HD + RD)
    half_tokens = tokens_dev // 2
    own_tokens = half_tokens // n_model
    spread = tokens_dev // n_model
    hidden_dev = ffn_gate.shape[1]
    out_width = heads_dev * HD
    down_rows = query_down.shape[0]
    width = QR + KVR + RD
    gain_rows = 16
    order = (1, 0)

    def own_rows(value):
        return lax.dynamic_slice_in_dim(value, place * own_tokens, own_tokens, 0)

    def half_of(value, half):
        return value[half * half_tokens : (half + 1) * half_tokens]

    up_rows = query_up.shape[0]
    kv_rows = latent_up.shape[0]
    up_width = latent_up.shape[1]
    gains_high = lax.reduce_precision(norm_gains, 8, 7)
    up_pack = jnp.concatenate(
        [
            jnp.pad(query_up.astype(low_type), ((0, 0), (0, up_width - query_up.shape[1]))),
            latent_up.astype(low_type),
            jnp.pad(
                jnp.stack([gains_high, norm_gains - gains_high]).astype(low_type),
                ((0, gain_rows - 2), (0, up_width - norm_gains.shape[0])),
            ),
        ],
        axis=0,
    )
    down_own = jnp.concatenate([query_down, latent_down], axis=1).astype(low_type)
    up_flow = Plane(up_pack, n_data)
    down_flow = Direct(down_own, n_model)
    out_flow = Gather(out_proj.T.astype(low_type), n_model, 1)
    clock = Clock()
    clock.move(down_flow)
    clock.tick()
    down_flow = Plane(down_flow.result(), n_data)
    for unused in range(3):
        clock.move(down_flow, up_flow, out_flow)
        clock.tick()
    up_all = up_flow.result().reshape(n_data, -1, up_width)
    down_all = down_flow.result()
    out_all = lax.all_gather(out_flow.result(), "dp", axis=0, tiled=True)
    out_own = lax.dynamic_slice_in_dim(out_all, place * out_width, out_width, 1).T
    ffn_pack = jnp.stack([ffn_gate, ffn_up, ffn_down.T]).astype(low_type)
    ffn_all = lax.all_gather(ffn_pack, "dp", axis=0, tiled=False)
    query_up_all = up_all[:, :up_rows, : query_up.shape[1]].reshape(QR, query_up.shape[1])
    latent_up_all = up_all[:, up_rows : up_rows + kv_rows].reshape(KVR, up_width)
    gains_sent = wide(up_all[:, up_rows + kv_rows : up_rows + kv_rows + 2, : norm_gains.shape[0]])
    gains_all = (gains_sent[:, 0] + gains_sent[:, 1]).reshape(-1)
    gain_in = gains_all[:D]
    gain_query = gains_all[D : D + QR]
    gain_latent = gains_all[D + QR : D + QR + KVR]
    gain_mid = gains_all[D + QR + KVR :]
    cosines, sines = tables(LEN)
    cosines = cosines.T
    sines = sines.T

    normed_in, latents, q_normed, kv_normed, key_rope = latents_forward(
        inputs, gain_in[None], down_all, gain_query[None], gain_latent[None], cosines, sines
    )
    queries, keys, values = heads_forward(
        q_normed, kv_normed, key_rope, query_up_all.T, latent_up_all.T, cosines, sines
    )
    mixed = {}
    log_sums = {}
    resid_mid = {}
    normed_mid = {}
    grad_ffn = (RESID_SCALE * wide(cotangent)).astype(low_type)
    mixed_flow = {}
    for half in order:
        asked = queries if half == 1 else clock.wait(queries)
        mixed[half], log_sums[half] = attend_forward(asked, keys, values, half)
        mixed[half] = mixed[half].reshape(out_width, half_tokens)
        mixed_flow[half] = Gather(mixed[half], n_model, 0)
        clock.tick(mixed[half])
        clock.move(mixed_flow[1])
    grad_hidden = hidden_back(clock.wait(grad_ffn), ffn_all)
    clock.tick(grad_hidden)
    clock.move(mixed_flow[1])
    clock.tick()
    clock.move(mixed_flow[0])

    def middle(half):
        mixed_all = clock.wait(mixed_flow[half].result())
        attn_out = contract("ht,dh->td", mixed_all, out_all)
        resid_mid[half] = wide(half_of(inputs, half)) + RESID_SCALE * attn_out
        normed_mid[half] = normalize(resid_mid[half], gain_mid).astype(low_type)
        clock.tick(normed_mid[half])

    hidden = {}
    grad_gate = {}
    grad_up = {}
    part_mid = {}
    mid_own = {}
    for half in order:
        middle(half)
        clock.move(mixed_flow[0])
        hidden[half], grad_gate[half], grad_up[half] = ffn_inner(
            clock.wait(normed_mid[half]), grad_hidden, ffn_all, half
        )
        clock.tick(grad_up[half])
        clock.move(mixed_flow[0])
        part_mid[half] = ffn_back([clock.wait(grad_gate[half]), grad_up[half]], ffn_all, 0)
        clock.tick(part_mid[half])
        sent_mid = part_mid[half] if half == 1 else after(part_mid[half], mid_own[1])
        mid_own[half] = lax.psum_scatter(sent_mid, "mp", scatter_dimension=0, tiled=True)
    pairs = lambda values: [values[half] for half in order]
    both = lambda values: [values[half] for half in (0, 1)]
    mid_norm = {}
    mid_flow = {}
    gain_mid_part = {}
    grad_attn = {}
    grad_mixed = {}

    def mid_back(half):
        own, gain_mid_part[half] = middle_back(
            place[None], mid_own[half], resid_mid[half], gain_mid[None]
        )
        mid_flow[half] = Gather(own, n_model, 0)

    def mixed_back(half):
        mid_norm[half] = mid_flow[half].result()
        grad_attn[half], grad_mixed[half] = mixed_gradient(
            clock.wait(mid_norm[half]), cotangent, out_own, half
        )

    mid_back(1)
    clock.move(mid_flow[1])
    grad_gate[1] = clock.wait(grad_gate[1])
    held = ffn_outer(pairs(normed_mid), (0, 0), pairs(grad_gate), n_data, 0, None)
    held = ffn_outer(pairs(normed_mid), (0, 0), pairs(grad_up), n_data, 1, held)
    ffn_grads, mark = ffn_outer([grad_ffn, grad_ffn], order, pairs(hidden), n_data, 2, held)
    clock.tick(mark)
    clock.move(mid_flow[1])
    ffn_term = {}
    ffn_term[1] = ffn_back([clock.wait(hidden[1])], ffn_all, 2)
    clock.tick(ffn_term[1])
    clock.move(mid_flow[1])
    ffn_term[0] = ffn_back([clock.wait(hidden[0])], ffn_all, 2)
    mid_own[0] = clock.wait(mid_own[0])
    mid_back(0)
    clock.tick(ffn_term[0], mid_flow[0].own)
    ffn_grads = after(ffn_grads, mid_own[0])
    ffn_sum = lax.psum_scatter(ffn_grads.reshape(-1, hidden_dev), "dp", scatter_dimension=0, tiled=True)
    resid_all = jnp.concatenate([resid_mid[0], resid_mid[1]], axis=0)

    seeds = ()
    grad_q_heads = {}
    grad_kv_heads = {}
    grad_rope = {}

    def heads_back(half):
        back = attend_backward(
            queries,
            keys,
            values,
            grad_mixed[half].reshape(heads_dev, HD, half_tokens),
            log_sums[half],
            cosines,
            sines,
            half,
            seeds,
        )
        grad_q_heads[half] = back[0].reshape(heads_dev * (HD + RD), half_tokens)
        grad_kv_heads[half] = back[1].reshape(heads_dev * 2 * HD, half_tokens)
        grad_rope[half] = back[2]
        return back[3:]

    clock.move(mid_flow[0])
    mixed_back(1)
    seeds = heads_back(1)
    clock.tick(grad_rope[1])
    out_flow = Scatter(jnp.concatenate(both(ffn_term), axis=0), n_model)
    clock.move(mid_flow[0], out_flow)
    clock.tick()
    clock.move(mid_flow[0], out_flow)
    clock.tick()
    clock.move(out_flow)
    mixed_back(0)
    seeds = heads_back(0)
    part_latents = latent_back(
        both(grad_q_heads),
        both(grad_kv_heads),
        both(grad_rope),
        query_up_all,
        latent_up_all,
        both(gain_mid_part),
        gain_rows,
    )
    clock.tick(part_latents)
    latents_sum = lax.psum(after(part_latents, ffn_sum), "mp")
    ffn_own = out_flow.result()

    def wide_rows(value):
        return lax.dynamic_slice_in_dim(value, place * spread, spread, 0)

    output_own = (wide_rows(resid_all) + RESID_SCALE * ffn_own).astype(low_type)
    output_flow = Gather(output_own, n_model, 0)
    output_flow.advance(clock.gate)
    output_flow.advance(tie)
    head_grads = heads_outer(
        both(grad_attn),
        both(mixed),
        both(grad_q_heads),
        both(grad_kv_heads),
        clock.wait(q_normed),
        kv_normed,
        n_data,
        mark,
    )
    head_sum = lax.psum_scatter(
        after(head_grads, latents_sum).reshape(-1, up_width), "dp", scatter_dimension=0, tiled=True
    )
    out_rows = D // n_data // 2
    grad_latents, gain_query_sum, gain_latent_sum = latents_turned(
        latents_sum, latents, cosines, sines, gain_query[None], gain_latent[None]
    )

    def later(*values):
        return lax.optimization_barrier((*values, grad_latents))[: len(values)]

    while output_flow.advance(later):
        pass
    output = output_flow.result()
    gain_rest = jnp.concatenate(
        [gain_query_sum[0], gain_latent_sum[0], wide(latents_sum[tokens_dev:, : QR + KVR]).reshape(-1)[:D]]
    )

    grad_down, gain_in_part = down_outer(normed_in, grad_latents, down_all, gain_in[:, None])
    gain_grad = jnp.concatenate([gain_in_part[:, 0], gain_rest]).reshape(n_data, 1, -1)
    gain_count = gain_grad.shape[2]
    gain_grad = jnp.pad(gain_grad, ((0, 0), (0, gain_rows - 1), (0, width - gain_count)))
    down_mine = lax.dynamic_index_in_dim(
        grad_down.reshape(n_data, n_model, down_rows, width), place, axis=1, keepdims=False
    )
    down_flow = PlaneScatter(
        jnp.concatenate([down_mine, gain_grad.astype(low_type)], axis=1), n_data
    )
    clock.tick(grad_down)
    clock.move(down_flow)
    clock.tick()
    clock.move(down_flow)
    input_grad = input_back(
        clock.wait(grad_latents),
        down_all,
        inputs,
        cotangent,
        jnp.concatenate([mid_norm[0], mid_norm[1]], axis=0),
        gain_in[None],
    )
    clock.tick(input_grad)
    clock.move(down_flow)
    down_sum = wide(down_flow.result())
    ffn_parts = ffn_sum.reshape(3, -1, hidden_dev)
    reduced = (
        down_sum[down_rows, :gain_count],
        down_sum[:down_rows, :QR],
        down_sum[:down_rows, QR:],
        wide(head_sum[out_rows : out_rows + up_rows, : query_up.shape[1]]),
        wide(head_sum[out_rows + up_rows :]),
        wide(
            jnp.concatenate([head_sum[:out_rows, :out_width], head_sum[:out_rows, out_width:]], axis=0).T
        ),
        wide(ffn_parts[0]),
        wide(ffn_parts[1]),
        wide(ffn_parts[2].T),
    )
    weights = (
        norm_gains,
        query_down,
        latent_down,
        query_up,
        latent_up,
        out_proj,
        ffn_gate,
        ffn_up,
        ffn_down,
    )
    firsts = (
        norm_gains_first,
        query_down_first,
        latent_down_first,
        query_up_first,
        latent_up_first,
        out_proj_first,
        ffn_gate_first,
        ffn_up_first,
        ffn_down_first,
    )
    seconds = (
        norm_gains_second,
        query_down_second,
        latent_down_second,
        query_up_second,
        latent_up_second,
        out_proj_second,
        ffn_gate_second,
        ffn_up_second,
        ffn_down_second,
    )
    rates = update_rates()
    updated = [
        adam_step(weights[number], reduced[number], firsts[number], seconds[number], rates[number])
        for number in range(9)
    ]
    return (
        output,
        input_grad,
        updated[0][0],
        updated[0][1],
        updated[0][2],
        updated[1][0],
        updated[1][1],
        updated[1][2],
        updated[2][0],
        updated[2][1],
        updated[2][2],
        updated[3][0],
        updated[3][1],
        updated[3][2],
        updated[4][0],
        updated[4][1],
        updated[4][2],
        updated[5][0],
        updated[5][1],
        updated[5][2],
        updated[6][0],
        updated[6][1],
        updated[6][2],
        updated[7][0],
        updated[7][1],
        updated[7][2],
        updated[8][0],
        updated[8][1],
        updated[8][2],
    )


def solution(mesh):
    placed = (
        P("dp", None),
        P("dp", None),
        P("dp"),
        P("dp"),
        P("dp"),
        P(("dp", "mp"), None),
        P(("dp", "mp"), None),
        P(("dp", "mp"), None),
        P(("dp", "mp"), None),
        P(("dp", "mp"), None),
        P(("dp", "mp"), None),
        P("dp", "mp"),
        P("dp", "mp"),
        P("dp", "mp"),
        P("dp", "mp"),
        P("dp", "mp"),
        P("dp", "mp"),
        P("mp", "dp"),
        P("mp", "dp"),
        P("mp", "dp"),
        P("dp", "mp"),
        P("dp", "mp"),
        P("dp", "mp"),
        P("dp", "mp"),
        P("dp", "mp"),
        P("dp", "mp"),
        P("mp", "dp"),
        P("mp", "dp"),
        P("mp", "dp"),
    )
    return jax.shard_map(
        local,
        mesh=mesh,
        in_specs=placed,
        out_specs=(
            P("dp", None),
            P("dp", None),
            P("dp"),
            P("dp"),
            P("dp"),
            P(("dp", "mp"), None),
            P(("dp", "mp"), None),
            P(("dp", "mp"), None),
            P(("dp", "mp"), None),
            P(("dp", "mp"), None),
            P(("dp", "mp"), None),
            P("dp", "mp"),
            P("dp", "mp"),
            P("dp", "mp"),
            P("dp", "mp"),
            P("dp", "mp"),
            P("dp", "mp"),
            P("mp", "dp"),
            P("mp", "dp"),
            P("mp", "dp"),
            P("dp", "mp"),
            P("dp", "mp"),
            P("dp", "mp"),
            P("dp", "mp"),
            P("dp", "mp"),
            P("dp", "mp"),
            P("mp", "dp"),
            P("mp", "dp"),
            P("mp", "dp"),
        ),
        check_vma=False,
    )
```

```python
import functools
import math

import jax
import jax.numpy as jnp
from jax import lax
from jax.experimental import pallas as pl
from jax.experimental.pallas import tpu as pltpu
from jax.sharding import PartitionSpec as P

D = 2560
QR = 768
KVR = 256
HD = 64
RD = 32
LEN = 1024
STEP = 5


NORM_EPS = 1e-05
RESID_SCALE = 1.4 / math.sqrt(62.0)
ROPE_BASE = 10000.0
BETA_ONE = 0.9
BETA_TWO = 0.95
ADAM_EPS = 1e-08
DECAY_RATE = 0.1


def normalize(vector, gain_vec):
    return (
        vector * lax.rsqrt(jnp.mean(vector * vector, axis=-1, keepdims=True) + NORM_EPS) * gain_vec
    )


def norm_back(vector, gain_vec, gradient):
    unused, pull_back = jax.vjp(normalize, vector, gain_vec)
    return pull_back(gradient)


def tables(length):
    positions = jnp.arange(length).astype(jnp.float32)
    frequency = jnp.exp(jnp.arange(RD // 2).astype(jnp.float32) * (-2.0 * math.log(ROPE_BASE) / RD))
    angles = positions[:, None] * frequency[None, :]
    return (jnp.cos(angles), jnp.sin(angles))


def product(left, right):
    return jnp.dot(left, right, preferred_element_type=jnp.float32)


def contract(spec, left, right):
    return jnp.einsum(spec, left, right, preferred_element_type=jnp.float32)


BLK = 256
ROWS = 512
LIGHT = 100000
VMEM_CAP = 56 * 1024 * 1024


def dot_nn(left, right):
    return lax.dot_general(left, right, (((1,), (0,)), ((), ())), preferred_element_type=jnp.float32)


def dot_nt(left, right):
    return lax.dot_general(left, right, (((1,), (1,)), ((), ())), preferred_element_type=jnp.float32)


def dot_tn(left, right):
    return lax.dot_general(left, right, (((0,), (0,)), ((), ())), preferred_element_type=jnp.float32)


def kernel_params():
    return pltpu.CompilerParams(vmem_limit_bytes=VMEM_CAP)


def light(flops):
    return pl.CostEstimate(flops=flops // LIGHT, bytes_accessed=1024, transcendentals=0)


def causal_tile():
    keys = lax.broadcasted_iota(jnp.int32, (BLK, BLK), 0)
    rows = lax.broadcasted_iota(jnp.int32, (BLK, BLK), 1)
    return keys <= rows


def forward_kernel(first, q_ref, k_ref, v_ref, mixed_ref, lse_ref, score_ref):
    scale_val = (HD + RD) ** (-0.5)
    key_rows = k_ref[0].T
    keep = causal_tile()
    for i in range(q_ref.shape[2] // BLK):
        cols = slice(i * BLK, (i + 1) * BLK)
        q_blk = q_ref[0, :, cols]
        last = first + i
        top = None
        for c in range(last + 1):
            part = slice(c * BLK, (c + 1) * BLK)
            scores = scale_val * dot_nn(key_rows[part], q_blk)
            if c == last:
                scores = jnp.where(keep, scores, -1e30)
            score_ref[part, :] = scores
            peak = jnp.max(scores, axis=0, keepdims=True)
            top = peak if top is None else jnp.maximum(top, peak)
        total = jnp.zeros((1, BLK), jnp.float32)
        mixed = jnp.zeros((HD, BLK), jnp.float32)
        for c in range(last + 1):
            part = slice(c * BLK, (c + 1) * BLK)
            weights = jnp.exp(score_ref[part, :] - top)
            total = total + jnp.sum(weights, axis=0, keepdims=True)
            mixed = mixed + dot_nn(v_ref[0, :, part], weights.astype(jnp.bfloat16))
        mixed_ref[0, :, cols] = (mixed / total).astype(jnp.bfloat16)
        lse_ref[0, :, cols] = top + jnp.log(total)


def attend_forward(queries, keys, values, half):
    heads, unused, length = queries.shape
    size = length // 2
    seen = size * (half + 1)
    spec = lambda rows, cols, place: pl.BlockSpec((1, rows, cols), lambda h: (h, 0, place))
    return pl.pallas_call(
        functools.partial(forward_kernel, half * size // BLK),
        grid=(heads,),
        in_specs=[spec(HD + RD, size, half), spec(HD + RD, seen, 0), spec(HD, seen, 0)],
        out_specs=[spec(HD, size, 0), spec(1, size, 0)],
        out_shape=[
            jax.ShapeDtypeStruct((heads, HD, size), jnp.bfloat16),
            jax.ShapeDtypeStruct((heads, 1, size), jnp.float32),
        ],
        scratch_shapes=[pltpu.VMEM((seen, BLK), jnp.float32)],
        compiler_params=kernel_params(),
        cost_estimate=light(heads * size * seen * 1400),
        name="attend_forward",
    )(queries, keys, values)


def backward_kernel(first, seeded, *refs):
    q_ref, k_ref, v_ref, grad_ref, lse_ref, cos_ref, sin_ref = refs[:7]
    refs = refs[7:]
    if seeded:
        dk_seed, dv_seed = refs[:2]
        dq_ref, dkv_ref, rope_ref = refs[2:5]
        refs = refs[5:]
    else:
        dq_ref, dkv_ref, rope_ref, dk_out, dv_out = refs[:5]
        refs = refs[5:]
    prob_ref, gp_ref, dk_ref, dv_ref = refs
    scale_val = (HD + RD) ** (-0.5)
    half = RD // 2
    key_rows = k_ref[0].T
    value_rows = v_ref[0].T
    keep = causal_tile()
    size = q_ref.shape[2]
    if seeded:
        dk_ref[...] = dk_seed[0]
        dv_ref[...] = dv_seed[0]
    final = size // BLK - 1
    for i in range(final, -1, -1):
        cols = slice(i * BLK, (i + 1) * BLK)
        q_blk = q_ref[0, :, cols]
        grad_blk = grad_ref[0, :, cols]
        lse_blk = lse_ref[0, :, cols]
        last = first + i
        delta = jnp.zeros((1, BLK), jnp.float32)
        for c in range(last + 1):
            part = slice(c * BLK, (c + 1) * BLK)
            scores = scale_val * dot_nn(key_rows[part], q_blk)
            if c == last:
                scores = jnp.where(keep, scores, -1e30)
            probs = jnp.exp(scores - lse_blk)
            grad_probs = dot_nn(value_rows[part], grad_blk)
            prob_ref[part, :] = probs
            gp_ref[part, :] = grad_probs
            delta = delta + jnp.sum(probs * grad_probs, axis=0, keepdims=True)
        dq = jnp.zeros((HD + RD, BLK), jnp.float32)
        for c in range(last + 1):
            part = slice(c * BLK, (c + 1) * BLK)
            probs = prob_ref[part, :]
            grad_scores = (probs * (gp_ref[part, :] - delta)).astype(jnp.bfloat16)
            dq = dq + dot_nn(k_ref[0, :, part], grad_scores)
            dk_part = dot_nt(q_blk, grad_scores)
            dv_part = dot_nt(grad_blk, probs.astype(jnp.bfloat16))
            if i == final and not seeded:
                dk_ref[:, part] = dk_part
                dv_ref[:, part] = dv_part
            else:
                dk_ref[:, part] += dk_part
                dv_ref[:, part] += dv_part
        dq = scale_val * dq
        low = dq[HD : HD + half]
        high = dq[HD + half :]
        cos_blk = cos_ref[:, cols]
        sin_blk = sin_ref[:, cols]
        dq_ref[0, :HD, cols] = dq[:HD].astype(jnp.bfloat16)
        dq_ref[0, HD : HD + half, cols] = (low * cos_blk + high * sin_blk).astype(jnp.bfloat16)
        dq_ref[0, HD + half :, cols] = (high * cos_blk - low * sin_blk).astype(jnp.bfloat16)
    own = slice(first * BLK, first * BLK + size)
    dkv_ref[0, :HD, :] = (scale_val * dk_ref[:HD, own]).astype(jnp.bfloat16)
    dkv_ref[0, HD:, :] = dv_ref[:, own].astype(jnp.bfloat16)
    if not seeded:
        dk_out[0] = dk_ref[:, : first * BLK]
        dv_out[0] = dv_ref[:, : first * BLK]

    @pl.when(pl.program_id(0) == 0)
    def _():
        rope_ref[...] = scale_val * dk_ref[HD:, own]

    @pl.when(pl.program_id(0) != 0)
    def _():
        rope_ref[...] += scale_val * dk_ref[HD:, own]


def attend_backward(queries, keys, values, grad_mixed, lse, cosines, sines, half, seeds):
    heads, unused, length = queries.shape
    size = length // 2
    seen = size * (half + 1)
    spec = lambda rows, cols, place: pl.BlockSpec((1, rows, cols), lambda h: (h, 0, place))
    flat = lambda rows, place: pl.BlockSpec((rows, size), lambda h: (0, place))
    in_specs = [
        spec(HD + RD, size, half),
        spec(HD + RD, seen, 0),
        spec(HD, seen, 0),
        spec(HD, size, 0),
        spec(1, size, 0),
        flat(RD // 2, half),
        flat(RD // 2, half),
    ]
    out_specs = [spec(HD + RD, size, 0), spec(2 * HD, size, 0), flat(RD, 0)]
    out_shape = [
        jax.ShapeDtypeStruct((heads, HD + RD, size), jnp.bfloat16),
        jax.ShapeDtypeStruct((heads, 2 * HD, size), jnp.bfloat16),
        jax.ShapeDtypeStruct((RD, size), jnp.float32),
    ]
    pair = [spec(HD + RD, size, 0), spec(HD, size, 0)]
    if half == 0:
        in_specs = in_specs + pair
    else:
        out_specs = out_specs + pair
        out_shape = out_shape + [
            jax.ShapeDtypeStruct((heads, HD + RD, size), jnp.float32),
            jax.ShapeDtypeStruct((heads, HD, size), jnp.float32),
        ]
    return pl.pallas_call(
        functools.partial(backward_kernel, half * size // BLK, half == 0),
        grid=(heads,),
        in_specs=in_specs,
        out_specs=out_specs,
        out_shape=out_shape,
        scratch_shapes=[
            pltpu.VMEM((seen, BLK), jnp.float32),
            pltpu.VMEM((seen, BLK), jnp.float32),
            pltpu.VMEM((HD + RD, seen), jnp.float32),
            pltpu.VMEM((HD, seen), jnp.float32),
        ],
        compiler_params=kernel_params(),
        cost_estimate=light(heads * size * seen * 3000),
        name="attend_backward",
    )(queries, keys, values, grad_mixed, lse, cosines, sines, *seeds)


def update_rates():
    return [
        (0.25, 0.0),
        (2.5 / math.sqrt(D), DECAY_RATE),
        (2.5 / math.sqrt(D), DECAY_RATE),
        (2.5 / math.sqrt(QR), DECAY_RATE),
        (2.5 / math.sqrt(KVR), DECAY_RATE),
        (1.75, DECAY_RATE),
        (2.5 / math.sqrt(D), DECAY_RATE),
        (2.5 / math.sqrt(D), DECAY_RATE),
        (0.375, DECAY_RATE),
    ]


def adam_step(weight, gradient, first, second, rate_pair):
    first_new = BETA_ONE * first + (1.0 - BETA_ONE) * gradient
    second_new = BETA_TWO * second + (1.0 - BETA_TWO) * gradient * gradient
    first_hat = first_new / (1.0 - BETA_ONE**STEP)
    second_hat = second_new / (1.0 - BETA_TWO**STEP)
    weight_new = weight - rate_pair[0] * (
        first_hat / (jnp.sqrt(second_hat) + ADAM_EPS) + rate_pair[1] * weight
    )
    return (first_new, second_new, weight_new)


def hidden_kernel(grad_ref, weight_ref, out_ref):
    weight = weight_ref[...].reshape(-1, weight_ref.shape[3])

    @pl.when(pl.program_id(1) == 0)
    def _():
        out_ref[...] = dot_nn(grad_ref[...], weight)

    @pl.when(pl.program_id(1) != 0)
    def _():
        out_ref[...] += dot_nn(grad_ref[...], weight)


def hidden_back(grad_out, weights):
    tokens, model = grad_out.shape
    blocks, unused, rows, units = weights.shape
    return pl.pallas_call(
        hidden_kernel,
        grid=(tokens // ROWS, 2),
        in_specs=[
            pl.BlockSpec((ROWS, model // 2), lambda i, k: (i, k)),
            pl.BlockSpec((blocks // 2, 1, rows, units), lambda i, k: (k, 2, 0, 0)),
        ],
        out_specs=pl.BlockSpec((ROWS, units), lambda i, k: (i, 0)),
        out_shape=jax.ShapeDtypeStruct((tokens, units), jnp.float32),
        compiler_params=kernel_params(),
        cost_estimate=light(2 * tokens * model * units),
        name="hidden_back",
    )(grad_out, weights)


def inner_kernel(normed_ref, grad_ref, weight_ref, hidden_ref, gate_ref, up_ref, sum_ref):
    which = pl.program_id(1)
    step = pl.program_id(2)
    weight = weight_ref[...].reshape(-1, weight_ref.shape[3])

    @pl.when(step == 0)
    def _():
        sum_ref[which] = dot_nn(normed_ref[...], weight)

    @pl.when(step != 0)
    def _():
        sum_ref[which] += dot_nn(normed_ref[...], weight)

    @pl.when((which == 1) & (step == pl.num_programs(2) - 1))
    def _():
        gate_val = sum_ref[0]
        up_val = sum_ref[1]
        grad_hidden = grad_ref[...]
        sigmoid_gate = jax.nn.sigmoid(gate_val)
        silu_gate = gate_val * sigmoid_gate
        hidden_ref[...] = (silu_gate * up_val).astype(jnp.bfloat16)
        gate_ref[...] = (
            grad_hidden * up_val * sigmoid_gate * (1.0 + gate_val * (1.0 - sigmoid_gate))
        ).astype(jnp.bfloat16)
        up_ref[...] = (grad_hidden * silu_gate).astype(jnp.bfloat16)


def ffn_inner(normed, grad_hidden, weights, place):
    tokens, model = normed.shape
    blocks, unused, rows, units = weights.shape
    steps = tokens // ROWS
    out = jax.ShapeDtypeStruct((tokens, units), jnp.bfloat16)
    result = pl.BlockSpec((ROWS, units), lambda i, w, k: (i, 0))
    return pl.pallas_call(
        inner_kernel,
        grid=(steps, 2, 2),
        in_specs=[
            pl.BlockSpec((ROWS, model // 2), lambda i, w, k: (i, k)),
            pl.BlockSpec((ROWS, units), lambda i, w, k: (i + place * steps, 0)),
            pl.BlockSpec((blocks // 2, 1, rows, units), lambda i, w, k: (k, w, 0, 0)),
        ],
        out_specs=[result, result, result],
        out_shape=[out, out, out],
        scratch_shapes=[pltpu.VMEM((2, ROWS, units), jnp.float32)],
        compiler_params=kernel_params(),
        cost_estimate=light(4 * tokens * model * units),
        name="ffn_inner",
    )(normed, grad_hidden, weights)


def back_kernel(count, *refs):
    lefts = refs[:count]
    weight_ref = refs[count]
    out_ref = refs[count + 1]
    units = weight_ref.shape[3]
    total = None
    for number in range(count):
        term = dot_nt(lefts[number][...], weight_ref[:, number].reshape(-1, units))
        total = term if total is None else total + term
    out_ref[...] = total.astype(jnp.bfloat16)


def ffn_back(lefts, weights, first):
    tokens, units = lefts[0].shape
    blocks, unused, rows, unused_units = weights.shape
    count = len(lefts)
    model = blocks * rows
    return pl.pallas_call(
        functools.partial(back_kernel, count),
        grid=(2, tokens // ROWS),
        in_specs=[pl.BlockSpec((ROWS, units), lambda k, i: (i, 0)) for unused_left in lefts]
        + [pl.BlockSpec((blocks // 2, count, rows, units), lambda k, i: (k, first, 0, 0))],
        out_specs=pl.BlockSpec((ROWS, model // 2), lambda k, i: (i, k)),
        out_shape=jax.ShapeDtypeStruct((tokens, model), jnp.bfloat16),
        compiler_params=kernel_params(),
        cost_estimate=light(4 * count * tokens * model * units),
        name="ffn_back",
    )(*lefts, weights)


def outer_kernel(count, *refs):
    out_ref, mark_ref = refs[-2:]
    total = dot_tn(refs[0][...], refs[count][...])
    for number in range(1, count):
        total = total + dot_tn(refs[number][...], refs[count + number][...])
    out_ref[...] = total.astype(jnp.bfloat16).reshape(out_ref.shape)
    mark_ref[...] = jnp.zeros(mark_ref.shape, jnp.float32)


def ffn_outer(lefts, places, rights, blocks, slot, held):
    tokens, units = rights[0].shape
    model = lefts[0].shape[1]
    rows = model // blocks
    count = len(lefts)
    left_spec = lambda place: pl.BlockSpec((tokens, model // 2), lambda k: (place, k))
    mark_spec = pl.BlockSpec((8, 128), lambda k: (0, 0))
    held_specs = [] if held is None else [pl.BlockSpec(memory_space=pl.ANY), mark_spec]
    return pl.pallas_call(
        functools.partial(outer_kernel, count),
        grid=(2,),
        in_specs=[left_spec(place) for place in places]
        + [pl.BlockSpec((tokens, units), lambda k: (0, 0)) for unused in rights]
        + held_specs,
        out_specs=[
            pl.BlockSpec((blocks // 2, 1, rows, units), lambda k: (k, slot, 0, 0)),
            mark_spec,
        ],
        out_shape=[
            jax.ShapeDtypeStruct((blocks, 3, rows, units), jnp.bfloat16),
            jax.ShapeDtypeStruct((8, 128), jnp.float32),
        ],
        input_output_aliases={} if held is None else {2 * count: 0},
        compiler_params=kernel_params(),
        cost_estimate=light(4 * count * tokens * model * units),
        name="ffn_outer",
    )(*lefts, *rights, *(held or ()))


def down_kernel(normed_ref, grad_ref, weight_ref, gain_ref, out_ref, part_ref):
    total = dot_tn(normed_ref[...], grad_ref[...])
    out_ref[...] = total.astype(jnp.bfloat16)
    summed = jnp.sum(total * weight_ref[...].astype(jnp.float32), axis=1, keepdims=True)
    part_ref[...] = summed / gain_ref[...]


def down_outer(normed, grads, weights, gains):
    tokens, model = normed.shape
    width = grads.shape[1]
    block = model // 4
    row_spec = lambda cols: pl.BlockSpec((block, cols), lambda k: (k, 0))
    return pl.pallas_call(
        down_kernel,
        grid=(4,),
        in_specs=[
            pl.BlockSpec((tokens, block), lambda k: (0, k)),
            pl.BlockSpec((tokens, width), lambda k: (0, 0)),
            row_spec(width),
            row_spec(1),
        ],
        out_specs=[row_spec(width), row_spec(1)],
        out_shape=[
            jax.ShapeDtypeStruct((model, width), jnp.bfloat16),
            jax.ShapeDtypeStruct((model, 1), jnp.float32),
        ],
        compiler_params=kernel_params(),
        cost_estimate=light(4 * tokens * model * width),
        name="down_outer",
    )(normed, grads, weights, gains)


def input_kernel(grad_ref, weight_ref, inputs_ref, cot_ref, mid_ref, gain_ref, out_ref):
    value = inputs_ref[...].astype(jnp.float32)
    scaled = dot_nt(grad_ref[...], weight_ref[...]) * gain_ref[...]
    rate = lax.rsqrt(jnp.mean(value * value, axis=1, keepdims=True) + NORM_EPS)
    dotted = jnp.mean(scaled * value, axis=1, keepdims=True)
    residual = cot_ref[...].astype(jnp.float32) + mid_ref[...].astype(jnp.float32)
    out_ref[...] = residual + rate * (scaled - value * (rate * rate * dotted))


def input_back(grads, weights, inputs, cotangent, mid_norm, gains):
    tokens, width = grads.shape
    model = inputs.shape[1]
    row_spec = lambda cols: pl.BlockSpec((BLK, cols), lambda i: (i, 0))
    return pl.pallas_call(
        input_kernel,
        grid=(tokens // BLK,),
        in_specs=[
            row_spec(width),
            pl.BlockSpec((model, width), lambda i: (0, 0)),
            row_spec(model),
            row_spec(model),
            row_spec(model),
            pl.BlockSpec((1, model), lambda i: (0, 0)),
        ],
        out_specs=row_spec(model),
        out_shape=jax.ShapeDtypeStruct((tokens, model), jnp.float32),
        compiler_params=kernel_params(),
        cost_estimate=light(4 * tokens * model * width),
        name="input_back",
    )(grads, weights, inputs, cotangent, mid_norm, gains)


def latent_kernel(count, *refs):
    out_ref = refs[-1]
    query_up, latent_up = refs[3 * count], refs[3 * count + 1]
    size = refs[0].shape[1]
    for number in range(count):
        grad_q, grad_kv, rope = refs[number], refs[count + number], refs[2 * count + number]
        rows = slice(number * size, (number + 1) * size)
        out_ref[rows, :QR] = dot_nt(grad_q[...].T, query_up[...]).astype(jnp.bfloat16)
        out_ref[rows, QR : QR + KVR] = dot_nt(grad_kv[...].T, latent_up[...]).astype(jnp.bfloat16)
        out_ref[rows, QR + KVR :] = rope[...].T.astype(jnp.bfloat16)
    mid_part = refs[3 * count + 2][...] + refs[3 * count + 3][...]
    lane = QR + KVR
    lines = []
    for start in range(0, D, lane):
        line = mid_part[:, start : start + lane]
        lines.append(jnp.pad(line, ((0, 0), (0, lane - line.shape[1]))))
    extra = out_ref.shape[0] - count * size
    lines.append(jnp.zeros((extra - len(lines), lane), jnp.float32))
    out_ref[count * size :, :lane] = jnp.concatenate(lines, axis=0).astype(jnp.bfloat16)
    out_ref[count * size :, lane:] = jnp.zeros((extra, RD), jnp.bfloat16)


def latent_back(grads_q, grads_kv, ropes, query_up, latent_up, mid_parts, extra):
    count = len(grads_q)
    tokens = count * grads_q[0].shape[1]
    return pl.pallas_call(
        functools.partial(latent_kernel, count),
        out_shape=jax.ShapeDtypeStruct((tokens + extra, QR + KVR + RD), jnp.bfloat16),
        compiler_params=kernel_params(),
        cost_estimate=light(tokens * (QR + KVR) * 4000),
        name="latent_back",
    )(*grads_q, *grads_kv, *ropes, query_up, latent_up, *mid_parts)


def heads_kernel(count, *refs):
    out_ref = refs[-1]
    q_normed, kv_normed = refs[4 * count], refs[4 * count + 1]
    blocks = out_ref.shape[0]
    size = refs[0].shape[0]
    outer = query_outer = latent_outer = None
    for number in range(count):
        grad_attn, mixed = refs[number], refs[count + number]
        grad_q, grad_kv = refs[2 * count + number], refs[3 * count + number]
        rows = slice(number * size, (number + 1) * size)
        terms = (
            dot_nt(grad_attn[...].T, mixed[...]),
            dot_nt(q_normed[rows].T, grad_q[...]),
            dot_nt(kv_normed[rows].T, grad_kv[...]),
        )
        outer = terms[0] if outer is None else outer + terms[0]
        query_outer = terms[1] if query_outer is None else query_outer + terms[1]
        latent_outer = terms[2] if latent_outer is None else latent_outer + terms[2]
    side = outer.shape[1]
    low = outer.astype(jnp.bfloat16).reshape(blocks, -1, side)
    spread = low.shape[1] // 2
    out_ref[:, :spread, :side] = low[:, :spread]
    out_ref[:, :spread, side:] = low[:, spread:]
    query_rows = query_outer.shape[0] // blocks
    columns = query_outer.shape[1]
    middle = slice(spread, spread + query_rows)
    out_ref[:, middle, :columns] = query_outer.astype(jnp.bfloat16).reshape(blocks, query_rows, columns)
    out_ref[:, middle, columns:] = jnp.zeros(
        (blocks, query_rows, out_ref.shape[2] - columns), jnp.bfloat16
    )
    out_ref[:, spread + query_rows :] = latent_outer.astype(jnp.bfloat16).reshape(
        blocks, -1, out_ref.shape[2]
    )


def heads_outer(grads_attn, mixed, grads_q, grads_kv, q_normed, kv_normed, blocks, mark):
    count = len(mixed)
    size = grads_attn[0].shape[0]
    wide_cols = grads_kv[0].shape[0]
    rows = D // blocks // 2 + QR // blocks + KVR // blocks
    whole = lambda value: pl.BlockSpec(value.shape, lambda k: (0, 0))
    return pl.pallas_call(
        functools.partial(heads_kernel, count),
        grid=(2,),
        in_specs=[pl.BlockSpec((size, D // 2), lambda k: (0, k)) for unused in grads_attn]
        + [whole(value) for value in (*mixed, *grads_q, *grads_kv)]
        + [
            pl.BlockSpec((q_normed.shape[0], QR // 2), lambda k: (0, k)),
            pl.BlockSpec((kv_normed.shape[0], KVR // 2), lambda k: (0, k)),
            pl.BlockSpec((8, 128), lambda k: (0, 0)),
        ],
        out_specs=pl.BlockSpec((blocks // 2, rows, wide_cols), lambda k: (k, 0, 0)),
        out_shape=jax.ShapeDtypeStruct((blocks, rows, wide_cols), jnp.bfloat16),
        compiler_params=kernel_params(),
        cost_estimate=light(count * size * D * wide_cols * 2),
        name="heads_outer",
    )(*grads_attn, *mixed, *grads_q, *grads_kv, q_normed, kv_normed, mark)


def scaled_rate(value):
    return lax.rsqrt(jnp.mean(value * value, axis=1, keepdims=True) + NORM_EPS)


def norm_pull(value, gain_vec, gradient):
    rate = scaled_rate(value)
    scaled = gradient * gain_vec
    dotted = jnp.mean(scaled * value, axis=1, keepdims=True)
    pulled = rate * (scaled - value * (rate * rate * dotted))
    return pulled, jnp.sum(gradient * value * rate, axis=0, keepdims=True)


def latents_kernel(
    inputs_ref, gain_in, down_ref, gain_query, gain_latent, cos_ref, sin_ref,
    normed_ref, latents_ref, q_ref, kv_ref, rope_ref,
):
    value = inputs_ref[...].astype(jnp.float32)
    normed = (value * scaled_rate(value) * gain_in[...]).astype(jnp.bfloat16)
    normed_ref[...] = normed
    latents = dot_nn(normed, down_ref[...])
    latents_ref[...] = latents
    q_latent = latents[:, :QR]
    kv_latent = latents[:, QR : QR + KVR]
    q_ref[...] = (q_latent * scaled_rate(q_latent) * gain_query[...]).astype(jnp.bfloat16)
    kv_ref[...] = (kv_latent * scaled_rate(kv_latent) * gain_latent[...]).astype(jnp.bfloat16)
    rope = latents[:, QR + KVR :].T
    low, high = rope[: RD // 2], rope[RD // 2 :]
    cos_blk, sin_blk = cos_ref[...], sin_ref[...]
    rope_ref[: RD // 2, :] = (low * cos_blk - high * sin_blk).astype(jnp.bfloat16)
    rope_ref[RD // 2 :, :] = (high * cos_blk + low * sin_blk).astype(jnp.bfloat16)


def latents_forward(inputs, gain_in, down_all, gain_query, gain_latent, cosines, sines):
    tokens, model = inputs.shape
    width = down_all.shape[1]
    row_spec = lambda cols: pl.BlockSpec((BLK, cols), lambda i: (i, 0))
    column_spec = lambda rows: pl.BlockSpec((rows, BLK), lambda i: (0, i))
    whole = lambda value: pl.BlockSpec(value.shape, lambda i: (0, 0))
    return pl.pallas_call(
        latents_kernel,
        grid=(tokens // BLK,),
        in_specs=[row_spec(model), whole(gain_in), whole(down_all), whole(gain_query), whole(gain_latent)]
        + [column_spec(RD // 2), column_spec(RD // 2)],
        out_specs=[row_spec(model), row_spec(width), row_spec(QR), row_spec(KVR), column_spec(RD)],
        out_shape=[
            jax.ShapeDtypeStruct((tokens, model), jnp.bfloat16),
            jax.ShapeDtypeStruct((tokens, width), jnp.float32),
            jax.ShapeDtypeStruct((tokens, QR), jnp.bfloat16),
            jax.ShapeDtypeStruct((tokens, KVR), jnp.bfloat16),
            jax.ShapeDtypeStruct((RD, tokens), jnp.bfloat16),
        ],
        compiler_params=kernel_params(),
        cost_estimate=light(tokens * model * width),
        name="latents_forward",
    )(inputs, gain_in, down_all, gain_query, gain_latent, cosines, sines)


def split_kernel(q_ref, kv_ref, rope_ref, query_up, latent_up, cos_ref, sin_ref, queries, keys, values):
    heads = queries.shape[0]
    half = RD // 2
    grown = dot_nt(query_up[...], q_ref[...]).reshape(heads, HD + RD, -1)
    low, high = grown[:, HD : HD + half], grown[:, HD + half :]
    cos_blk, sin_blk = cos_ref[...][None], sin_ref[...][None]
    queries[:, :HD] = grown[:, :HD].astype(jnp.bfloat16)
    queries[:, HD : HD + half] = (low * cos_blk - high * sin_blk).astype(jnp.bfloat16)
    queries[:, HD + half :] = (high * cos_blk + low * sin_blk).astype(jnp.bfloat16)
    grown = dot_nt(latent_up[...], kv_ref[...]).astype(jnp.bfloat16).reshape(heads, 2 * HD, -1)
    keys[:, :HD] = grown[:, :HD]
    keys[:, HD:] = jnp.broadcast_to(rope_ref[...][None], (heads, RD, rope_ref.shape[1]))
    values[...] = grown[:, HD:]


def heads_forward(q_normed, kv_normed, key_rope, query_up, latent_up, cosines, sines):
    tokens = q_normed.shape[0]
    heads = query_up.shape[0] // (HD + RD)
    row_spec = lambda cols: pl.BlockSpec((BLK, cols), lambda i: (i, 0))
    column_spec = lambda rows: pl.BlockSpec((rows, BLK), lambda i: (0, i))
    head_spec = lambda rows: pl.BlockSpec((heads, rows, BLK), lambda i: (0, 0, i))
    whole = lambda value: pl.BlockSpec(value.shape, lambda i: (0, 0))
    return pl.pallas_call(
        split_kernel,
        grid=(tokens // BLK,),
        in_specs=[
            row_spec(QR),
            row_spec(KVR),
            column_spec(RD),
            whole(query_up),
            whole(latent_up),
            column_spec(RD // 2),
            column_spec(RD // 2),
        ],
        out_specs=[head_spec(HD + RD), head_spec(HD + RD), head_spec(HD)],
        out_shape=[
            jax.ShapeDtypeStruct((heads, HD + RD, tokens), jnp.bfloat16),
            jax.ShapeDtypeStruct((heads, HD + RD, tokens), jnp.bfloat16),
            jax.ShapeDtypeStruct((heads, HD, tokens), jnp.bfloat16),
        ],
        compiler_params=kernel_params(),
        cost_estimate=light(tokens * QR),
        name="heads_forward",
    )(q_normed, kv_normed, key_rope, query_up, latent_up, cosines, sines)


def middle_kernel(place_ref, grad_ref, resid_ref, gain_ref, out_ref, part_ref):
    pulled, part = norm_pull(resid_ref[...], gain_ref[...], grad_ref[...].astype(jnp.float32))
    out_ref[...] = pulled.astype(jnp.bfloat16)
    part_ref[...] = part


def middle_back(place, grads, resid, gain_mid):
    rows, model = grads.shape
    fixed = lambda size: pl.BlockSpec((size, model), lambda i, place_ref: (0, 0))
    return pl.pallas_call(
        middle_kernel,
        grid_spec=pltpu.PrefetchScalarGridSpec(
            num_scalar_prefetch=1,
            grid=(1,),
            in_specs=[
                fixed(rows),
                pl.BlockSpec((rows, model), lambda i, place_ref: (place_ref[0], 0)),
                fixed(1),
            ],
            out_specs=[fixed(rows), fixed(1)],
        ),
        out_shape=[
            jax.ShapeDtypeStruct((rows, model), jnp.bfloat16),
            jax.ShapeDtypeStruct((1, model), jnp.float32),
        ],
        compiler_params=kernel_params(),
        cost_estimate=light(rows * model),
        name="middle_back",
    )(place, grads, resid, gain_mid)


def turned_kernel(
    total_ref, latents_ref, cos_ref, sin_ref, gain_query, gain_latent, out_ref, query_ref, latent_ref
):
    half = RD // 2
    total = total_ref[...].astype(jnp.float32)
    latents = latents_ref[...]
    q_pulled, q_part = norm_pull(latents[:, :QR], gain_query[...], total[:, :QR])
    kv_pulled, kv_part = norm_pull(
        latents[:, QR : QR + KVR], gain_latent[...], total[:, QR : QR + KVR]
    )
    low = total[:, QR + KVR : QR + KVR + half]
    high = total[:, QR + KVR + half :]
    cos_blk = cos_ref[...].T
    sin_blk = sin_ref[...].T
    out_ref[:, :QR] = q_pulled.astype(jnp.bfloat16)
    out_ref[:, QR : QR + KVR] = kv_pulled.astype(jnp.bfloat16)
    out_ref[:, QR + KVR : QR + KVR + half] = (low * cos_blk + high * sin_blk).astype(jnp.bfloat16)
    out_ref[:, QR + KVR + half :] = (high * cos_blk - low * sin_blk).astype(jnp.bfloat16)

    @pl.when(pl.program_id(0) == 0)
    def _():
        query_ref[...] = q_part
        latent_ref[...] = kv_part

    @pl.when(pl.program_id(0) != 0)
    def _():
        query_ref[...] += q_part
        latent_ref[...] += kv_part


def latents_turned(total, latents, cosines, sines, gain_query, gain_latent):
    tokens, width = latents.shape
    row_spec = lambda cols: pl.BlockSpec((BLK, cols), lambda i: (i, 0))
    column_spec = pl.BlockSpec((RD // 2, BLK), lambda i: (0, i))
    whole = lambda cols: pl.BlockSpec((1, cols), lambda i: (0, 0))
    return pl.pallas_call(
        turned_kernel,
        grid=(tokens // BLK,),
        in_specs=[
            row_spec(width),
            row_spec(width),
            column_spec,
            column_spec,
            whole(QR),
            whole(KVR),
        ],
        out_specs=[row_spec(width), whole(QR), whole(KVR)],
        out_shape=[
            jax.ShapeDtypeStruct((tokens, width), jnp.bfloat16),
            jax.ShapeDtypeStruct((1, QR), jnp.float32),
            jax.ShapeDtypeStruct((1, KVR), jnp.float32),
        ],
        compiler_params=kernel_params(),
        cost_estimate=light(tokens * width),
        name="latents_turned",
    )(total, latents, cosines, sines, gain_query, gain_latent)


def mixed_kernel(mid_ref, cot_ref, weight_ref, attn_ref, mixed_ref):
    grad_mid = cot_ref[...].astype(jnp.float32) + mid_ref[...].astype(jnp.float32)
    grad_attn = (RESID_SCALE * grad_mid).astype(jnp.bfloat16)
    attn_ref[...] = grad_attn
    mixed_ref[...] = dot_nt(weight_ref[...], grad_attn).astype(jnp.bfloat16)


def mixed_gradient(mid_norm, cotangent, out_own, half):
    tokens, model = mid_norm.shape
    heads_width = out_own.shape[0]
    steps = tokens // BLK
    row_spec = pl.BlockSpec((BLK, model), lambda i: (i, 0))
    return pl.pallas_call(
        mixed_kernel,
        grid=(steps,),
        in_specs=[
            row_spec,
            pl.BlockSpec((BLK, model), lambda i: (i + half * steps, 0)),
            pl.BlockSpec(out_own.shape, lambda i: (0, 0)),
        ],
        out_specs=[row_spec, pl.BlockSpec((heads_width, BLK), lambda i: (0, i))],
        out_shape=[
            jax.ShapeDtypeStruct((tokens, model), jnp.bfloat16),
            jax.ShapeDtypeStruct((heads_width, tokens), jnp.bfloat16),
        ],
        compiler_params=kernel_params(),
        cost_estimate=light(tokens * model),
        name="mixed_gradient",
    )(mid_norm, cotangent, out_own)


def adam_kernel(rate_pair, weight_ref, grad_ref, first_ref, second_ref, first_out, second_out, weight_out):
    gradient = grad_ref[...].astype(jnp.float32)
    updates = adam_step(weight_ref[...], gradient, first_ref[...], second_ref[...], rate_pair)
    first_out[...], second_out[...], weight_out[...] = updates


def adam_rows(weight, grads, slot, first, second, rate_pair):
    rows, cols = weight.shape
    block = pl.BlockSpec((rows // 5, cols), lambda i: (i, 0))
    shape = jax.ShapeDtypeStruct((rows, cols), jnp.float32)
    return pl.pallas_call(
        functools.partial(adam_kernel, rate_pair),
        grid=(5,),
        in_specs=[
            block,
            pl.BlockSpec((rows // 5, cols), lambda i: (5 * slot + i, 0)),
            block,
            block,
        ],
        out_specs=[block, block, block],
        out_shape=[shape, shape, shape],
        compiler_params=kernel_params(),
        cost_estimate=light(rows * cols),
        name="adam_rows",
    )(weight, grads, first, second)


def wide(value):
    return value.astype(jnp.float32)


def tie(*values):
    return lax.optimization_barrier(values)


def after(value, *others):
    return lax.optimization_barrier((value, *others))[0]


def chunk_of(stacked, place):
    return lax.dynamic_index_in_dim(stacked, place, axis=0, keepdims=False)


class Gather:
    def __init__(self, own, count, axis):
        self.own, self.count, self.axis = own, count, axis
        self.below, self.above = [own], [own]

    def advance(self, gate):
        step = len(self.below)
        if step == self.count:
            return []
        up, down = gate(self.below[-1], self.above[-1])
        ups = [(k, k + 1) for k in range(step - 1, self.count - 1)]
        downs = [(k + 1, k) for k in range(self.count - step)]
        self.below.append(lax.ppermute(up, "mp", ups))
        self.above.append(lax.ppermute(down, "mp", downs))
        return [self.below[-1], self.above[-1]]

    def result(self):
        while self.advance(tie):
            pass
        place = lax.axis_index("mp")
        blocks = []
        for slot in range(self.count):
            block = self.own
            for step in range(1, self.count):
                if slot + step < self.count:
                    block = jnp.where(place - step == slot, self.below[step], block)
                if slot - step >= 0:
                    block = jnp.where(place + step == slot, self.above[step], block)
            blocks.append(block)
        return jnp.concatenate(blocks, axis=self.axis)


class Direct:
    def __init__(self, own, count):
        self.own, self.count, self.came = own, count, None

    def advance(self, gate):
        if self.came is not None:
            return []
        (sent,) = gate(self.own)
        count = self.count
        self.came = [
            lax.ppermute(sent, "mp", [(k, (k + step) % count) for k in range(count)])
            for step in range(1, count)
        ]
        return self.came

    def result(self):
        self.advance(tie)
        place = lax.axis_index("mp")
        blocks = []
        for slot in range(self.count):
            block = self.own
            for step in range(1, self.count):
                block = jnp.where((place - step) % self.count == slot, self.came[step - 1], block)
            blocks.append(block)
        return jnp.concatenate(blocks, axis=0)


class Scatter:
    def __init__(self, partial, count):
        self.stacked = partial.reshape(count, partial.shape[0] // count, partial.shape[1])
        self.count, self.step = count, 0
        self.below = self.above = None

    def advance(self, gate):
        count = self.count
        if self.step == count - 1:
            return []
        self.step = step = self.step + 1
        place = lax.axis_index("mp")
        up = chunk_of(self.stacked, jnp.clip(count - step + place, 0, count - 1))
        down = chunk_of(self.stacked, jnp.clip(step - count + place, 0, count - 1))
        if step > 1:
            up = (wide(up) + wide(self.below)).astype(up.dtype)
            down = (wide(down) + wide(self.above)).astype(down.dtype)
        up, down = gate(up, down)
        self.below = lax.ppermute(up, "mp", [(k, k + 1) for k in range(step)])
        downs = [(count - 1 - k, count - 2 - k) for k in range(step)]
        self.above = lax.ppermute(down, "mp", downs)
        return [self.below, self.above]

    def arrived(self):
        while self.advance(tie):
            pass
        return self.below, self.above

    def result(self):
        self.arrived()
        own = chunk_of(self.stacked, lax.axis_index("mp"))
        return wide(own) + wide(self.below) + wide(self.above)


class Plane:
    def __init__(self, block, count):
        rows = block.shape[0] // 2
        bits = [1 << k for k in range(1, count.bit_length() - 1)]
        self.count, self.step = count, 0
        self.orders = [bits + [1], bits[::-1] + [1]]
        self.held = [block[None, :rows], block[None, rows:]]

    def advance(self, gate):
        if self.step == len(self.orders[0]):
            return []
        held = gate(*self.held)
        came = []
        for part, order in zip(held, self.orders):
            pairs = [(k, k ^ order[self.step]) for k in range(self.count)]
            came.append(lax.ppermute(part, "dp", pairs))
        self.held = [jnp.concatenate([part, other], axis=0) for part, other in zip(self.held, came)]
        self.step += 1
        return came

    def result(self):
        while self.advance(tie):
            pass
        place = lax.axis_index("dp")
        blocks = []
        for number in range(self.count):
            apart = jnp.bitwise_xor(place, number)
            for part, order in zip(self.held, self.orders):
                spot = sum(
                    jnp.where(jnp.bitwise_and(apart, bit) != 0, 1 << step, 0)
                    for step, bit in enumerate(order)
                )
                blocks.append(chunk_of(part, spot))
        return jnp.concatenate(blocks, axis=0)


class PlaneScatter:
    def __init__(self, stacked, count):
        self.bits = count.bit_length() - 1
        self.left = stacked.reshape((2,) * self.bits + stacked.shape[1:])
        self.step = 0

    def advance(self, gate):
        if self.step == self.bits:
            return []
        bit = 1 << self.step
        axis = self.bits - 1 - self.step
        mine = jnp.where(jnp.bitwise_and(lax.axis_index("dp"), bit) != 0, 1, 0)
        kept = lax.dynamic_index_in_dim(self.left, mine, axis, keepdims=False)
        (gone,) = gate(lax.dynamic_index_in_dim(self.left, 1 - mine, axis, keepdims=False))
        pairs = [(k, k ^ bit) for k in range(1 << self.bits)]
        came = lax.ppermute(gone, "dp", pairs)
        self.left = (wide(kept) + wide(came)).astype(kept.dtype)
        self.step += 1
        return [came]

    def result(self):
        while self.advance(tie):
            pass
        return self.left


class Clock:
    def __init__(self):
        self.past, self.present = (), []

    def gate(self, *values):
        return lax.optimization_barrier((*values, *self.past))[: len(values)]

    def wait(self, value):
        return self.gate(value)[0]

    def move(self, *flows):
        for flow in flows:
            self.present += flow.advance(self.gate)

    def tick(self, *values):
        if self.present or values:
            self.past = (*self.present, *values)
            self.present = []


def local(
    inputs,
    cotangent,
    norm_gains,
    norm_gains_first,
    norm_gains_second,
    query_down,
    query_down_first,
    query_down_second,
    latent_down,
    latent_down_first,
    latent_down_second,
    query_up,
    query_up_first,
    query_up_second,
    latent_up,
    latent_up_first,
    latent_up_second,
    out_proj,
    out_proj_first,
    out_proj_second,
    ffn_gate,
    ffn_gate_first,
    ffn_gate_second,
    ffn_up,
    ffn_up_first,
    ffn_up_second,
    ffn_down,
    ffn_down_first,
    ffn_down_second,
):
    low_type = jnp.bfloat16
    tokens_dev = inputs.shape[0]
    n_data = lax.axis_size("dp")
    n_model = lax.axis_size("mp")
    place = lax.axis_index("mp")
    heads_dev = query_up.shape[1] // (HD + RD)
    half_tokens = tokens_dev // 2
    own_tokens = half_tokens // n_model
    spread = tokens_dev // n_model
    hidden_dev = ffn_gate.shape[1]
    out_width = heads_dev * HD
    down_rows = query_down.shape[0]
    width = QR + KVR + RD
    gain_rows = 16
    order = (1, 0)

    def own_rows(value):
        return lax.dynamic_slice_in_dim(value, place * own_tokens, own_tokens, 0)

    def half_of(value, half):
        return value[half * half_tokens : (half + 1) * half_tokens]

    up_rows = query_up.shape[0]
    kv_rows = latent_up.shape[0]
    up_width = latent_up.shape[1]
    gains_high = lax.reduce_precision(norm_gains, 8, 7)
    up_pack = jnp.concatenate(
        [
            jnp.pad(query_up.astype(low_type), ((0, 0), (0, up_width - query_up.shape[1]))),
            latent_up.astype(low_type),
            jnp.pad(
                jnp.stack([gains_high, norm_gains - gains_high]).astype(low_type),
                ((0, gain_rows - 2), (0, up_width - norm_gains.shape[0])),
            ),
        ],
        axis=0,
    )
    down_own = jnp.concatenate([query_down, latent_down], axis=1).astype(low_type)
    up_flow = Plane(up_pack, n_data)
    down_flow = Direct(down_own, n_model)
    out_flow = Gather(out_proj.T.astype(low_type), n_model, 1)
    clock = Clock()
    clock.move(down_flow)
    clock.tick()
    down_flow = Plane(down_flow.result(), n_data)
    for unused in range(3):
        clock.move(down_flow, up_flow, out_flow)
        clock.tick()
    up_all = up_flow.result().reshape(n_data, -1, up_width)
    down_all = down_flow.result()
    out_all = lax.all_gather(out_flow.result(), "dp", axis=0, tiled=True)
    out_own = lax.dynamic_slice_in_dim(out_all, place * out_width, out_width, 1).T
    ffn_pack = jnp.stack([ffn_gate, ffn_up, ffn_down.T]).astype(low_type)
    ffn_all = lax.all_gather(ffn_pack, "dp", axis=0, tiled=False)
    query_up_all = up_all[:, :up_rows, : query_up.shape[1]].reshape(QR, query_up.shape[1])
    latent_up_all = up_all[:, up_rows : up_rows + kv_rows].reshape(KVR, up_width)
    gains_sent = wide(up_all[:, up_rows + kv_rows : up_rows + kv_rows + 2, : norm_gains.shape[0]])
    gains_all = (gains_sent[:, 0] + gains_sent[:, 1]).reshape(-1)
    gain_in = gains_all[:D]
    gain_query = gains_all[D : D + QR]
    gain_latent = gains_all[D + QR : D + QR + KVR]
    gain_mid = gains_all[D + QR + KVR :]
    cosines, sines = tables(LEN)
    cosines = cosines.T
    sines = sines.T

    normed_in, latents, q_normed, kv_normed, key_rope = latents_forward(
        inputs, gain_in[None], down_all, gain_query[None], gain_latent[None], cosines, sines
    )
    queries, keys, values = heads_forward(
        q_normed, kv_normed, key_rope, query_up_all.T, latent_up_all.T, cosines, sines
    )
    mixed = {}
    log_sums = {}
    resid_mid = {}
    normed_mid = {}
    grad_ffn = (RESID_SCALE * wide(cotangent)).astype(low_type)
    mixed_flow = {}
    for half in order:
        asked = queries if half == 1 else clock.wait(queries)
        mixed[half], log_sums[half] = attend_forward(asked, keys, values, half)
        mixed[half] = mixed[half].reshape(out_width, half_tokens)
        mixed_flow[half] = Gather(mixed[half], n_model, 0)
        clock.tick(mixed[half])
        clock.move(mixed_flow[1])
    grad_hidden = hidden_back(clock.wait(grad_ffn), ffn_all)
    clock.tick(grad_hidden)
    clock.move(mixed_flow[1])
    clock.tick()
    clock.move(mixed_flow[0])

    def middle(half):
        mixed_all = clock.wait(mixed_flow[half].result())
        attn_out = contract("ht,dh->td", mixed_all, out_all)
        resid_mid[half] = wide(half_of(inputs, half)) + RESID_SCALE * attn_out
        normed_mid[half] = normalize(resid_mid[half], gain_mid).astype(low_type)
        clock.tick(normed_mid[half])

    hidden = {}
    grad_gate = {}
    grad_up = {}
    part_mid = {}
    mid_own = {}
    for half in order:
        middle(half)
        clock.move(mixed_flow[0])
        hidden[half], grad_gate[half], grad_up[half] = ffn_inner(
            clock.wait(normed_mid[half]), grad_hidden, ffn_all, half
        )
        clock.tick(grad_up[half])
        clock.move(mixed_flow[0])
        part_mid[half] = ffn_back([clock.wait(grad_gate[half]), grad_up[half]], ffn_all, 0)
        clock.tick(part_mid[half])
        sent_mid = part_mid[half] if half == 1 else after(part_mid[half], mid_own[1])
        mid_own[half] = lax.psum_scatter(sent_mid, "mp", scatter_dimension=0, tiled=True)
    pairs = lambda values: [values[half] for half in order]
    both = lambda values: [values[half] for half in (0, 1)]
    mid_norm = {}
    mid_flow = {}
    gain_mid_part = {}
    grad_attn = {}
    grad_mixed = {}

    def mid_back(half):
        own, gain_mid_part[half] = middle_back(
            place[None], mid_own[half], resid_mid[half], gain_mid[None]
        )
        mid_flow[half] = Gather(own, n_model, 0)

    def mixed_back(half):
        mid_norm[half] = mid_flow[half].result()
        grad_attn[half], grad_mixed[half] = mixed_gradient(
            clock.wait(mid_norm[half]), cotangent, out_own, half
        )

    mid_back(1)
    clock.move(mid_flow[1])
    grad_gate[1] = clock.wait(grad_gate[1])
    held = ffn_outer(pairs(normed_mid), (0, 0), pairs(grad_gate), n_data, 0, None)
    grad_up[1] = after(grad_up[1], out_own)
    held = ffn_outer(pairs(normed_mid), (0, 0), pairs(grad_up), n_data, 1, held)
    ffn_grads, mark = ffn_outer([grad_ffn, grad_ffn], order, pairs(hidden), n_data, 2, held)
    clock.tick(mark)
    clock.move(mid_flow[1])
    ffn_term = {}
    for half in order:
        ffn_term[half] = ffn_back([clock.wait(hidden[half])], ffn_all, 2)
    clock.tick(ffn_term[1], ffn_term[0])
    clock.move(mid_flow[1])
    ffn_term = jnp.concatenate([clock.wait(ffn_term[0]), ffn_term[1]], axis=0)
    mid_own[0] = clock.wait(mid_own[0])
    mid_back(0)
    clock.tick(ffn_term, mid_flow[0].own)
    ffn_grads = after(ffn_grads, mid_own[0])
    ffn_sum = lax.psum_scatter(ffn_grads.reshape(-1, hidden_dev), "dp", scatter_dimension=0, tiled=True)
    resid_all = jnp.concatenate([resid_mid[0], resid_mid[1]], axis=0)

    seeds = ()
    grad_q_heads = {}
    grad_kv_heads = {}
    grad_rope = {}

    def heads_back(half):
        back = attend_backward(
            queries,
            keys,
            values,
            grad_mixed[half].reshape(heads_dev, HD, half_tokens),
            log_sums[half],
            cosines,
            sines,
            half,
            seeds,
        )
        grad_q_heads[half] = back[0].reshape(heads_dev * (HD + RD), half_tokens)
        grad_kv_heads[half] = back[1].reshape(heads_dev * 2 * HD, half_tokens)
        grad_rope[half] = back[2]
        return back[3:]

    clock.move(mid_flow[0])
    mixed_back(1)
    seeds = heads_back(1)
    clock.tick(grad_rope[1])
    out_flow = Scatter(ffn_term, n_model)
    clock.move(mid_flow[0], out_flow)
    clock.tick()
    clock.move(mid_flow[0], out_flow)
    clock.tick()
    clock.move(out_flow)
    mixed_back(0)
    seeds = heads_back(0)
    part_latents = latent_back(
        both(grad_q_heads),
        both(grad_kv_heads),
        both(grad_rope),
        query_up_all,
        latent_up_all,
        both(gain_mid_part),
        gain_rows,
    )
    clock.tick(part_latents)
    latents_sum = lax.psum(after(part_latents, ffn_sum), "mp")
    ffn_own = out_flow.result()

    def wide_rows(value):
        return lax.dynamic_slice_in_dim(value, place * spread, spread, 0)

    output_own = (wide_rows(resid_all) + RESID_SCALE * ffn_own).astype(low_type)
    output_flow = Gather(output_own, n_model, 0)
    arrived = output_flow.advance(clock.gate)
    output_flow.advance(tie)
    head_grads = heads_outer(
        both(grad_attn),
        both(mixed),
        both(grad_q_heads),
        both(grad_kv_heads),
        after(q_normed, *arrived),
        kv_normed,
        n_data,
        mark,
    )
    ffn_rates = update_rates()[6:]
    ffn_late = after(ffn_sum, *arrived)
    gate_updates = adam_rows(ffn_gate, ffn_late, 0, ffn_gate_first, ffn_gate_second, ffn_rates[0])
    up_updates = adam_rows(ffn_up, ffn_late, 1, ffn_up_first, ffn_up_second, ffn_rates[1])
    latents_sum = after(latents_sum, head_grads, gate_updates[2], up_updates[2])
    head_sum = lax.psum_scatter(
        after(head_grads, latents_sum).reshape(-1, up_width), "dp", scatter_dimension=0, tiled=True
    )
    out_rows = D // n_data // 2
    grad_latents, gain_query_sum, gain_latent_sum = latents_turned(
        latents_sum, latents, cosines, sines, gain_query[None], gain_latent[None]
    )

    def later(*values):
        return lax.optimization_barrier((*values, grad_latents))[: len(values)]

    while output_flow.advance(later):
        pass
    output = output_flow.result()
    gain_rest = jnp.concatenate(
        [gain_query_sum[0], gain_latent_sum[0], wide(latents_sum[tokens_dev:, : QR + KVR]).reshape(-1)[:D]]
    )

    grad_down, gain_in_part = down_outer(normed_in, grad_latents, down_all, gain_in[:, None])
    gain_grad = jnp.concatenate([gain_in_part[:, 0], gain_rest]).reshape(n_data, 1, -1)
    gain_count = gain_grad.shape[2]
    gain_grad = jnp.pad(gain_grad, ((0, 0), (0, gain_rows - 1), (0, width - gain_count)))
    down_mine = lax.dynamic_index_in_dim(
        grad_down.reshape(n_data, n_model, down_rows, width), place, axis=1, keepdims=False
    )
    down_flow = PlaneScatter(
        jnp.concatenate([down_mine, gain_grad.astype(low_type)], axis=1), n_data
    )
    clock.tick(grad_down)
    clock.move(down_flow)
    clock.tick()
    clock.move(down_flow)
    input_grad = input_back(
        clock.wait(grad_latents),
        down_all,
        inputs,
        cotangent,
        jnp.concatenate([mid_norm[0], mid_norm[1]], axis=0),
        gain_in[None],
    )
    clock.tick(input_grad)
    clock.move(down_flow)
    down_sum = wide(down_flow.result())
    down_rate = ffn_rates[2]
    down_part = ffn_sum.reshape(3, -1, hidden_dev)[2].T
    ffn_updated = [
        gate_updates,
        up_updates,
        adam_step(ffn_down, wide(down_part), ffn_down_first, ffn_down_second, down_rate),
    ]
    reduced = (
        down_sum[down_rows, :gain_count],
        down_sum[:down_rows, :QR],
        down_sum[:down_rows, QR:],
        wide(head_sum[out_rows : out_rows + up_rows, : query_up.shape[1]]),
        wide(head_sum[out_rows + up_rows :]),
        wide(
            jnp.concatenate([head_sum[:out_rows, :out_width], head_sum[:out_rows, out_width:]], axis=0).T
        ),
    )
    weights = (
        norm_gains,
        query_down,
        latent_down,
        query_up,
        latent_up,
        out_proj,
        ffn_gate,
        ffn_up,
        ffn_down,
    )
    firsts = (
        norm_gains_first,
        query_down_first,
        latent_down_first,
        query_up_first,
        latent_up_first,
        out_proj_first,
        ffn_gate_first,
        ffn_up_first,
        ffn_down_first,
    )
    seconds = (
        norm_gains_second,
        query_down_second,
        latent_down_second,
        query_up_second,
        latent_up_second,
        out_proj_second,
        ffn_gate_second,
        ffn_up_second,
        ffn_down_second,
    )
    rates = update_rates()
    updated = [
        adam_step(weights[number], reduced[number], firsts[number], seconds[number], rates[number])
        for number in range(6)
    ] + ffn_updated
    return (
        output,
        input_grad,
        updated[0][0],
        updated[0][1],
        updated[0][2],
        updated[1][0],
        updated[1][1],
        updated[1][2],
        updated[2][0],
        updated[2][1],
        updated[2][2],
        updated[3][0],
        updated[3][1],
        updated[3][2],
        updated[4][0],
        updated[4][1],
        updated[4][2],
        updated[5][0],
        updated[5][1],
        updated[5][2],
        updated[6][0],
        updated[6][1],
        updated[6][2],
        updated[7][0],
        updated[7][1],
        updated[7][2],
        updated[8][0],
        updated[8][1],
        updated[8][2],
    )


def solution(mesh):
    placed = (
        P("dp", None),
        P("dp", None),
        P("dp"),
        P("dp"),
        P("dp"),
        P(("dp", "mp"), None),
        P(("dp", "mp"), None),
        P(("dp", "mp"), None),
        P(("dp", "mp"), None),
        P(("dp", "mp"), None),
        P(("dp", "mp"), None),
        P("dp", "mp"),
        P("dp", "mp"),
        P("dp", "mp"),
        P("dp", "mp"),
        P("dp", "mp"),
        P("dp", "mp"),
        P("mp", "dp"),
        P("mp", "dp"),
        P("mp", "dp"),
        P("dp", "mp"),
        P("dp", "mp"),
        P("dp", "mp"),
        P("dp", "mp"),
        P("dp", "mp"),
        P("dp", "mp"),
        P("mp", "dp"),
        P("mp", "dp"),
        P("mp", "dp"),
    )
    return jax.shard_map(
        local,
        mesh=mesh,
        in_specs=placed,
        out_specs=(
            P("dp", None),
            P("dp", None),
            P("dp"),
            P("dp"),
            P("dp"),
            P(("dp", "mp"), None),
            P(("dp", "mp"), None),
            P(("dp", "mp"), None),
            P(("dp", "mp"), None),
            P(("dp", "mp"), None),
            P(("dp", "mp"), None),
            P("dp", "mp"),
            P("dp", "mp"),
            P("dp", "mp"),
            P("dp", "mp"),
            P("dp", "mp"),
            P("dp", "mp"),
            P("mp", "dp"),
            P("mp", "dp"),
            P("mp", "dp"),
            P("dp", "mp"),
            P("dp", "mp"),
            P("dp", "mp"),
            P("dp", "mp"),
            P("dp", "mp"),
            P("dp", "mp"),
            P("mp", "dp"),
            P("mp", "dp"),
            P("mp", "dp"),
        ),
        check_vma=False,
    )
```

```python
import functools
import math

import jax
import jax.numpy as jnp
from jax import lax
from jax.experimental import pallas as pl
from jax.experimental.pallas import tpu as pltpu
from jax.sharding import PartitionSpec as P

D = 2560
QR = 768
KVR = 256
HD = 64
RD = 32
LEN = 1024
STEP = 5


NORM_EPS = 1e-05
RESID_SCALE = 1.4 / math.sqrt(62.0)
ROPE_BASE = 10000.0
BETA_ONE = 0.9
BETA_TWO = 0.95
ADAM_EPS = 1e-08
DECAY_RATE = 0.1


def normalize(vector, gain_vec):
    return (
        vector * lax.rsqrt(jnp.mean(vector * vector, axis=-1, keepdims=True) + NORM_EPS) * gain_vec
    )


def norm_back(vector, gain_vec, gradient):
    unused, pull_back = jax.vjp(normalize, vector, gain_vec)
    return pull_back(gradient)


def tables(length):
    positions = jnp.arange(length).astype(jnp.float32)
    frequency = jnp.exp(jnp.arange(RD // 2).astype(jnp.float32) * (-2.0 * math.log(ROPE_BASE) / RD))
    angles = positions[:, None] * frequency[None, :]
    return (jnp.cos(angles), jnp.sin(angles))


def product(left, right):
    return jnp.dot(left, right, preferred_element_type=jnp.float32)


def contract(spec, left, right):
    return jnp.einsum(spec, left, right, preferred_element_type=jnp.float32)


BLK = 256
ROWS = 512
LIGHT = 100000
VMEM_CAP = 56 * 1024 * 1024


def dot_nn(left, right):
    return lax.dot_general(left, right, (((1,), (0,)), ((), ())), preferred_element_type=jnp.float32)


def dot_nt(left, right):
    return lax.dot_general(left, right, (((1,), (1,)), ((), ())), preferred_element_type=jnp.float32)


def dot_tn(left, right):
    return lax.dot_general(left, right, (((0,), (0,)), ((), ())), preferred_element_type=jnp.float32)


def kernel_params():
    return pltpu.CompilerParams(vmem_limit_bytes=VMEM_CAP)


def light(flops):
    return pl.CostEstimate(flops=flops // LIGHT, bytes_accessed=1024, transcendentals=0)


def causal_tile():
    keys = lax.broadcasted_iota(jnp.int32, (BLK, BLK), 0)
    rows = lax.broadcasted_iota(jnp.int32, (BLK, BLK), 1)
    return keys <= rows


def forward_kernel(first, q_ref, k_ref, v_ref, mixed_ref, lse_ref, score_ref):
    scale_val = (HD + RD) ** (-0.5)
    key_rows = k_ref[0].T
    keep = causal_tile()
    for i in range(q_ref.shape[2] // BLK):
        cols = slice(i * BLK, (i + 1) * BLK)
        q_blk = q_ref[0, :, cols]
        last = first + i
        top = None
        for c in range(last + 1):
            part = slice(c * BLK, (c + 1) * BLK)
            scores = scale_val * dot_nn(key_rows[part], q_blk)
            if c == last:
                scores = jnp.where(keep, scores, -1e30)
            score_ref[part, :] = scores
            peak = jnp.max(scores, axis=0, keepdims=True)
            top = peak if top is None else jnp.maximum(top, peak)
        total = jnp.zeros((1, BLK), jnp.float32)
        mixed = jnp.zeros((HD, BLK), jnp.float32)
        for c in range(last + 1):
            part = slice(c * BLK, (c + 1) * BLK)
            weights = jnp.exp(score_ref[part, :] - top)
            total = total + jnp.sum(weights, axis=0, keepdims=True)
            mixed = mixed + dot_nn(v_ref[0, :, part], weights.astype(jnp.bfloat16))
        mixed_ref[0, :, cols] = (mixed / total).astype(jnp.bfloat16)
        lse_ref[0, :, cols] = top + jnp.log(total)


def attend_forward(queries, keys, values, half):
    heads, unused, length = queries.shape
    size = length // 2
    seen = size * (half + 1)
    spec = lambda rows, cols, place: pl.BlockSpec((1, rows, cols), lambda h: (h, 0, place))
    return pl.pallas_call(
        functools.partial(forward_kernel, half * size // BLK),
        grid=(heads,),
        in_specs=[spec(HD + RD, size, half), spec(HD + RD, seen, 0), spec(HD, seen, 0)],
        out_specs=[spec(HD, size, 0), spec(1, size, 0)],
        out_shape=[
            jax.ShapeDtypeStruct((heads, HD, size), jnp.bfloat16),
            jax.ShapeDtypeStruct((heads, 1, size), jnp.float32),
        ],
        scratch_shapes=[pltpu.VMEM((seen, BLK), jnp.float32)],
        compiler_params=kernel_params(),
        cost_estimate=light(heads * size * seen * 1400),
        name="attend_forward",
    )(queries, keys, values)


def backward_kernel(first, seeded, *refs):
    q_ref, k_ref, v_ref, grad_ref, lse_ref, cos_ref, sin_ref = refs[:7]
    refs = refs[7:]
    if seeded:
        dk_seed, dv_seed = refs[:2]
        dq_ref, dkv_ref, rope_ref = refs[2:5]
        refs = refs[5:]
    else:
        dq_ref, dkv_ref, rope_ref, dk_out, dv_out = refs[:5]
        refs = refs[5:]
    prob_ref, gp_ref, dk_ref, dv_ref = refs
    scale_val = (HD + RD) ** (-0.5)
    half = RD // 2
    key_rows = k_ref[0].T
    value_rows = v_ref[0].T
    keep = causal_tile()
    size = q_ref.shape[2]
    if seeded:
        dk_ref[...] = dk_seed[0]
        dv_ref[...] = dv_seed[0]
    final = size // BLK - 1
    for i in range(final, -1, -1):
        cols = slice(i * BLK, (i + 1) * BLK)
        q_blk = q_ref[0, :, cols]
        grad_blk = grad_ref[0, :, cols]
        lse_blk = lse_ref[0, :, cols]
        last = first + i
        delta = jnp.zeros((1, BLK), jnp.float32)
        for c in range(last + 1):
            part = slice(c * BLK, (c + 1) * BLK)
            scores = scale_val * dot_nn(key_rows[part], q_blk)
            if c == last:
                scores = jnp.where(keep, scores, -1e30)
            probs = jnp.exp(scores - lse_blk)
            grad_probs = dot_nn(value_rows[part], grad_blk)
            prob_ref[part, :] = probs
            gp_ref[part, :] = grad_probs
            delta = delta + jnp.sum(probs * grad_probs, axis=0, keepdims=True)
        dq = jnp.zeros((HD + RD, BLK), jnp.float32)
        for c in range(last + 1):
            part = slice(c * BLK, (c + 1) * BLK)
            probs = prob_ref[part, :]
            grad_scores = (probs * (gp_ref[part, :] - delta)).astype(jnp.bfloat16)
            dq = dq + dot_nn(k_ref[0, :, part], grad_scores)
            dk_part = dot_nt(q_blk, grad_scores)
            dv_part = dot_nt(grad_blk, probs.astype(jnp.bfloat16))
            if i == final and not seeded:
                dk_ref[:, part] = dk_part
                dv_ref[:, part] = dv_part
            else:
                dk_ref[:, part] += dk_part
                dv_ref[:, part] += dv_part
        dq = scale_val * dq
        low = dq[HD : HD + half]
        high = dq[HD + half :]
        cos_blk = cos_ref[:, cols]
        sin_blk = sin_ref[:, cols]
        dq_ref[0, :HD, cols] = dq[:HD].astype(jnp.bfloat16)
        dq_ref[0, HD : HD + half, cols] = (low * cos_blk + high * sin_blk).astype(jnp.bfloat16)
        dq_ref[0, HD + half :, cols] = (high * cos_blk - low * sin_blk).astype(jnp.bfloat16)
    own = slice(first * BLK, first * BLK + size)
    dkv_ref[0, :HD, :] = (scale_val * dk_ref[:HD, own]).astype(jnp.bfloat16)
    dkv_ref[0, HD:, :] = dv_ref[:, own].astype(jnp.bfloat16)
    if not seeded:
        dk_out[0] = dk_ref[:, : first * BLK]
        dv_out[0] = dv_ref[:, : first * BLK]

    @pl.when(pl.program_id(0) == 0)
    def _():
        rope_ref[...] = scale_val * dk_ref[HD:, own]

    @pl.when(pl.program_id(0) != 0)
    def _():
        rope_ref[...] += scale_val * dk_ref[HD:, own]


def attend_backward(queries, keys, values, grad_mixed, lse, cosines, sines, half, seeds):
    heads, unused, length = queries.shape
    size = length // 2
    seen = size * (half + 1)
    spec = lambda rows, cols, place: pl.BlockSpec((1, rows, cols), lambda h: (h, 0, place))
    flat = lambda rows, place: pl.BlockSpec((rows, size), lambda h: (0, place))
    in_specs = [
        spec(HD + RD, size, half),
        spec(HD + RD, seen, 0),
        spec(HD, seen, 0),
        spec(HD, size, 0),
        spec(1, size, 0),
        flat(RD // 2, half),
        flat(RD // 2, half),
    ]
    out_specs = [spec(HD + RD, size, 0), spec(2 * HD, size, 0), flat(RD, 0)]
    out_shape = [
        jax.ShapeDtypeStruct((heads, HD + RD, size), jnp.bfloat16),
        jax.ShapeDtypeStruct((heads, 2 * HD, size), jnp.bfloat16),
        jax.ShapeDtypeStruct((RD, size), jnp.float32),
    ]
    pair = [spec(HD + RD, size, 0), spec(HD, size, 0)]
    if half == 0:
        in_specs = in_specs + pair
    else:
        out_specs = out_specs + pair
        out_shape = out_shape + [
            jax.ShapeDtypeStruct((heads, HD + RD, size), jnp.float32),
            jax.ShapeDtypeStruct((heads, HD, size), jnp.float32),
        ]
    return pl.pallas_call(
        functools.partial(backward_kernel, half * size // BLK, half == 0),
        grid=(heads,),
        in_specs=in_specs,
        out_specs=out_specs,
        out_shape=out_shape,
        scratch_shapes=[
            pltpu.VMEM((seen, BLK), jnp.float32),
            pltpu.VMEM((seen, BLK), jnp.float32),
            pltpu.VMEM((HD + RD, seen), jnp.float32),
            pltpu.VMEM((HD, seen), jnp.float32),
        ],
        compiler_params=kernel_params(),
        cost_estimate=light(heads * size * seen * 3000),
        name="attend_backward",
    )(queries, keys, values, grad_mixed, lse, cosines, sines, *seeds)


def update_rates():
    return [
        (0.25, 0.0),
        (2.5 / math.sqrt(D), DECAY_RATE),
        (2.5 / math.sqrt(D), DECAY_RATE),
        (2.5 / math.sqrt(QR), DECAY_RATE),
        (2.5 / math.sqrt(KVR), DECAY_RATE),
        (1.75, DECAY_RATE),
        (2.5 / math.sqrt(D), DECAY_RATE),
        (2.5 / math.sqrt(D), DECAY_RATE),
        (0.375, DECAY_RATE),
    ]


def adam_step(weight, gradient, first, second, rate_pair):
    first_new = BETA_ONE * first + (1.0 - BETA_ONE) * gradient
    second_new = BETA_TWO * second + (1.0 - BETA_TWO) * gradient * gradient
    first_hat = first_new / (1.0 - BETA_ONE**STEP)
    second_hat = second_new / (1.0 - BETA_TWO**STEP)
    weight_new = weight - rate_pair[0] * (
        first_hat / (jnp.sqrt(second_hat) + ADAM_EPS) + rate_pair[1] * weight
    )
    return (first_new, second_new, weight_new)


def hidden_kernel(grad_ref, weight_ref, out_ref):
    weight = weight_ref[...].reshape(-1, weight_ref.shape[3])

    @pl.when(pl.program_id(1) == 0)
    def _():
        out_ref[...] = dot_nn(grad_ref[...], weight)

    @pl.when(pl.program_id(1) != 0)
    def _():
        out_ref[...] += dot_nn(grad_ref[...], weight)


def hidden_back(grad_out, weights):
    tokens, model = grad_out.shape
    blocks, unused, rows, units = weights.shape
    return pl.pallas_call(
        hidden_kernel,
        grid=(tokens // ROWS, 2),
        in_specs=[
            pl.BlockSpec((ROWS, model // 2), lambda i, k: (i, k)),
            pl.BlockSpec((blocks // 2, 1, rows, units), lambda i, k: (k, 2, 0, 0)),
        ],
        out_specs=pl.BlockSpec((ROWS, units), lambda i, k: (i, 0)),
        out_shape=jax.ShapeDtypeStruct((tokens, units), jnp.float32),
        compiler_params=kernel_params(),
        cost_estimate=light(2 * tokens * model * units),
        name="hidden_back",
    )(grad_out, weights)


def inner_kernel(normed_ref, grad_ref, weight_ref, hidden_ref, gate_ref, up_ref, sum_ref):
    which = pl.program_id(1)
    step = pl.program_id(2)
    weight = weight_ref[...].reshape(-1, weight_ref.shape[3])

    @pl.when(step == 0)
    def _():
        sum_ref[which] = dot_nn(normed_ref[...], weight)

    @pl.when(step != 0)
    def _():
        sum_ref[which] += dot_nn(normed_ref[...], weight)

    @pl.when((which == 1) & (step == pl.num_programs(2) - 1))
    def _():
        gate_val = sum_ref[0]
        up_val = sum_ref[1]
        grad_hidden = grad_ref[...]
        sigmoid_gate = jax.nn.sigmoid(gate_val)
        silu_gate = gate_val * sigmoid_gate
        hidden_ref[...] = (silu_gate * up_val).astype(jnp.bfloat16)
        gate_ref[...] = (
            grad_hidden * up_val * sigmoid_gate * (1.0 + gate_val * (1.0 - sigmoid_gate))
        ).astype(jnp.bfloat16)
        up_ref[...] = (grad_hidden * silu_gate).astype(jnp.bfloat16)


def ffn_inner(normed, grad_hidden, weights, place):
    tokens, model = normed.shape
    blocks, unused, rows, units = weights.shape
    steps = tokens // ROWS
    out = jax.ShapeDtypeStruct((tokens, units), jnp.bfloat16)
    result = pl.BlockSpec((ROWS, units), lambda i, w, k: (i, 0))
    return pl.pallas_call(
        inner_kernel,
        grid=(steps, 2, 2),
        in_specs=[
            pl.BlockSpec((ROWS, model // 2), lambda i, w, k: (i, k)),
            pl.BlockSpec((ROWS, units), lambda i, w, k: (i + place * steps, 0)),
            pl.BlockSpec((blocks // 2, 1, rows, units), lambda i, w, k: (k, w, 0, 0)),
        ],
        out_specs=[result, result, result],
        out_shape=[out, out, out],
        scratch_shapes=[pltpu.VMEM((2, ROWS, units), jnp.float32)],
        compiler_params=kernel_params(),
        cost_estimate=light(4 * tokens * model * units),
        name="ffn_inner",
    )(normed, grad_hidden, weights)


def back_kernel(count, *refs):
    lefts = refs[:count]
    weight_ref = refs[count]
    out_ref = refs[count + 1]
    units = weight_ref.shape[3]
    total = None
    for number in range(count):
        term = dot_nt(lefts[number][...], weight_ref[:, number].reshape(-1, units))
        total = term if total is None else total + term
    out_ref[...] = total.astype(jnp.bfloat16)


def ffn_back(lefts, weights, first):
    tokens, units = lefts[0].shape
    blocks, unused, rows, unused_units = weights.shape
    count = len(lefts)
    model = blocks * rows
    return pl.pallas_call(
        functools.partial(back_kernel, count),
        grid=(2, tokens // ROWS),
        in_specs=[pl.BlockSpec((ROWS, units), lambda k, i: (i, 0)) for unused_left in lefts]
        + [pl.BlockSpec((blocks // 2, count, rows, units), lambda k, i: (k, first, 0, 0))],
        out_specs=pl.BlockSpec((ROWS, model // 2), lambda k, i: (i, k)),
        out_shape=jax.ShapeDtypeStruct((tokens, model), jnp.bfloat16),
        compiler_params=kernel_params(),
        cost_estimate=light(4 * count * tokens * model * units),
        name="ffn_back",
    )(*lefts, weights)


def outer_kernel(count, *refs):
    out_ref, mark_ref = refs[-2:]
    total = dot_tn(refs[0][...], refs[count][...])
    for number in range(1, count):
        total = total + dot_tn(refs[number][...], refs[count + number][...])
    out_ref[...] = total.astype(jnp.bfloat16).reshape(out_ref.shape)
    mark_ref[...] = jnp.zeros(mark_ref.shape, jnp.float32)


def ffn_outer(lefts, places, rights, blocks, slot, held):
    tokens, units = rights[0].shape
    model = lefts[0].shape[1]
    rows = model // blocks
    count = len(lefts)
    left_spec = lambda place: pl.BlockSpec((tokens, model // 2), lambda k: (place, k))
    mark_spec = pl.BlockSpec((8, 128), lambda k: (0, 0))
    held_specs = [] if held is None else [pl.BlockSpec(memory_space=pl.ANY), mark_spec]
    return pl.pallas_call(
        functools.partial(outer_kernel, count),
        grid=(2,),
        in_specs=[left_spec(place) for place in places]
        + [pl.BlockSpec((tokens, units), lambda k: (0, 0)) for unused in rights]
        + held_specs,
        out_specs=[
            pl.BlockSpec((blocks // 2, 1, rows, units), lambda k: (k, slot, 0, 0)),
            mark_spec,
        ],
        out_shape=[
            jax.ShapeDtypeStruct((blocks, 3, rows, units), jnp.bfloat16),
            jax.ShapeDtypeStruct((8, 128), jnp.float32),
        ],
        input_output_aliases={} if held is None else {2 * count: 0},
        compiler_params=kernel_params(),
        cost_estimate=light(4 * count * tokens * model * units),
        name="ffn_outer",
    )(*lefts, *rights, *(held or ()))


def down_kernel(normed_ref, grad_ref, weight_ref, gain_ref, out_ref, part_ref):
    total = dot_tn(normed_ref[...], grad_ref[...])
    out_ref[...] = total.astype(jnp.bfloat16)
    summed = jnp.sum(total * weight_ref[...].astype(jnp.float32), axis=1, keepdims=True)
    part_ref[...] = summed / gain_ref[...]


def down_outer(normed, grads, weights, gains):
    tokens, model = normed.shape
    width = grads.shape[1]
    block = model // 4
    row_spec = lambda cols: pl.BlockSpec((block, cols), lambda k: (k, 0))
    return pl.pallas_call(
        down_kernel,
        grid=(4,),
        in_specs=[
            pl.BlockSpec((tokens, block), lambda k: (0, k)),
            pl.BlockSpec((tokens, width), lambda k: (0, 0)),
            row_spec(width),
            row_spec(1),
        ],
        out_specs=[row_spec(width), row_spec(1)],
        out_shape=[
            jax.ShapeDtypeStruct((model, width), jnp.bfloat16),
            jax.ShapeDtypeStruct((model, 1), jnp.float32),
        ],
        compiler_params=kernel_params(),
        cost_estimate=light(4 * tokens * model * width),
        name="down_outer",
    )(normed, grads, weights, gains)


def input_kernel(grad_ref, weight_ref, inputs_ref, cot_ref, mid_ref, gain_ref, out_ref):
    value = inputs_ref[...].astype(jnp.float32)
    scaled = dot_nt(grad_ref[...], weight_ref[...]) * gain_ref[...]
    rate = lax.rsqrt(jnp.mean(value * value, axis=1, keepdims=True) + NORM_EPS)
    dotted = jnp.mean(scaled * value, axis=1, keepdims=True)
    residual = cot_ref[...].astype(jnp.float32) + mid_ref[...].astype(jnp.float32)
    out_ref[...] = residual + rate * (scaled - value * (rate * rate * dotted))


def input_back(grads, weights, inputs, cotangent, mid_norm, gains):
    tokens, width = grads.shape
    model = inputs.shape[1]
    row_spec = lambda cols: pl.BlockSpec((BLK, cols), lambda i: (i, 0))
    return pl.pallas_call(
        input_kernel,
        grid=(tokens // BLK,),
        in_specs=[
            row_spec(width),
            pl.BlockSpec((model, width), lambda i: (0, 0)),
            row_spec(model),
            row_spec(model),
            row_spec(model),
            pl.BlockSpec((1, model), lambda i: (0, 0)),
        ],
        out_specs=row_spec(model),
        out_shape=jax.ShapeDtypeStruct((tokens, model), jnp.float32),
        compiler_params=kernel_params(),
        cost_estimate=light(4 * tokens * model * width),
        name="input_back",
    )(grads, weights, inputs, cotangent, mid_norm, gains)


def latent_kernel(count, *refs):
    out_ref = refs[-1]
    query_up, latent_up = refs[3 * count], refs[3 * count + 1]
    size = refs[0].shape[1]
    for number in range(count):
        grad_q, grad_kv, rope = refs[number], refs[count + number], refs[2 * count + number]
        rows = slice(number * size, (number + 1) * size)
        out_ref[rows, :QR] = dot_nt(grad_q[...].T, query_up[...]).astype(jnp.bfloat16)
        out_ref[rows, QR : QR + KVR] = dot_nt(grad_kv[...].T, latent_up[...]).astype(jnp.bfloat16)
        out_ref[rows, QR + KVR :] = rope[...].T.astype(jnp.bfloat16)
    mid_part = refs[3 * count + 2][...] + refs[3 * count + 3][...]
    lane = QR + KVR
    lines = []
    for start in range(0, D, lane):
        line = mid_part[:, start : start + lane]
        lines.append(jnp.pad(line, ((0, 0), (0, lane - line.shape[1]))))
    extra = out_ref.shape[0] - count * size
    lines.append(jnp.zeros((extra - len(lines), lane), jnp.float32))
    out_ref[count * size :, :lane] = jnp.concatenate(lines, axis=0).astype(jnp.bfloat16)
    out_ref[count * size :, lane:] = jnp.zeros((extra, RD), jnp.bfloat16)


def latent_back(grads_q, grads_kv, ropes, query_up, latent_up, mid_parts, extra):
    count = len(grads_q)
    tokens = count * grads_q[0].shape[1]
    return pl.pallas_call(
        functools.partial(latent_kernel, count),
        out_shape=jax.ShapeDtypeStruct((tokens + extra, QR + KVR + RD), jnp.bfloat16),
        compiler_params=kernel_params(),
        cost_estimate=light(tokens * (QR + KVR) * 4000),
        name="latent_back",
    )(*grads_q, *grads_kv, *ropes, query_up, latent_up, *mid_parts)


def heads_kernel(count, *refs):
    out_ref = refs[-1]
    q_normed, kv_normed = refs[4 * count], refs[4 * count + 1]
    blocks = out_ref.shape[0]
    size = refs[0].shape[0]
    outer = query_outer = latent_outer = None
    for number in range(count):
        grad_attn, mixed = refs[number], refs[count + number]
        grad_q, grad_kv = refs[2 * count + number], refs[3 * count + number]
        rows = slice(number * size, (number + 1) * size)
        terms = (
            dot_nt(grad_attn[...].T, mixed[...]),
            dot_nt(q_normed[rows].T, grad_q[...]),
            dot_nt(kv_normed[rows].T, grad_kv[...]),
        )
        outer = terms[0] if outer is None else outer + terms[0]
        query_outer = terms[1] if query_outer is None else query_outer + terms[1]
        latent_outer = terms[2] if latent_outer is None else latent_outer + terms[2]
    side = outer.shape[1]
    low = outer.astype(jnp.bfloat16).reshape(blocks, -1, side)
    spread = low.shape[1] // 2
    out_ref[:, :spread, :side] = low[:, :spread]
    out_ref[:, :spread, side:] = low[:, spread:]
    query_rows = query_outer.shape[0] // blocks
    columns = query_outer.shape[1]
    middle = slice(spread, spread + query_rows)
    out_ref[:, middle, :columns] = query_outer.astype(jnp.bfloat16).reshape(blocks, query_rows, columns)
    out_ref[:, middle, columns:] = jnp.zeros(
        (blocks, query_rows, out_ref.shape[2] - columns), jnp.bfloat16
    )
    out_ref[:, spread + query_rows :] = latent_outer.astype(jnp.bfloat16).reshape(
        blocks, -1, out_ref.shape[2]
    )


def heads_outer(grads_attn, mixed, grads_q, grads_kv, q_normed, kv_normed, blocks, mark):
    count = len(mixed)
    size = grads_attn[0].shape[0]
    wide_cols = grads_kv[0].shape[0]
    rows = D // blocks // 2 + QR // blocks + KVR // blocks
    whole = lambda value: pl.BlockSpec(value.shape, lambda k: (0, 0))
    return pl.pallas_call(
        functools.partial(heads_kernel, count),
        grid=(2,),
        in_specs=[pl.BlockSpec((size, D // 2), lambda k: (0, k)) for unused in grads_attn]
        + [whole(value) for value in (*mixed, *grads_q, *grads_kv)]
        + [
            pl.BlockSpec((q_normed.shape[0], QR // 2), lambda k: (0, k)),
            pl.BlockSpec((kv_normed.shape[0], KVR // 2), lambda k: (0, k)),
            pl.BlockSpec((8, 128), lambda k: (0, 0)),
        ],
        out_specs=pl.BlockSpec((blocks // 2, rows, wide_cols), lambda k: (k, 0, 0)),
        out_shape=jax.ShapeDtypeStruct((blocks, rows, wide_cols), jnp.bfloat16),
        compiler_params=kernel_params(),
        cost_estimate=light(count * size * D * wide_cols * 2),
        name="heads_outer",
    )(*grads_attn, *mixed, *grads_q, *grads_kv, q_normed, kv_normed, mark)


def scaled_rate(value):
    return lax.rsqrt(jnp.mean(value * value, axis=1, keepdims=True) + NORM_EPS)


def norm_pull(value, gain_vec, gradient):
    rate = scaled_rate(value)
    scaled = gradient * gain_vec
    dotted = jnp.mean(scaled * value, axis=1, keepdims=True)
    pulled = rate * (scaled - value * (rate * rate * dotted))
    return pulled, jnp.sum(gradient * value * rate, axis=0, keepdims=True)


def latents_kernel(
    inputs_ref, gain_in, down_ref, gain_query, gain_latent, cos_ref, sin_ref,
    normed_ref, latents_ref, q_ref, kv_ref, rope_ref,
):
    value = inputs_ref[...].astype(jnp.float32)
    normed = (value * scaled_rate(value) * gain_in[...]).astype(jnp.bfloat16)
    normed_ref[...] = normed
    latents = dot_nn(normed, down_ref[...])
    latents_ref[...] = latents
    q_latent = latents[:, :QR]
    kv_latent = latents[:, QR : QR + KVR]
    q_ref[...] = (q_latent * scaled_rate(q_latent) * gain_query[...]).astype(jnp.bfloat16)
    kv_ref[...] = (kv_latent * scaled_rate(kv_latent) * gain_latent[...]).astype(jnp.bfloat16)
    rope = latents[:, QR + KVR :].T
    low, high = rope[: RD // 2], rope[RD // 2 :]
    cos_blk, sin_blk = cos_ref[...], sin_ref[...]
    rope_ref[: RD // 2, :] = (low * cos_blk - high * sin_blk).astype(jnp.bfloat16)
    rope_ref[RD // 2 :, :] = (high * cos_blk + low * sin_blk).astype(jnp.bfloat16)


def latents_forward(inputs, gain_in, down_all, gain_query, gain_latent, cosines, sines):
    tokens, model = inputs.shape
    width = down_all.shape[1]
    row_spec = lambda cols: pl.BlockSpec((BLK, cols), lambda i: (i, 0))
    column_spec = lambda rows: pl.BlockSpec((rows, BLK), lambda i: (0, i))
    whole = lambda value: pl.BlockSpec(value.shape, lambda i: (0, 0))
    return pl.pallas_call(
        latents_kernel,
        grid=(tokens // BLK,),
        in_specs=[row_spec(model), whole(gain_in), whole(down_all), whole(gain_query), whole(gain_latent)]
        + [column_spec(RD // 2), column_spec(RD // 2)],
        out_specs=[row_spec(model), row_spec(width), row_spec(QR), row_spec(KVR), column_spec(RD)],
        out_shape=[
            jax.ShapeDtypeStruct((tokens, model), jnp.bfloat16),
            jax.ShapeDtypeStruct((tokens, width), jnp.float32),
            jax.ShapeDtypeStruct((tokens, QR), jnp.bfloat16),
            jax.ShapeDtypeStruct((tokens, KVR), jnp.bfloat16),
            jax.ShapeDtypeStruct((RD, tokens), jnp.bfloat16),
        ],
        compiler_params=kernel_params(),
        cost_estimate=light(tokens * model * width),
        name="latents_forward",
    )(inputs, gain_in, down_all, gain_query, gain_latent, cosines, sines)


def split_kernel(q_ref, kv_ref, rope_ref, query_up, latent_up, cos_ref, sin_ref, queries, keys, values):
    heads = queries.shape[0]
    half = RD // 2
    grown = dot_nt(query_up[...], q_ref[...]).reshape(heads, HD + RD, -1)
    low, high = grown[:, HD : HD + half], grown[:, HD + half :]
    cos_blk, sin_blk = cos_ref[...][None], sin_ref[...][None]
    queries[:, :HD] = grown[:, :HD].astype(jnp.bfloat16)
    queries[:, HD : HD + half] = (low * cos_blk - high * sin_blk).astype(jnp.bfloat16)
    queries[:, HD + half :] = (high * cos_blk + low * sin_blk).astype(jnp.bfloat16)
    grown = dot_nt(latent_up[...], kv_ref[...]).astype(jnp.bfloat16).reshape(heads, 2 * HD, -1)
    keys[:, :HD] = grown[:, :HD]
    keys[:, HD:] = jnp.broadcast_to(rope_ref[...][None], (heads, RD, rope_ref.shape[1]))
    values[...] = grown[:, HD:]


def heads_forward(q_normed, kv_normed, key_rope, query_up, latent_up, cosines, sines):
    tokens = q_normed.shape[0]
    heads = query_up.shape[0] // (HD + RD)
    row_spec = lambda cols: pl.BlockSpec((BLK, cols), lambda i: (i, 0))
    column_spec = lambda rows: pl.BlockSpec((rows, BLK), lambda i: (0, i))
    head_spec = lambda rows: pl.BlockSpec((heads, rows, BLK), lambda i: (0, 0, i))
    whole = lambda value: pl.BlockSpec(value.shape, lambda i: (0, 0))
    return pl.pallas_call(
        split_kernel,
        grid=(tokens // BLK,),
        in_specs=[
            row_spec(QR),
            row_spec(KVR),
            column_spec(RD),
            whole(query_up),
            whole(latent_up),
            column_spec(RD // 2),
            column_spec(RD // 2),
        ],
        out_specs=[head_spec(HD + RD), head_spec(HD + RD), head_spec(HD)],
        out_shape=[
            jax.ShapeDtypeStruct((heads, HD + RD, tokens), jnp.bfloat16),
            jax.ShapeDtypeStruct((heads, HD + RD, tokens), jnp.bfloat16),
            jax.ShapeDtypeStruct((heads, HD, tokens), jnp.bfloat16),
        ],
        compiler_params=kernel_params(),
        cost_estimate=light(tokens * QR),
        name="heads_forward",
    )(q_normed, kv_normed, key_rope, query_up, latent_up, cosines, sines)


def middle_kernel(place_ref, grad_ref, resid_ref, gain_ref, out_ref, part_ref):
    pulled, part = norm_pull(resid_ref[...], gain_ref[...], grad_ref[...].astype(jnp.float32))
    out_ref[...] = pulled.astype(jnp.bfloat16)
    part_ref[...] = part


def middle_back(place, grads, resid, gain_mid):
    rows, model = grads.shape
    fixed = lambda size: pl.BlockSpec((size, model), lambda i, place_ref: (0, 0))
    return pl.pallas_call(
        middle_kernel,
        grid_spec=pltpu.PrefetchScalarGridSpec(
            num_scalar_prefetch=1,
            grid=(1,),
            in_specs=[
                fixed(rows),
                pl.BlockSpec((rows, model), lambda i, place_ref: (place_ref[0], 0)),
                fixed(1),
            ],
            out_specs=[fixed(rows), fixed(1)],
        ),
        out_shape=[
            jax.ShapeDtypeStruct((rows, model), jnp.bfloat16),
            jax.ShapeDtypeStruct((1, model), jnp.float32),
        ],
        compiler_params=kernel_params(),
        cost_estimate=light(rows * model),
        name="middle_back",
    )(place, grads, resid, gain_mid)


def turned_kernel(
    total_ref, latents_ref, cos_ref, sin_ref, gain_query, gain_latent, out_ref, query_ref, latent_ref
):
    half = RD // 2
    total = total_ref[...].astype(jnp.float32)
    latents = latents_ref[...]
    q_pulled, q_part = norm_pull(latents[:, :QR], gain_query[...], total[:, :QR])
    kv_pulled, kv_part = norm_pull(
        latents[:, QR : QR + KVR], gain_latent[...], total[:, QR : QR + KVR]
    )
    low = total[:, QR + KVR : QR + KVR + half]
    high = total[:, QR + KVR + half :]
    cos_blk = cos_ref[...].T
    sin_blk = sin_ref[...].T
    out_ref[:, :QR] = q_pulled.astype(jnp.bfloat16)
    out_ref[:, QR : QR + KVR] = kv_pulled.astype(jnp.bfloat16)
    out_ref[:, QR + KVR : QR + KVR + half] = (low * cos_blk + high * sin_blk).astype(jnp.bfloat16)
    out_ref[:, QR + KVR + half :] = (high * cos_blk - low * sin_blk).astype(jnp.bfloat16)

    @pl.when(pl.program_id(0) == 0)
    def _():
        query_ref[...] = q_part
        latent_ref[...] = kv_part

    @pl.when(pl.program_id(0) != 0)
    def _():
        query_ref[...] += q_part
        latent_ref[...] += kv_part


def latents_turned(total, latents, cosines, sines, gain_query, gain_latent):
    tokens, width = latents.shape
    row_spec = lambda cols: pl.BlockSpec((BLK, cols), lambda i: (i, 0))
    column_spec = pl.BlockSpec((RD // 2, BLK), lambda i: (0, i))
    whole = lambda cols: pl.BlockSpec((1, cols), lambda i: (0, 0))
    return pl.pallas_call(
        turned_kernel,
        grid=(tokens // BLK,),
        in_specs=[
            row_spec(width),
            row_spec(width),
            column_spec,
            column_spec,
            whole(QR),
            whole(KVR),
        ],
        out_specs=[row_spec(width), whole(QR), whole(KVR)],
        out_shape=[
            jax.ShapeDtypeStruct((tokens, width), jnp.bfloat16),
            jax.ShapeDtypeStruct((1, QR), jnp.float32),
            jax.ShapeDtypeStruct((1, KVR), jnp.float32),
        ],
        compiler_params=kernel_params(),
        cost_estimate=light(tokens * width),
        name="latents_turned",
    )(total, latents, cosines, sines, gain_query, gain_latent)


def mixed_kernel(mid_ref, cot_ref, weight_ref, attn_ref, mixed_ref):
    grad_mid = cot_ref[...].astype(jnp.float32) + mid_ref[...].astype(jnp.float32)
    grad_attn = (RESID_SCALE * grad_mid).astype(jnp.bfloat16)
    attn_ref[...] = grad_attn
    mixed_ref[...] = dot_nt(weight_ref[...], grad_attn).astype(jnp.bfloat16)


def mixed_gradient(mid_norm, cotangent, out_own, half):
    tokens, model = mid_norm.shape
    heads_width = out_own.shape[0]
    steps = tokens // BLK
    row_spec = pl.BlockSpec((BLK, model), lambda i: (i, 0))
    return pl.pallas_call(
        mixed_kernel,
        grid=(steps,),
        in_specs=[
            row_spec,
            pl.BlockSpec((BLK, model), lambda i: (i + half * steps, 0)),
            pl.BlockSpec(out_own.shape, lambda i: (0, 0)),
        ],
        out_specs=[row_spec, pl.BlockSpec((heads_width, BLK), lambda i: (0, i))],
        out_shape=[
            jax.ShapeDtypeStruct((tokens, model), jnp.bfloat16),
            jax.ShapeDtypeStruct((heads_width, tokens), jnp.bfloat16),
        ],
        compiler_params=kernel_params(),
        cost_estimate=light(tokens * model),
        name="mixed_gradient",
    )(mid_norm, cotangent, out_own)


def adam_kernel(rate_pair, weight_ref, grad_ref, first_ref, second_ref, first_out, second_out, weight_out):
    gradient = grad_ref[...].astype(jnp.float32)
    updates = adam_step(weight_ref[...], gradient, first_ref[...], second_ref[...], rate_pair)
    first_out[...], second_out[...], weight_out[...] = updates


def adam_rows(weight, grads, slot, first, second, rate_pair):
    rows, cols = weight.shape
    block = pl.BlockSpec((rows // 5, cols), lambda i: (i, 0))
    shape = jax.ShapeDtypeStruct((rows, cols), jnp.float32)
    return pl.pallas_call(
        functools.partial(adam_kernel, rate_pair),
        grid=(5,),
        in_specs=[
            block,
            pl.BlockSpec((rows // 5, cols), lambda i: (5 * slot + i, 0)),
            block,
            block,
        ],
        out_specs=[block, block, block],
        out_shape=[shape, shape, shape],
        compiler_params=kernel_params(),
        cost_estimate=light(rows * cols),
        name="adam_rows",
    )(weight, grads, first, second)


def wide(value):
    return value.astype(jnp.float32)


def tie(*values):
    return lax.optimization_barrier(values)


def after(value, *others):
    return lax.optimization_barrier((value, *others))[0]


def chunk_of(stacked, place):
    return lax.dynamic_index_in_dim(stacked, place, axis=0, keepdims=False)


class Gather:
    def __init__(self, own, count, axis):
        self.own, self.count, self.axis = own, count, axis
        self.below, self.above = [own], [own]

    def advance(self, gate):
        step = len(self.below)
        if step == self.count:
            return []
        up, down = gate(self.below[-1], self.above[-1])
        ups = [(k, k + 1) for k in range(step - 1, self.count - 1)]
        downs = [(k + 1, k) for k in range(self.count - step)]
        self.below.append(lax.ppermute(up, "mp", ups))
        self.above.append(lax.ppermute(down, "mp", downs))
        return [self.below[-1], self.above[-1]]

    def result(self):
        while self.advance(tie):
            pass
        place = lax.axis_index("mp")
        blocks = []
        for slot in range(self.count):
            block = self.own
            for step in range(1, self.count):
                if slot + step < self.count:
                    block = jnp.where(place - step == slot, self.below[step], block)
                if slot - step >= 0:
                    block = jnp.where(place + step == slot, self.above[step], block)
            blocks.append(block)
        return jnp.concatenate(blocks, axis=self.axis)


class Direct:
    def __init__(self, own, count):
        self.own, self.count, self.came = own, count, None

    def advance(self, gate):
        if self.came is not None:
            return []
        (sent,) = gate(self.own)
        count = self.count
        self.came = [
            lax.ppermute(sent, "mp", [(k, (k + step) % count) for k in range(count)])
            for step in range(1, count)
        ]
        return self.came

    def result(self):
        self.advance(tie)
        place = lax.axis_index("mp")
        blocks = []
        for slot in range(self.count):
            block = self.own
            for step in range(1, self.count):
                block = jnp.where((place - step) % self.count == slot, self.came[step - 1], block)
            blocks.append(block)
        return jnp.concatenate(blocks, axis=0)


class Scatter:
    def __init__(self, partial, count):
        self.stacked = partial.reshape(count, partial.shape[0] // count, partial.shape[1])
        self.count, self.step = count, 0
        self.below = self.above = None

    def advance(self, gate):
        count = self.count
        if self.step == count - 1:
            return []
        self.step = step = self.step + 1
        place = lax.axis_index("mp")
        up = chunk_of(self.stacked, jnp.clip(count - step + place, 0, count - 1))
        down = chunk_of(self.stacked, jnp.clip(step - count + place, 0, count - 1))
        if step > 1:
            up = (wide(up) + wide(self.below)).astype(up.dtype)
            down = (wide(down) + wide(self.above)).astype(down.dtype)
        up, down = gate(up, down)
        self.below = lax.ppermute(up, "mp", [(k, k + 1) for k in range(step)])
        downs = [(count - 1 - k, count - 2 - k) for k in range(step)]
        self.above = lax.ppermute(down, "mp", downs)
        return [self.below, self.above]

    def arrived(self):
        while self.advance(tie):
            pass
        return self.below, self.above

    def result(self):
        self.arrived()
        own = chunk_of(self.stacked, lax.axis_index("mp"))
        return wide(own) + wide(self.below) + wide(self.above)


class Plane:
    def __init__(self, block, count):
        rows = block.shape[0] // 2
        bits = [1 << k for k in range(1, count.bit_length() - 1)]
        self.count, self.step = count, 0
        self.orders = [bits + [1], bits[::-1] + [1]]
        self.held = [block[None, :rows], block[None, rows:]]

    def advance(self, gate):
        if self.step == len(self.orders[0]):
            return []
        held = gate(*self.held)
        came = []
        for part, order in zip(held, self.orders):
            pairs = [(k, k ^ order[self.step]) for k in range(self.count)]
            came.append(lax.ppermute(part, "dp", pairs))
        self.held = [jnp.concatenate([part, other], axis=0) for part, other in zip(self.held, came)]
        self.step += 1
        return came

    def result(self):
        while self.advance(tie):
            pass
        place = lax.axis_index("dp")
        blocks = []
        for number in range(self.count):
            apart = jnp.bitwise_xor(place, number)
            for part, order in zip(self.held, self.orders):
                spot = sum(
                    jnp.where(jnp.bitwise_and(apart, bit) != 0, 1 << step, 0)
                    for step, bit in enumerate(order)
                )
                blocks.append(chunk_of(part, spot))
        return jnp.concatenate(blocks, axis=0)


class PlaneScatter:
    def __init__(self, stacked, count):
        self.bits = count.bit_length() - 1
        self.left = stacked.reshape((2,) * self.bits + stacked.shape[1:])
        self.step = 0

    def advance(self, gate):
        if self.step == self.bits:
            return []
        bit = 1 << self.step
        axis = self.bits - 1 - self.step
        mine = jnp.where(jnp.bitwise_and(lax.axis_index("dp"), bit) != 0, 1, 0)
        kept = lax.dynamic_index_in_dim(self.left, mine, axis, keepdims=False)
        (gone,) = gate(lax.dynamic_index_in_dim(self.left, 1 - mine, axis, keepdims=False))
        pairs = [(k, k ^ bit) for k in range(1 << self.bits)]
        came = lax.ppermute(gone, "dp", pairs)
        self.left = (wide(kept) + wide(came)).astype(kept.dtype)
        self.step += 1
        return [came]

    def result(self):
        while self.advance(tie):
            pass
        return self.left


class Clock:
    def __init__(self):
        self.past, self.present = (), []

    def gate(self, *values):
        return lax.optimization_barrier((*values, *self.past))[: len(values)]

    def wait(self, value):
        return self.gate(value)[0]

    def move(self, *flows):
        for flow in flows:
            self.present += flow.advance(self.gate)

    def tick(self, *values):
        if self.present or values:
            self.past = (*self.present, *values)
            self.present = []


def local(
    inputs,
    cotangent,
    norm_gains,
    norm_gains_first,
    norm_gains_second,
    query_down,
    query_down_first,
    query_down_second,
    latent_down,
    latent_down_first,
    latent_down_second,
    query_up,
    query_up_first,
    query_up_second,
    latent_up,
    latent_up_first,
    latent_up_second,
    out_proj,
    out_proj_first,
    out_proj_second,
    ffn_gate,
    ffn_gate_first,
    ffn_gate_second,
    ffn_up,
    ffn_up_first,
    ffn_up_second,
    ffn_down,
    ffn_down_first,
    ffn_down_second,
):
    low_type = jnp.bfloat16
    tokens_dev = inputs.shape[0]
    n_data = lax.axis_size("dp")
    n_model = lax.axis_size("mp")
    place = lax.axis_index("mp")
    heads_dev = query_up.shape[1] // (HD + RD)
    half_tokens = tokens_dev // 2
    own_tokens = half_tokens // n_model
    spread = tokens_dev // n_model
    hidden_dev = ffn_gate.shape[1]
    out_width = heads_dev * HD
    down_rows = query_down.shape[0]
    width = QR + KVR + RD
    gain_rows = 16
    order = (1, 0)

    def own_rows(value):
        return lax.dynamic_slice_in_dim(value, place * own_tokens, own_tokens, 0)

    def half_of(value, half):
        return value[half * half_tokens : (half + 1) * half_tokens]

    up_rows = query_up.shape[0]
    kv_rows = latent_up.shape[0]
    up_width = latent_up.shape[1]
    gains_high = lax.reduce_precision(norm_gains, 8, 7)
    up_pack = jnp.concatenate(
        [
            jnp.pad(query_up.astype(low_type), ((0, 0), (0, up_width - query_up.shape[1]))),
            latent_up.astype(low_type),
            jnp.pad(
                jnp.stack([gains_high, norm_gains - gains_high]).astype(low_type),
                ((0, gain_rows - 2), (0, up_width - norm_gains.shape[0])),
            ),
        ],
        axis=0,
    )
    down_own = jnp.concatenate([query_down, latent_down], axis=1).astype(low_type)
    up_flow = Plane(up_pack, n_data)
    down_flow = Direct(down_own, n_model)
    out_flow = Gather(out_proj.T.astype(low_type), n_model, 1)
    clock = Clock()
    clock.move(down_flow)
    clock.tick()
    down_flow = Plane(down_flow.result(), n_data)
    for unused in range(3):
        clock.move(down_flow, up_flow, out_flow)
        clock.tick()
    up_all = up_flow.result().reshape(n_data, -1, up_width)
    down_all = down_flow.result()
    out_all = lax.all_gather(out_flow.result(), "dp", axis=0, tiled=True)
    out_own = lax.dynamic_slice_in_dim(out_all, place * out_width, out_width, 1).T
    ffn_pack = jnp.stack([ffn_gate, ffn_up, ffn_down.T]).astype(low_type)
    ffn_all = lax.all_gather(ffn_pack, "dp", axis=0, tiled=False)
    query_up_all = up_all[:, :up_rows, : query_up.shape[1]].reshape(QR, query_up.shape[1])
    latent_up_all = up_all[:, up_rows : up_rows + kv_rows].reshape(KVR, up_width)
    gains_sent = wide(up_all[:, up_rows + kv_rows : up_rows + kv_rows + 2, : norm_gains.shape[0]])
    gains_all = (gains_sent[:, 0] + gains_sent[:, 1]).reshape(-1)
    gain_in = gains_all[:D]
    gain_query = gains_all[D : D + QR]
    gain_latent = gains_all[D + QR : D + QR + KVR]
    gain_mid = gains_all[D + QR + KVR :]
    cosines, sines = tables(LEN)
    cosines = cosines.T
    sines = sines.T

    normed_in, latents, q_normed, kv_normed, key_rope = latents_forward(
        inputs, gain_in[None], down_all, gain_query[None], gain_latent[None], cosines, sines
    )
    queries, keys, values = heads_forward(
        q_normed, kv_normed, key_rope, query_up_all.T, latent_up_all.T, cosines, sines
    )
    mixed = {}
    log_sums = {}
    resid_mid = {}
    normed_mid = {}
    grad_ffn = (RESID_SCALE * wide(cotangent)).astype(low_type)
    mixed_flow = {}
    for half in order:
        asked = queries if half == 1 else clock.wait(queries)
        mixed[half], log_sums[half] = attend_forward(asked, keys, values, half)
        mixed[half] = mixed[half].reshape(out_width, half_tokens)
        mixed_flow[half] = Gather(mixed[half], n_model, 0)
        clock.tick(mixed[half])
        clock.move(mixed_flow[1])
    grad_hidden = hidden_back(clock.wait(grad_ffn), ffn_all)
    clock.tick(grad_hidden)
    clock.move(mixed_flow[1])
    clock.tick()
    clock.move(mixed_flow[0])

    def middle(half):
        mixed_all = clock.wait(mixed_flow[half].result())
        attn_out = contract("ht,dh->td", mixed_all, out_all)
        resid_mid[half] = wide(half_of(inputs, half)) + RESID_SCALE * attn_out
        normed_mid[half] = normalize(resid_mid[half], gain_mid).astype(low_type)
        clock.tick(normed_mid[half])

    hidden = {}
    grad_gate = {}
    grad_up = {}
    part_mid = {}
    mid_own = {}
    for half in order:
        middle(half)
        clock.move(mixed_flow[0])
        hidden[half], grad_gate[half], grad_up[half] = ffn_inner(
            clock.wait(normed_mid[half]), grad_hidden, ffn_all, half
        )
        clock.tick(grad_up[half])
        clock.move(mixed_flow[0])
        part_mid[half] = ffn_back([clock.wait(grad_gate[half]), grad_up[half]], ffn_all, 0)
        clock.tick(part_mid[half])
        sent_mid = part_mid[half] if half == 1 else after(part_mid[half], mid_own[1])
        mid_own[half] = lax.psum_scatter(sent_mid, "mp", scatter_dimension=0, tiled=True)
    pairs = lambda values: [values[half] for half in order]
    both = lambda values: [values[half] for half in (0, 1)]
    mid_norm = {}
    mid_flow = {}
    gain_mid_part = {}
    grad_attn = {}
    grad_mixed = {}

    def mid_back(half):
        own, gain_mid_part[half] = middle_back(
            place[None], mid_own[half], resid_mid[half], gain_mid[None]
        )
        mid_flow[half] = Gather(own, n_model, 0)

    def mixed_back(half):
        mid_norm[half] = mid_flow[half].result()
        grad_attn[half], grad_mixed[half] = mixed_gradient(
            clock.wait(mid_norm[half]), cotangent, out_own, half
        )

    mid_back(1)
    clock.move(mid_flow[1])
    grad_gate[1] = clock.wait(grad_gate[1])
    held = ffn_outer(pairs(normed_mid), (0, 0), pairs(grad_gate), n_data, 0, None)
    grad_up[1] = after(grad_up[1], out_own)
    held = ffn_outer(pairs(normed_mid), (0, 0), pairs(grad_up), n_data, 1, held)
    ffn_grads, mark = ffn_outer([grad_ffn, grad_ffn], order, pairs(hidden), n_data, 2, held)
    clock.tick(mark)
    clock.move(mid_flow[1])
    ffn_term = {}
    for half in order:
        ffn_term[half] = ffn_back([clock.wait(hidden[half])], ffn_all, 2)
    clock.tick(ffn_term[1], ffn_term[0])
    clock.move(mid_flow[1])
    ffn_term = jnp.concatenate([clock.wait(ffn_term[0]), ffn_term[1]], axis=0)
    mid_own[0] = clock.wait(mid_own[0])
    mid_back(0)
    clock.tick(ffn_term, mid_flow[0].own)
    ffn_grads = after(ffn_grads, mid_own[0])
    ffn_sum = lax.psum_scatter(ffn_grads.reshape(-1, hidden_dev), "dp", scatter_dimension=0, tiled=True)
    resid_all = jnp.concatenate([resid_mid[0], resid_mid[1]], axis=0)

    seeds = ()
    grad_q_heads = {}
    grad_kv_heads = {}
    grad_rope = {}

    def heads_back(half):
        back = attend_backward(
            queries,
            keys,
            values,
            grad_mixed[half].reshape(heads_dev, HD, half_tokens),
            log_sums[half],
            cosines,
            sines,
            half,
            seeds,
        )
        grad_q_heads[half] = back[0].reshape(heads_dev * (HD + RD), half_tokens)
        grad_kv_heads[half] = back[1].reshape(heads_dev * 2 * HD, half_tokens)
        grad_rope[half] = back[2]
        return back[3:]

    clock.move(mid_flow[0])
    mixed_back(1)
    seeds = heads_back(1)
    clock.tick(grad_rope[1])
    out_flow = Scatter(ffn_term, n_model)
    clock.move(mid_flow[0])
    out_flow.advance(clock.gate)
    clock.tick()
    clock.move(mid_flow[0])
    out_flow.advance(tie)
    clock.tick()
    out_flow.advance(tie)
    mixed_back(0)
    seeds = heads_back(0)
    part_latents = latent_back(
        both(grad_q_heads),
        both(grad_kv_heads),
        both(grad_rope),
        query_up_all,
        latent_up_all,
        both(gain_mid_part),
        gain_rows,
    )
    clock.tick(part_latents)
    latents_sum = lax.psum(after(part_latents, ffn_sum), "mp")
    ffn_own = out_flow.result()

    def wide_rows(value):
        return lax.dynamic_slice_in_dim(value, place * spread, spread, 0)

    output_own = (wide_rows(resid_all) + RESID_SCALE * ffn_own).astype(low_type)
    output_flow = Gather(output_own, n_model, 0)
    arrived = output_flow.advance(clock.gate)
    output_flow.advance(tie)
    head_grads = heads_outer(
        both(grad_attn),
        both(mixed),
        both(grad_q_heads),
        both(grad_kv_heads),
        after(q_normed, *arrived),
        kv_normed,
        n_data,
        mark,
    )
    ffn_rates = update_rates()[6:]
    ffn_late = after(ffn_sum, *arrived)
    gate_updates = adam_rows(ffn_gate, ffn_late, 0, ffn_gate_first, ffn_gate_second, ffn_rates[0])
    up_updates = adam_rows(ffn_up, ffn_late, 1, ffn_up_first, ffn_up_second, ffn_rates[1])
    down_updates = adam_rows(
        ffn_down.T, ffn_late, 2, ffn_down_first.T, ffn_down_second.T, ffn_rates[2]
    )
    latents_sum = after(
        latents_sum, head_grads, gate_updates[2], up_updates[2], down_updates[2]
    )
    head_sum = lax.psum_scatter(
        after(head_grads, latents_sum).reshape(-1, up_width), "dp", scatter_dimension=0, tiled=True
    )
    out_rows = D // n_data // 2
    grad_latents, gain_query_sum, gain_latent_sum = latents_turned(
        latents_sum, latents, cosines, sines, gain_query[None], gain_latent[None]
    )

    def later(*values):
        return lax.optimization_barrier((*values, grad_latents))[: len(values)]

    while output_flow.advance(later):
        pass
    output = output_flow.result()
    gain_rest = jnp.concatenate(
        [gain_query_sum[0], gain_latent_sum[0], wide(latents_sum[tokens_dev:, : QR + KVR]).reshape(-1)[:D]]
    )

    grad_down, gain_in_part = down_outer(normed_in, grad_latents, down_all, gain_in[:, None])
    gain_grad = jnp.concatenate([gain_in_part[:, 0], gain_rest]).reshape(n_data, 1, -1)
    gain_count = gain_grad.shape[2]
    gain_grad = jnp.pad(gain_grad, ((0, 0), (0, gain_rows - 1), (0, width - gain_count)))
    down_mine = lax.dynamic_index_in_dim(
        grad_down.reshape(n_data, n_model, down_rows, width), place, axis=1, keepdims=False
    )
    down_flow = PlaneScatter(
        jnp.concatenate([down_mine, gain_grad.astype(low_type)], axis=1), n_data
    )
    clock.tick(grad_down)
    clock.move(down_flow)
    clock.tick()
    clock.move(down_flow)
    input_grad = input_back(
        clock.wait(grad_latents),
        down_all,
        inputs,
        cotangent,
        jnp.concatenate([mid_norm[0], mid_norm[1]], axis=0),
        gain_in[None],
    )
    clock.tick(input_grad)
    clock.move(down_flow)
    down_sum = wide(down_flow.result())
    ffn_updated = [gate_updates, up_updates, [update.T for update in down_updates]]
    reduced = (
        down_sum[down_rows, :gain_count],
        down_sum[:down_rows, :QR],
        down_sum[:down_rows, QR:],
        wide(head_sum[out_rows : out_rows + up_rows, : query_up.shape[1]]),
        wide(head_sum[out_rows + up_rows :]),
        wide(
            jnp.concatenate([head_sum[:out_rows, :out_width], head_sum[:out_rows, out_width:]], axis=0).T
        ),
    )
    weights = (
        norm_gains,
        query_down,
        latent_down,
        query_up,
        latent_up,
        out_proj,
        ffn_gate,
        ffn_up,
        ffn_down,
    )
    firsts = (
        norm_gains_first,
        query_down_first,
        latent_down_first,
        query_up_first,
        latent_up_first,
        out_proj_first,
        ffn_gate_first,
        ffn_up_first,
        ffn_down_first,
    )
    seconds = (
        norm_gains_second,
        query_down_second,
        latent_down_second,
        query_up_second,
        latent_up_second,
        out_proj_second,
        ffn_gate_second,
        ffn_up_second,
        ffn_down_second,
    )
    rates = update_rates()
    updated = [
        adam_step(weights[number], reduced[number], firsts[number], seconds[number], rates[number])
        for number in range(6)
    ] + ffn_updated
    return (
        output,
        input_grad,
        updated[0][0],
        updated[0][1],
        updated[0][2],
        updated[1][0],
        updated[1][1],
        updated[1][2],
        updated[2][0],
        updated[2][1],
        updated[2][2],
        updated[3][0],
        updated[3][1],
        updated[3][2],
        updated[4][0],
        updated[4][1],
        updated[4][2],
        updated[5][0],
        updated[5][1],
        updated[5][2],
        updated[6][0],
        updated[6][1],
        updated[6][2],
        updated[7][0],
        updated[7][1],
        updated[7][2],
        updated[8][0],
        updated[8][1],
        updated[8][2],
    )


def solution(mesh):
    placed = (
        P("dp", None),
        P("dp", None),
        P("dp"),
        P("dp"),
        P("dp"),
        P(("dp", "mp"), None),
        P(("dp", "mp"), None),
        P(("dp", "mp"), None),
        P(("dp", "mp"), None),
        P(("dp", "mp"), None),
        P(("dp", "mp"), None),
        P("dp", "mp"),
        P("dp", "mp"),
        P("dp", "mp"),
        P("dp", "mp"),
        P("dp", "mp"),
        P("dp", "mp"),
        P("mp", "dp"),
        P("mp", "dp"),
        P("mp", "dp"),
        P("dp", "mp"),
        P("dp", "mp"),
        P("dp", "mp"),
        P("dp", "mp"),
        P("dp", "mp"),
        P("dp", "mp"),
        P("mp", "dp"),
        P("mp", "dp"),
        P("mp", "dp"),
    )
    return jax.shard_map(
        local,
        mesh=mesh,
        in_specs=placed,
        out_specs=(
            P("dp", None),
            P("dp", None),
            P("dp"),
            P("dp"),
            P("dp"),
            P(("dp", "mp"), None),
            P(("dp", "mp"), None),
            P(("dp", "mp"), None),
            P(("dp", "mp"), None),
            P(("dp", "mp"), None),
            P(("dp", "mp"), None),
            P("dp", "mp"),
            P("dp", "mp"),
            P("dp", "mp"),
            P("dp", "mp"),
            P("dp", "mp"),
            P("dp", "mp"),
            P("mp", "dp"),
            P("mp", "dp"),
            P("mp", "dp"),
            P("dp", "mp"),
            P("dp", "mp"),
            P("dp", "mp"),
            P("dp", "mp"),
            P("dp", "mp"),
            P("dp", "mp"),
            P("mp", "dp"),
            P("mp", "dp"),
            P("mp", "dp"),
        ),
        check_vma=False,
    )
```
